512 devices in a mesh: gz: 32 (over x, y), xy: 16 (over z, core).
Axes of the slice: x: 4, y: 8, z: 8, core: 2. Of those that a mesh axis runs over, the one named last changes fastest.
Arguments:
- load_field: float32 [256, 256, 512], P('gz', 'xy'), may hold values from -8 to 8
- density: float32 [256, 256, 512], P('gz', 'xy'), may hold values from 0.2 to 1
- void_mask: int32 [32, 32, 64], P('gz', 'xy'), may hold values 0 or 1
Outputs:
- adjoint: float32 [256, 256, 512], P('gz', 'xy')
- residual: float32 [256, 256, 512], P('gz', 'xy')
The draws below stay inside these ranges and needn't reach their ends.
Inputs may be any that keep to these rules, and one draw needn't show every extreme that they name: `void_mask`: 1 marks a void brick.
All inputs are finite; a program needn't handle non-finite values. No bound on the sum of `void_mask` on one device may be relied on, other than what follows from the above.
Results may differ from the reference program's by a relative error of at most 0.0003.
Values sent between devices are 32-bit elements; how exact they have to be, the bound alone decides.
No kernel may reach another device: no remote copies, remote signals or barrier semaphores. Data moves between devices by JAX's collectives and lax.ppermute only.
A program may use at most 128 MiB of HBM per device.

```python
import jax
import jax.numpy as jnp

DEGREE = 4
LEVELS = 3
NZ = 256
NX = 256
NY = 512


def touch_ends(array, rng, smallest, largest):
    longest = array.shape.index(max(array.shape))
    spots = []
    for shift in (0, 1):
        where = [jax.random.randint(jax.random.fold_in(rng, axis), (), 0, length) for axis, length in enumerate(array.shape)]
        where[longest] = (where[longest] + shift) % array.shape[longest]
        spots.append(tuple(where))
    return array.at[spots[0]].set(smallest).at[spots[1]].set(largest)


def shard_levels(own_key, extent, split, low, high):
    level = 1.0
    for position, blocks in split:
        draws = jax.random.uniform(jax.random.fold_in(jax.random.fold_in(own_key, 6), position), (blocks,), jnp.float32, low / len(split), high / len(split))
        level = level * jnp.repeat(jnp.exp(draws), extent[position] // blocks).reshape((-1,) + (1,) * (len(extent) - 1 - position))
    return level


def scatter_about(own_key, extent, scale, most, split=(), held_as=jnp.bfloat16):
    drawn = jax.random.normal(own_key, extent, jnp.float32) * scale
    if len(split) > 0:
        drawn = shard_levels(own_key, extent, split, -0.22, 0.18) * drawn
    return jnp.clip(drawn, min=-most, max=most).astype(held_as)


def setup_inputs(seed: int = 0) -> dict:
    splits = jax.random.split(jax.random.key(seed), 4)
    load_field = scatter_about(splits[0], (NZ, NX, NY), 1.0, 8.0, ((0, 32), (1, 16)), jnp.float32)
    density = jnp.clip(0.2 + 0.8 * jax.random.uniform(splits[1], (NZ, NX, NY), jnp.float32) ** shard_levels(splits[1], (NZ, NX, NY), ((0, 32), (1, 16)), -0.2, 0.2), 0.2, 1.0)
    void_mask = touch_ends((jax.random.randint(splits[2], (NZ // 8, NX // 8, NY // 8), 0, 5) < 1).astype(jnp.int32), jax.random.fold_in(splits[2], 1), 0, 1)
    return {"load_field": load_field, "density": density, "void_mask": void_mask}


THETA = 1.15
DELTA = 0.85

def neighbours(padded):
    total = padded[2:, 1:-1, 1:-1] + padded[:-2, 1:-1, 1:-1]
    total = total + padded[1:-1, 2:, 1:-1] + padded[1:-1, :-2, 1:-1]
    return total + padded[1:-1, 1:-1, 2:] + padded[1:-1, 1:-1, :-2]

def operate(field, root):
    weighted = root * field
    return root * (6.0 * weighted - neighbours(jnp.pad(weighted, 1)))

def chebyshev(solution, remain, root):
    inverse = 1.0 / (6.0 * root * root)
    sigma = THETA / DELTA
    rho = 1.0 / sigma
    step = inverse * remain / THETA
    for turn in range(DEGREE):
        solution = solution + step
        remain = remain - operate(step, root)
        if turn + 1 < DEGREE:
            rho_next = 1.0 / (2.0 * sigma - rho)
            step = rho_next * rho * step + 2.0 * rho_next / DELTA * inverse * remain
            rho = rho_next
    return (solution, remain)

def blocks(field):
    a, b, c = field.shape
    return field.reshape(a // 2, 2, b // 2, 2, c // 2, 2).sum(axis=(1, 3, 5))

def prolong(field):
    return jnp.repeat(jnp.repeat(jnp.repeat(field, 2, 0), 2, 1), 2, 2)

def cycle(right, root, depth):
    solution, remain = chebyshev(jnp.zeros_like(right), right, root)
    if depth + 1 == LEVELS:
        return (solution, remain)
    coarse, unused = cycle(0.5 * blocks(remain), 0.125 * blocks(root), depth + 1)
    fine = prolong(coarse)
    solution = solution + fine
    remain = remain - operate(fine, root)
    return chebyshev(solution, remain, root)

def reference(load_field, density, void_mask):
    voids = jnp.repeat(jnp.repeat(jnp.repeat(void_mask, 8, 0), 8, 1), 8, 2)
    stiff = jnp.where(voids == 1, 0.01, 0.01 + 0.99 * density * density * density)
    return cycle(load_field, jnp.sqrt(stiff), 0)
```

```python
import jax
import jax.numpy as jnp
from jax import lax
from jax.experimental import pallas as pl
from jax.experimental.pallas import tpu as pltpu
from jax.sharding import PartitionSpec as P


DEGREE = 4
THETA = 1.15
DELTA = 0.85
FIRST = 1.0 / (6.0 * THETA)
LEAST = 0.05
F32 = jnp.float32
LANES = 128


def coefficients():
    sigma = THETA / DELTA
    rho = 1.0 / sigma
    pairs = []
    for turn in range(DEGREE - 1):
        rho_next = 1.0 / (2.0 * sigma - rho)
        pairs.append((rho_next * rho, 2.0 * rho_next / (6.0 * DELTA)))
        rho = rho_next
    return pairs


COEFFICIENTS = coefficients()


def iota(shape, dim):
    return lax.broadcasted_iota(jnp.int32, shape, dim)


def row_mask(rows, base, count):
    place = iota((rows, LANES), 0) + base
    return jnp.where((place >= 0) & (place < count), 1.0, 0.0).astype(F32)


def loop(low, high, body):
    def step(z, carry):
        body(z)
        return carry

    lax.fori_loop(low, high, step, 0)


def columns(ref, z):
    return [ref[z, :, pl.ds(k, LANES)] for k in range(0, ref.shape[2], LANES)]


def put(ref, z, cols):
    for k, col in enumerate(cols):
        ref[z, :, pl.ds(k * LANES, LANES)] = col


def neighbours(ref, z):
    here = columns(ref, z)
    rows = here[0].shape[0]
    lane = iota((rows, LANES), 1)
    above = [pltpu.roll(c, 1, 1) for c in here]
    below = [pltpu.roll(c, LANES - 1, 1) for c in here]
    out = []
    for k, c in enumerate(here):
        left = above[k - 1] if k > 0 else 0.0
        right = below[k + 1] if k + 1 < len(here) else 0.0
        total = jnp.where(lane == 0, left, above[k]) + jnp.where(lane == LANES - 1, right, below[k])
        total = total + (pltpu.roll(c, 1, 0) + pltpu.roll(c, rows - 1, 0))
        at = pl.ds(k * LANES, LANES)
        out.append(total + (ref[z - 1, :, at] + ref[z + 1, :, at]))
    return here, out


def smooth(bufs, q, y, low, high, y_low, y_high, y_off, y_new, mask, z_scale, passes, finish=None):
    first, second = bufs

    def begin(z, keep):
        scale = z_scale(z, FIRST)
        w = [(scale * mask) * c for c in columns(q, z)]
        put(first, z, w)
        if keep:
            old = [0.0] * len(w) if y_new else columns(y, z - y_off)
            put(y, z - y_off, [a + b for a, b in zip(old, w)])

    def ranged(lo, hi, make):
        if lo < min(y_low, hi):
            loop(lo, min(y_low, hi), lambda z: make(z, False))
        if max(lo, y_low) < min(hi, y_high):
            loop(max(lo, y_low), min(hi, y_high), lambda z: make(z, True))
        if max(lo, y_high) < hi:
            loop(max(lo, y_high), hi, lambda z: make(z, False))

    ranged(low, high, begin)
    for turn in range(passes):
        source, target = (first, second) if turn % 2 == 0 else (second, first)

        def advance(z, keep, source=source, target=target, turn=turn):
            here, around = neighbours(source, z)
            rest = [a - 6.0 * b + c for a, b, c in zip(columns(q, z), here, around)]
            if turn == DEGREE - 1 and finish is not None:
                finish(z, rest)
                return
            put(q, z, rest)
            if turn < DEGREE - 1:
                c1, c2 = COEFFICIENTS[turn]
                scale = z_scale(z, c2) * mask
                w = [c1 * a + scale * b for a, b in zip(here, rest)]
                put(target, z, w)
                if keep:
                    put(y, z - y_off, [a + b for a, b in zip(columns(y, z - y_off), w)])

        ranged(low + 1 + turn, high - 1 - turn, advance)


def z_mask(base, count):
    def scaled(z, value):
        place = z + base
        return jnp.where((place >= 0) & (place < count), F32(value), F32(0.0))

    return scaled


def odd_even(ref, at, start):
    return ref[at, pl.ds(start, 16, 2), :] + ref[at, pl.ds(start + 1, 16, 2), :]


def exact_product(left, right):
    high = left.astype(jnp.bfloat16)
    rest = left - high.astype(F32)
    middle = rest.astype(jnp.bfloat16)
    low = (rest - middle.astype(F32)).astype(jnp.bfloat16)
    parts = [jnp.dot(part, right, preferred_element_type=F32) for part in (high, middle, low)]
    return (parts[2] + parts[1]) + parts[0]


def pair_sum(length):
    at = iota((length, length // 2), 0)
    return jnp.where((at >> 1) == iota((length, length // 2), 1), 1.0, 0.0).astype(jnp.bfloat16)


def pair_copy(length):
    at = iota((length // 2, length), 1)
    return jnp.where((at >> 1) == iota((length // 2, length), 0), 1.0, 0.0).astype(jnp.bfloat16)


def scale_kernel(load, density, void, up, down, root):
    bricks = jnp.where(void[0] == 1, 1.0, 0.0).astype(F32)
    bricks = jnp.concatenate([jnp.broadcast_to(bricks[k : k + 1], (8, 64)) for k in range(2)], axis=0)
    spread = jnp.where((iota((64, 512), 1) >> 3) == iota((64, 512), 0), 1.0, 0.0).astype(jnp.bfloat16)
    voids = jnp.dot(bricks.astype(jnp.bfloat16), spread, preferred_element_type=F32)
    for z in range(8):
        d = density[z]
        r = jnp.sqrt(jnp.where(voids > 0.5, 0.01, 0.01 + 0.99 * d * d * d))
        q = load[z] / r
        up[z] = q
        down[z] = q
        root[z] = r
        if z >= 3:
            up[5 + z] = r
        if z < 5:
            down[8 + z] = r


def fine_pack_kernel(low, up, root, high, left, right):
    at = 0
    for ref, count in ((low, 13), (up, 8), (root, 8), (high, 13)):
        for k in range(count):
            left[at + k] = ref[k, 0:8]
            right[at + k] = ref[k, 8:16]
        at += count


def fine_pre_kernel(counts, low, up, root, high, left, right, q, y, r, mid_low, mid_high, w0, w1, s0, s1, m0):
    gz, xy = lax.axis_index("gz"), lax.axis_index("xy")
    mask = row_mask(32, 16 * xy - 8, 16 * counts[1])
    z_scale = z_mask(8 * gz - 8, 8 * counts[0])

    def row(target, z, ref, k, at):
        target[z, 0:8] = left[at + k]
        target[z, 8:24] = ref[k]
        target[z, 24:32] = right[at + k]

    for k in range(8):
        row(q, k, low, k, 0)
        row(q, 8 + k, up, k, 13)
        row(q, 16 + k, high, k, 29)
        row(r, 5 + k, root, k, 21)
    for k in range(5):
        row(r, k, low, 8 + k, 0)
        row(r, 13 + k, high, 8 + k, 29)
    smooth((w0, w1), q, y, 0, 24, 8, 16, 8, True, mask, z_scale, DEGREE)

    s0[:, 32:40] = jnp.zeros((32, 8, LANES), F32)
    s1[:, 32:40] = jnp.zeros((32, 8, LANES), F32)

    def fold(m):
        ra, rb = columns(r, 2 * m + 1), columns(r, 2 * m + 2)
        qa, qb = columns(q, 2 * m + 4), columns(q, 2 * m + 5)
        for k in range(4):
            s0[4 * m + k, 0:32] = ra[k] * qa[k] + rb[k] * qb[k]
            s1[4 * m + k, 0:32] = ra[k] + rb[k]

    loop(0, 8, fold)
    for m in range(8):
        for k in range(4):
            at = pl.ds(k * LANES, LANES)
            m0[m * 16 : m * 16 + 16, at] = odd_even(s0, 4 * m + k, 4)
            m0[128 + m * 16 : 144 + m * 16, at] = odd_even(s1, 4 * m + k, 4)
    sums = exact_product(m0[...], pair_sum(512))
    roots = 0.125 * sums[128:256]
    rights = 0.5 * sums[0:128] / jnp.maximum(roots, LEAST)
    for m in range(4):
        mid_low[m] = rights[m * 16 : m * 16 + 16]
        mid_low[4 + m] = roots[m * 16 : m * 16 + 16]
        mid_high[m] = rights[64 + m * 16 : 80 + m * 16]
        mid_high[4 + m] = roots[64 + m * 16 : 80 + m * 16]


def mid_pack_kernel(*refs):
    parts, left, right = refs[:6], refs[6], refs[7]
    for n, ref in enumerate(parts):
        for k in range(8):
            right[8 * n + k] = ref[k, 0:8]
            left[8 * n + k] = ref[k, 4:12]


def mid_pre_kernel(counts, *refs):
    parts, (left, right), rest = refs[:6], refs[6:8], refs[8:]
    q, y, r, coarse, coarse_low, coarse_high, coarse_root, w0, w1, s0, s1, m0 = rest
    gz, xy = lax.axis_index("gz"), lax.axis_index("xy")
    mask = row_mask(32, 8 * xy - 10, 8 * counts[1])
    z_scale = z_mask(4 * gz - 10, 4 * counts[0])
    for n, ref in enumerate(parts):
        for k in range(8):
            target, z = (q, 4 * n + k) if k < 4 else (r, 4 * n + k - 4)
            target[z, 0:8] = left[8 * n + k]
            target[z, 8:24] = ref[k]
            target[z, 20:28] = right[8 * n + k]
            target[z, 28:32] = jnp.zeros((4, 256), F32)
    smooth((w0, w1), q, y, 0, 24, 7, 17, 7, True, mask, z_scale, DEGREE)

    s0[:, 32:40] = jnp.zeros((16, 8, LANES), F32)
    s1[:, 32:40] = jnp.zeros((20, 8, LANES), F32)
    for m in range(10):
        ra, rb = columns(r, 2 * m + 2), columns(r, 2 * m + 3)
        qa, qb = columns(q, 2 * m + 2), columns(q, 2 * m + 3)
        for k in range(2):
            s1[2 * m + k, 0:32] = ra[k] + rb[k]
            if 0 < m < 9:
                s0[2 * m - 2 + k, 0:32] = ra[k] * qa[k] + rb[k] * qb[k]
    for m in range(10):
        for k in range(2):
            at = pl.ds(k * LANES, LANES)
            m0[m * 16 : m * 16 + 16, at] = odd_even(s1, 2 * m + k, 2)
            if 0 < m < 9:
                j = 160 + (m - 1) * 16
                m0[j : j + 16, at] = odd_even(s1, 2 * m + k, 4)
                j = 288 + (m - 1) * 16
                m0[j : j + 16, at] = odd_even(s0, 2 * m - 2 + k, 4)
    sums = exact_product(m0[...], pair_sum(256))
    rights = 0.5 * sums[288:416] / jnp.maximum(0.125 * sums[160:288], LEAST)
    for m in range(10):
        coarse_root[m] = 0.125 * sums[m * 16 : m * 16 + 16]
    for m in range(8):
        coarse[m] = rights[m * 16 : m * 16 + 16]
    for m in range(2):
        coarse_low[m] = rights[m * 16 : m * 16 + 16]
        coarse_high[m] = rights[96 + m * 16 : 112 + m * 16]


def coarse_pack_kernel(*refs):
    parts, left, right = refs[:5], refs[5], refs[6]
    at = 0
    for ref in parts:
        for k in range(ref.shape[0]):
            right[at + k] = ref[k, 0:8]
            left[at + k] = ref[k, 6:14]
        at += ref.shape[0]


def finish_kernel(counts, *refs):
    parts, (left, right), refs = refs[:5], refs[5:7], refs[7:]
    coarse_root, mid_q, mid_y, mid_r, fine_q, fine_y, fine_r, out_x, out_r = refs[:9]
    cq, cy, cw0, cw1, mq, my, mw0, mw1, mp, fq, fy, fw0, fw1, fp, e0, u0, e1, u1 = refs[9:]
    gz, xy = lax.axis_index("gz"), lax.axis_index("xy")

    at = 0
    for ref in parts:
        for k in range(ref.shape[0]):
            cq[at + k, 0:8] = left[at + k]
            cq[at + k, 4:20] = ref[k]
            cq[at + k, 14:22] = right[at + k]
            cq[at + k, 22:24] = jnp.zeros((2, 128), F32)
        at += ref.shape[0]
    mask = row_mask(24, 4 * xy - 7, 4 * counts[1])
    z_scale = z_mask(2 * gz - 7, 2 * counts[0])
    smooth((cw0, cw1), cq, cy, 0, 16, 3, 13, 3, True, mask, z_scale, DEGREE - 1)
    for k in range(10):
        e0[k * 16 : k * 16 + 16] = cy[k, 3:19] / jnp.maximum(coarse_root[k], LEAST)
    u0[...] = exact_product(e0[...], pair_copy(256))

    mp[...] = jnp.zeros((2, 32, LANES), F32)
    for k in range(10):
        for j in range(2):
            at = pl.ds(j * LANES, LANES)
            value = u0[k * 16 : k * 16 + 12, at]
            mp[j, pl.ds(2, 12, 2), :] = value
            mp[j, pl.ds(3, 12, 2), :] = value
            mw1[2 * k + 2, :, at] = mid_r[2 * k + 2, :, at] * mp[j]
            mw1[2 * k + 3, :, at] = mid_r[2 * k + 3, :, at] * mp[j]

    def correct(w, q_in, q_out, y_in, y_out, y_low, y_high):
        def body(z, keep):
            here, around = neighbours(w, z)
            put(q_out, z, [a - 6.0 * b + c for a, b, c in zip(columns(q_in, z), here, around)])
            if keep:
                put(y_out, z - y_low, [a + b for a, b in zip(columns(y_in, z - y_low), here)])

        loop(4, y_low, lambda z: body(z, False))
        loop(y_low, y_high, lambda z: body(z, True))
        loop(y_high, 20, lambda z: body(z, False))

    correct(mw1, mid_q, mq, mid_y, my, 7, 17)
    mask = row_mask(32, 8 * xy - 10, 8 * counts[1])
    z_scale = z_mask(4 * gz - 10, 4 * counts[0])
    smooth((mw0, mw1), mq, my, 4, 20, 7, 17, 7, False, mask, z_scale, DEGREE - 1)
    for k in range(10):
        e1[k * 16 : k * 16 + 16] = my[k, 7:23] / jnp.maximum(mid_r[7 + k, 7:23], LEAST)
    u1[...] = exact_product(e1[...], pair_copy(512))

    fp[...] = jnp.zeros((4, 32, LANES), F32)
    for k in range(10):
        for j in range(4):
            at = pl.ds(j * LANES, LANES)
            value = u1[k * 16 : k * 16 + 14, at]
            fp[j, pl.ds(2, 14, 2), :] = value
            fp[j, pl.ds(3, 14, 2), :] = value
            if k > 0:
                fw1[2 * k + 2, :, at] = fine_r[2 * k - 1, :, at] * fp[j]
            if k < 9:
                fw1[2 * k + 3, :, at] = fine_r[2 * k, :, at] * fp[j]
    correct(fw1, fine_q, fq, fine_y, fy, 8, 16)
    mask = row_mask(32, 16 * xy - 8, 16 * counts[1])
    z_scale = z_mask(8 * gz - 8, 8 * counts[0])

    def finish(z, rest):
        for k, col in enumerate(rest):
            at = pl.ds(k * LANES, LANES)
            r = fine_r[z - 3, 8:24, at]
            out_r[z - 8, :, at] = r * col[8:24]
            out_x[z - 8, :, at] = fy[z - 8, 8:24, at] / r

    smooth((fw0, fw1), fq, fy, 4, 20, 8, 16, 8, False, mask, z_scale, DEGREE, finish)


def call(kernel, operands, out_shapes, scratch=()):
    whole = pl.BlockSpec(memory_space=pltpu.VMEM)
    return pl.pallas_call(
        kernel,
        out_shape=[jax.ShapeDtypeStruct(s, F32) for s in out_shapes],
        in_specs=[whole] * len(operands),
        out_specs=[whole] * len(out_shapes),
        scratch_shapes=[pltpu.VMEM(s, F32) for s in scratch],
        compiler_params=pltpu.CompilerParams(vmem_limit_bytes=24 * 1024 * 1024),
    )(*operands)


def send(block, axis, shift):
    count = lax.axis_size(axis)
    pairs = [(i, i + shift) for i in range(count) if 0 <= i + shift < count]
    return lax.ppermute(block, axis, pairs)


def with_counts(kernel):
    counts = (lax.axis_size("gz"), lax.axis_size("xy"))
    return lambda *refs: kernel(counts, *refs)


def on_device(load_field, density, void_mask):
    up, down, root = call(
        scale_kernel, (load_field, density, void_mask), [(13, 16, 512), (13, 16, 512), (8, 16, 512)]
    )
    low, high = send(up, "gz", 1), send(down, "gz", -1)
    to_left, to_right = call(fine_pack_kernel, (low, up, root, high), [(42, 8, 512)] * 2)
    left, right = send(to_right, "xy", 1), send(to_left, "xy", -1)
    fine_q, fine_y, fine_r, mid_low, mid_high = call(
        with_counts(fine_pre_kernel),
        (low, up, root, high, left, right),
        [(24, 32, 512), (8, 32, 512), (18, 32, 512), (8, 16, 256), (8, 16, 256)],
        [(24, 32, 512), (24, 32, 512), (32, 40, LANES), (32, 40, LANES), (256, 512)],
    )
    a1, b1 = send(mid_low, "gz", 1), send(mid_high, "gz", -1)
    a2, b2 = send(mid_low, "gz", 2), send(mid_high, "gz", -2)
    parts = (a2, a1, mid_low, mid_high, b1, b2)
    to_left, to_right = call(mid_pack_kernel, parts, [(48, 8, 256)] * 2)
    left, right = send(to_right, "xy", 1), send(to_left, "xy", -1)
    mid_q, mid_y, mid_r, coarse, coarse_low, coarse_high, coarse_root = call(
        with_counts(mid_pre_kernel),
        parts + (left, right),
        [(24, 32, 256), (10, 32, 256), (24, 32, 256), (8, 16, 128), (2, 16, 128), (2, 16, 128), (10, 16, 128)],
        [(24, 32, 256), (24, 32, 256), (16, 40, LANES), (20, 40, LANES), (416, 256)],
    )
    a1, b1 = send(coarse_low, "gz", 1), send(coarse_high, "gz", -1)
    a2, b2 = send(coarse_low, "gz", 2), send(coarse_high, "gz", -2)
    parts = (a2, a1, coarse, b1, b2)
    to_left, to_right = call(coarse_pack_kernel, parts, [(16, 8, 128)] * 2)
    left, right = send(to_right, "xy", 1), send(to_left, "xy", -1)
    return tuple(
        call(
            with_counts(finish_kernel),
            parts + (left, right, coarse_root, mid_q, mid_y, mid_r, fine_q, fine_y, fine_r),
            [(8, 16, 512), (8, 16, 512)],
            [(16, 24, 128), (10, 24, 128), (16, 24, 128), (16, 24, 128)]
            + [(24, 32, 256), (10, 32, 256), (24, 32, 256), (24, 32, 256), (2, 32, LANES)]
            + [(24, 32, 512), (8, 32, 512), (24, 32, 512), (24, 32, 512), (4, 32, LANES)]
            + [(160, 128), (160, 256), (160, 256), (160, 512)],
        )
    )


def solution(mesh):
    specs = (P("gz", "xy", None), P("gz", "xy", None), P("gz", "xy", None))
    return jax.shard_map(
        on_device, mesh=mesh, in_specs=specs, out_specs=specs[:2], check_vma=False
    )
```

```python
import jax
import jax.numpy as jnp
from jax import lax
from jax.experimental import pallas as pl
from jax.experimental.pallas import tpu as pltpu
from jax.sharding import PartitionSpec as P


DEGREE = 4
THETA = 1.15
DELTA = 0.85
FIRST = 1.0 / (6.0 * THETA)
LEAST = 0.05
F32 = jnp.float32
LANES = 128


def coefficients():
    sigma = THETA / DELTA
    rho = 1.0 / sigma
    pairs = []
    for turn in range(DEGREE - 1):
        rho_next = 1.0 / (2.0 * sigma - rho)
        pairs.append((rho_next * rho, 2.0 * rho_next / (6.0 * DELTA)))
        rho = rho_next
    return pairs


COEFFICIENTS = coefficients()


def iota(shape, dim):
    return lax.broadcasted_iota(jnp.int32, shape, dim)


def row_masks(n, base, count):
    masks = []
    for x in range(n):
        place = n * iota((8, LANES), 0) + (x + base)
        masks.append(jnp.where((place >= 0) & (place < count), 1.0, 0.0).astype(F32))
    return masks


def z_mask(base, count):
    def scaled(z, value):
        place = z + base
        return jnp.where((place >= 0) & (place < count), F32(value), F32(0.0))

    return scaled


def loop(low, high, body, width=2):
    turns = (high - low) // width

    def step(t, carry):
        for j in range(width):
            body(low + width * t + j)
        return carry

    if turns > 0:
        lax.fori_loop(0, turns, step, 0)
    for z in range(low + turns * width, high):
        body(z)


def around(ref, z, n):
    count = ref.shape[1]
    blocks = count // n
    here = [ref[z, i] for i in range(count)]
    lane = iota((8, LANES), 1)
    before = [jnp.where(lane == 0, 0.0, pltpu.roll(here[(blocks - 1) * n + x], 1, 1)) for x in range(n)]
    after = [jnp.where(lane == LANES - 1, 0.0, pltpu.roll(here[x], LANES - 1, 1)) for x in range(n)]
    total = []
    for k in range(blocks):
        row = here[k * n : k * n + n]
        up = pltpu.roll(row[n - 1], 1, 0)
        down = pltpu.roll(row[0], 7, 0)
        for x in range(n):
            i = k * n + x
            left = here[i - n] if k > 0 else before[x]
            right = here[i + n] if k + 1 < blocks else after[x]
            north = row[x - 1] if x > 0 else up
            south = row[x + 1] if x + 1 < n else down
            total.append(((left + right) + (north + south)) + (ref[z - 1, i] + ref[z + 1, i]))
    return here, total


def applied(ref, z, n, q):
    here, total = around(ref, z, n)
    return here, [q[z, i] - (6.0 * here[i] - total[i]) for i in range(len(here))]


def smooth(w, q, low, high, n, masks, z_scale, passes, finish=None):
    for turn in range(passes):

        def advance(z, turn=turn):
            here, rest = applied(w[turn], z, n, q)
            if finish is not None and turn == DEGREE - 1:
                finish(z, rest)
                return
            if turn < passes - 1 or passes == DEGREE:
                for i, value in enumerate(rest):
                    q[z, i] = value
            if turn < DEGREE - 1:
                c1, c2 = COEFFICIENTS[turn]
                scales = [z_scale(z, c2) * mask for mask in masks]
                for i, value in enumerate(rest):
                    w[turn + 1][z, i] = c1 * here[i] + scales[i % n] * value

        loop(low + 1 + turn, high - 1 - turn, advance)


def weave(source, z, k, blocks, n, x):
    return source[z * blocks + k, pl.ds(x, 8, n), :]


def exact_product(left, right):
    high = left.astype(jnp.bfloat16)
    rest = left - high.astype(F32)
    middle = rest.astype(jnp.bfloat16)
    low = (rest - middle.astype(F32)).astype(jnp.bfloat16)
    parts = [jnp.dot(part, right, preferred_element_type=F32) for part in (high, middle, low)]
    return (parts[2] + parts[1]) + parts[0]


def weave_matrix(dim):
    plain, woven = iota((512, 512), dim), iota((512, 512), 1 - dim)
    same = plain == 4 * (woven & (LANES - 1)) + (woven >> 7)
    return jnp.where(same, 1.0, 0.0).astype(jnp.bfloat16)


def scale_kernel(load_hbm, density_hbm, void_hbm, up, down, root, both, void, sems):
    copies = [
        pltpu.make_async_copy(load_hbm, both.at[pl.ds(0, 8)], sems.at[0]),
        pltpu.make_async_copy(density_hbm, both.at[pl.ds(8, 8)], sems.at[1]),
        pltpu.make_async_copy(void_hbm, void, sems.at[2]),
    ]
    for copy in copies:
        copy.start()
    matrix = weave_matrix(0)
    copies[2].wait()
    bricks = jnp.where(void[0] == 1, 1.0, 0.0).astype(F32)
    bricks = jnp.concatenate([jnp.broadcast_to(bricks[k : k + 1], (8, 64)) for k in range(2)], axis=0)
    spread = jnp.where((iota((64, LANES), 1) >> 1) == iota((64, LANES), 0), 1.0, 0.0).astype(jnp.bfloat16)
    voids = jnp.dot(bricks.astype(jnp.bfloat16), spread, preferred_element_type=F32)
    copies[0].wait()
    copies[1].wait()
    fields = exact_product(both[...].reshape(256, 512), matrix)
    for z in range(8):
        for k in range(4):
            b = fields[16 * z : 16 * z + 16, LANES * k : LANES * k + LANES]
            d = fields[128 + 16 * z : 144 + 16 * z, LANES * k : LANES * k + LANES]
            r = jnp.sqrt(jnp.where(voids > 0.5, 0.01, 0.01 + 0.99 * d * d * d))
            q = b / r
            up[4 * z + k] = q
            down[4 * z + k] = q
            root[4 * z + k] = r
            if z >= 3:
                up[4 * (5 + z) + k] = r
            if z < 5:
                down[4 * (8 + z) + k] = r


def fine_pack_kernel(low, up, root, high, left, right):
    at = 0
    for ref in (low, up, high):
        for i in range(32):
            left[at : at + 8] = ref[i, 0:8]
            right[at : at + 8] = ref[i, 8:16]
            at += 8
    for ref, first, count in ((low, 36, 16), (root, 0, 32), (high, 32, 16)):
        for i in range(first, first + count):
            left[at : at + 5] = ref[i, 0:5]
            right[at : at + 5] = ref[i, 11:16]
            at += 5


def fine_pre_kernel(counts, low, up, root, high, left, right, q, y, r, mid_q, mid_r, low1, high1, low2, high2, *scratch):
    natural, w = scratch[0], scratch[1:5]
    gz, xy = lax.axis_index("gz"), lax.axis_index("xy")
    masks = row_masks(4, 16 * xy - 8, 16 * counts[1])
    z_scale = z_mask(8 * gz - 8, 8 * counts[0])

    for n, ref in enumerate((low, up, high)):
        for i in range(32):
            j = 32 * n + i
            natural[j, 0:8] = left[8 * j : 8 * j + 8]
            natural[j, 8:24] = ref[i]
            natural[j, 24:32] = right[8 * j : 8 * j + 8]

    def begin(z):
        for k in range(4):
            for x in range(4):
                value = weave(natural, z, k, 4, 4, x)
                q[z, 4 * k + x] = value
                w[0][z, 4 * k + x] = FIRST * value

    loop(0, 24, begin)

    place = 0
    for ref, first, count in ((low, 32, 20), (root, 0, 32), (high, 32, 20)):
        for i in range(first, first + count):
            natural[place, 0:8] = jnp.zeros((8, LANES), F32)
            natural[place, 8:24] = ref[i]
            natural[place, 24:32] = jnp.zeros((8, LANES), F32)
            if 4 <= place < 68:
                j = 768 + 5 * (place - 4)
                natural[place, 3:8] = left[j : j + 5]
                natural[place, 24:29] = right[j : j + 5]
            place += 1

    def roots(z):
        for k in range(4):
            for x in range(4):
                r[z, 4 * k + x] = weave(natural, z, k, 4, 4, x)

    loop(0, 18, roots)
    smooth(w, q, 0, 24, 4, masks, z_scale, DEGREE)

    def total(z):
        for i in range(16):
            y[z, i] = (w[0][z + 8, i] + w[1][z + 8, i]) + (w[2][z + 8, i] + w[3][z + 8, i])

    loop(0, 8, total)

    def fold(m):
        for k in range(2):
            for x in range(2):
                sums, roots = None, None
                for z in range(2):
                    for i in (8 * k + 2 * x, 8 * k + 2 * x + 1, 8 * k + 2 * x + 4, 8 * k + 2 * x + 5):
                        a = r[2 * m + 1 + z, i]
                        b = a * q[2 * m + 4 + z, i]
                        sums = b if sums is None else sums + b
                        roots = a if roots is None else roots + a
                roots = 0.125 * roots
                mid_r[2 * m + k, pl.ds(x, 8, 2), :] = roots
                mid_q[2 * m + k, pl.ds(x, 8, 2), :] = 0.5 * sums / jnp.maximum(roots, LEAST)

    loop(0, 8, fold)
    for i in range(8):
        for near, far, first in ((low1, low2, 0), (high1, high2, 8)):
            values = mid_q[first + i, 2:14]
            near[12 * i : 12 * i + 12] = values
            far[12 * i : 12 * i + 12] = values
            values = mid_r[first + i, 2:14]
            near[96 + 12 * i : 108 + 12 * i] = values
            j = i - 4 if first == 0 else i
            if 0 <= j < 4:
                far[96 + 12 * j : 108 + 12 * j] = values


def mid_parts(refs):
    low2, low1, mid_q, mid_r, high1, high2 = refs

    def rows(field, z, k):
        if 8 <= z < 16:
            return (mid_q, mid_r)[field][2 * (z - 8) + k, 2:14]
        ref, z = [(low2, z), (low1, z - 4), None, None, (high1, z - 16), (high2, z - 20)][z // 4]
        if field == 1 and ref is low2:
            z = z - 2
        at = 96 * field + 12 * (2 * z + k)
        return ref[at : at + 12]

    return rows


def mid_pack_kernel(*refs):
    rows, left, right = mid_parts(refs[:6]), refs[6], refs[7]
    at = 0
    for z in range(24):
        for k in range(2):
            value = rows(0, z, k)
            right[at : at + 8] = value[0:8]
            left[at : at + 8] = value[4:12]
            at += 8
    for z in range(2, 22):
        for k in range(2):
            value = rows(1, z, k)
            right[at : at + 6] = value[2:8]
            left[at : at + 6] = value[4:10]
            at += 6


def mid_pre_kernel(counts, *refs):
    rows, (left, right), refs = mid_parts(refs[:6]), refs[6:8], refs[8:]
    q, y, r, coarse, coarse_low, coarse_high, coarse_root, natural = refs[:8]
    w = refs[8:]
    gz, xy = lax.axis_index("gz"), lax.axis_index("xy")
    masks = row_masks(4, 8 * xy - 10, 8 * counts[1])
    z_scale = z_mask(4 * gz - 10, 4 * counts[0])
    for z in range(24):
        for k in range(2):
            i = 2 * z + k
            natural[i, 0:8] = left[8 * i : 8 * i + 8]
            natural[i, 8:20] = rows(0, z, k)
            natural[i, 20:28] = right[8 * i : 8 * i + 8]
            natural[i, 28:32] = jnp.zeros((4, LANES), F32)

    def begin(z):
        for k in range(2):
            for x in range(4):
                value = weave(natural, z, k, 2, 4, x)
                q[z, 4 * k + x] = value
                w[0][z, 4 * k + x] = FIRST * value

    loop(0, 24, begin)
    for z in range(20):
        for k in range(2):
            i = 2 * z + k
            natural[i, 0:8] = jnp.zeros((8, LANES), F32)
            natural[i, 24:32] = jnp.zeros((8, LANES), F32)
            natural[i, 2:8] = left[384 + 6 * i : 390 + 6 * i]
            natural[i, 8:20] = rows(1, z + 2, k)
            natural[i, 20:26] = right[384 + 6 * i : 390 + 6 * i]

    def roots(z):
        for k in range(2):
            for x in range(4):
                r[z, 4 * k + x] = weave(natural, z, k, 2, 4, x)

    loop(0, 20, roots)
    smooth(w, q, 0, 24, 4, masks, z_scale, DEGREE)

    def total(z):
        for i in range(8):
            y[z, i] = (w[0][z + 7, i] + w[1][z + 7, i]) + (w[2][z + 7, i] + w[3][z + 7, i])

    loop(0, 10, total)

    for m in range(10):
        for x in range(2):
            sums, mean = None, None
            for z in range(2):
                for i in (2 * x, 2 * x + 1, 2 * x + 4, 2 * x + 5):
                    a = r[2 * m + z, i]
                    b = a * q[2 * m + 2 + z, i]
                    sums = b if sums is None else sums + b
                    mean = a if mean is None else mean + a
            mean = 0.125 * mean
            coarse_root[m, pl.ds(x, 8, 2), :] = mean
            if 0 < m < 9:
                coarse[m - 1, pl.ds(x, 8, 2), :] = 0.5 * sums / jnp.maximum(mean, LEAST)
    for m in range(2):
        coarse_low[m] = coarse[m]
        coarse_high[m] = coarse[6 + m]


def coarse_pack_kernel(*refs):
    parts, left, right = refs[:5], refs[5], refs[6]
    at = 0
    for ref in parts:
        for k in range(ref.shape[0]):
            right[at + k] = ref[k, 0:8]
            left[at + k] = ref[k, 8:16]
        at += ref.shape[0]


def finish_kernel(counts, *refs):
    parts, (left, right), refs = refs[:5], refs[5:7], refs[7:]
    coarse_root, mid_q, mid_y, mid_r, fine_q, fine_y, fine_r, out_x, out_r = refs[:9]
    natural, cq, error, spread, mq, mt, fq, ft, plain_x, plain_r, rows_x, rows_r = refs[9:21]
    cw, mw, fw = refs[21:25], refs[25:29], refs[29:33]
    gz, xy = lax.axis_index("gz"), lax.axis_index("xy")

    at = 0
    for ref in parts:
        for k in range(ref.shape[0]):
            natural[at, 0:4] = left[at, 2:6]
            natural[at, 4:14] = ref[k, 2:12]
            natural[at, 14:18] = right[at, 0:4]
            natural[at, 18:24] = jnp.zeros((6, LANES), F32)
            for x in range(3):
                value = weave(natural, at, 0, 1, 3, x)
                cq[at, x] = value
                cw[0][at, x] = FIRST * value
            at += 1
    masks = row_masks(3, 4 * xy - 7, 4 * counts[1])
    smooth(cw, cq, 0, 16, 3, masks, z_mask(2 * gz - 7, 2 * counts[0]), DEGREE - 1)
    for k in range(10):
        for x in range(3):
            total = (cw[0][k + 3, x] + cw[1][k + 3, x]) + (cw[2][k + 3, x] + cw[3][k + 3, x])
            natural[k, pl.ds(x, 8, 3), :] = total
        error[k] = natural[k, 2:18] / jnp.maximum(coarse_root[k], LEAST)

    for k in range(10):
        for x in range(4):
            value = error[k, pl.ds(x >> 1, 8, 2), :]
            for i in (x, 4 + x):
                mt[2 * k + 2, i] = mid_r[2 * k, i] * value
                mt[2 * k + 3, i] = mid_r[2 * k + 1, i] * value

    masks = row_masks(4, 8 * xy - 10, 8 * counts[1])
    z_scale = z_mask(4 * gz - 10, 4 * counts[0])

    def mid_correct(z):
        _, rest = applied(mt, z, 4, mid_q)
        scales = [z_scale(z, FIRST) * mask for mask in masks]
        for i, value in enumerate(rest):
            mq[z, i] = value
            mw[0][z, i] = scales[i % 4] * value

    loop(4, 20, mid_correct)
    smooth(mw, mq, 4, 20, 4, masks, z_scale, DEGREE - 1)

    def mid_error(z):
        for k in range(2):
            for x in range(4):
                i = 4 * k + x
                total = (mw[0][z, i] + mw[1][z, i]) + (mw[2][z, i] + mw[3][z, i])
                total = total + (mid_y[z - 7, i] + mt[z, i])
                spread[2 * (z - 7) + k, pl.ds(x, 8, 4), :] = total / jnp.maximum(mid_r[z - 2, i], LEAST)

    loop(7, 17, mid_error)

    def fine_prolong(k):
        for j in range(2):
            for x in range(4):
                value = spread[2 * k + j, pl.ds(6 + (x >> 1), 8, 2), :]
                for i in (8 * j + x, 8 * j + 4 + x):
                    ft[2 * k + 2, i] = fine_r[jnp.maximum(2 * k - 1, 0), i] * value
                    ft[2 * k + 3, i] = fine_r[jnp.minimum(2 * k, 17), i] * value

    loop(0, 10, fine_prolong, 1)
    masks = row_masks(4, 16 * xy - 8, 16 * counts[1])
    z_scale = z_mask(8 * gz - 8, 8 * counts[0])

    def fine_correct(z):
        _, rest = applied(ft, z, 4, fine_q)
        scales = [z_scale(z, FIRST) * mask for mask in masks]
        for i, value in enumerate(rest):
            fq[z, i] = value
            fw[0][z, i] = scales[i % 4] * value

    loop(4, 20, fine_correct)

    def finish(z, rest):
        for k in range(4):
            for x in range(4):
                i = 4 * k + x
                r = fine_r[z - 3, i]
                total = (fw[0][z, i] + fw[1][z, i]) + (fw[2][z, i] + fw[3][z, i])
                total = total + (fine_y[z - 8, i] + ft[z, i])
                plain_x[4 * (z - 8) + k, pl.ds(x, 8, 4), :] = total / r
                plain_r[4 * (z - 8) + k, pl.ds(x, 8, 4), :] = r * rest[i]

    smooth(fw, fq, 4, 20, 4, masks, z_scale, DEGREE, finish)
    matrix = weave_matrix(1)
    for plain, rows, out in ((plain_x, rows_x, out_x), (plain_r, rows_r, out_r)):
        for z in range(8):
            for k in range(4):
                rows[16 * z : 16 * z + 16, LANES * k : LANES * k + LANES] = plain[4 * z + k, 8:24]
        out[...] = exact_product(rows[...], matrix).reshape(8, 16, 512)


def call(kernel, operands, out_shapes, scratch=(), space=pltpu.VMEM):
    whole = pl.BlockSpec(memory_space=pltpu.VMEM)
    return pl.pallas_call(
        kernel,
        out_shape=[jax.ShapeDtypeStruct(s, F32) for s in out_shapes],
        in_specs=[pl.BlockSpec(memory_space=space)] * len(operands),
        out_specs=[whole] * len(out_shapes),
        scratch_shapes=[pltpu.VMEM(s, F32) if isinstance(s, tuple) else s for s in scratch],
        compiler_params=pltpu.CompilerParams(vmem_limit_bytes=30 * 1024 * 1024),
    )(*operands)


def send(block, axis, shift):
    count = lax.axis_size(axis)
    pairs = [(i, i + shift) for i in range(count) if 0 <= i + shift < count]
    return lax.ppermute(block, axis, pairs)


def with_counts(kernel):
    counts = (lax.axis_size("gz"), lax.axis_size("xy"))
    return lambda *refs: kernel(counts, *refs)


def on_device(load_field, density, void_mask):
    up, down, root = call(
        scale_kernel,
        (load_field, density, void_mask),
        [(52, 16, LANES), (52, 16, LANES), (32, 16, LANES)],
        [(16, 16, 512), pltpu.VMEM((1, 2, 64), jnp.int32), pltpu.SemaphoreType.DMA((3,))],
        pl.ANY,
    )
    low, high = send(up, "gz", 1), send(down, "gz", -1)
    to_left, to_right = call(fine_pack_kernel, (low, up, root, high), [(1088, LANES)] * 2)
    left, right = send(to_right, "xy", 1), send(to_left, "xy", -1)
    fine = (24, 16, 8, LANES)
    fine_q, fine_y, fine_r, mid_q, mid_r, low1, high1, low2, high2 = call(
        with_counts(fine_pre_kernel),
        (low, up, root, high, left, right),
        [fine, (8, 16, 8, LANES), (18, 16, 8, LANES)] + [(16, 16, LANES)] * 2 + [(192, LANES)] * 2 + [(144, LANES)] * 2,
        [(96, 32, LANES)] + [fine] * 4,
    )
    a1, b1 = send(low1, "gz", 1), send(high1, "gz", -1)
    a2, b2 = send(low2, "gz", 2), send(high2, "gz", -2)
    parts = (a2, a1, mid_q, mid_r, b1, b2)
    to_left, to_right = call(mid_pack_kernel, parts, [(624, LANES)] * 2)
    left, right = send(to_right, "xy", 1), send(to_left, "xy", -1)
    mid = (24, 8, 8, LANES)
    mid_q, mid_y, mid_r, coarse, coarse_low, coarse_high, coarse_root = call(
        with_counts(mid_pre_kernel),
        parts + (left, right),
        [mid, (10, 8, 8, LANES), (20, 8, 8, LANES), (8, 16, LANES)] + [(2, 16, LANES)] * 2 + [(10, 16, LANES)],
        [(48, 32, LANES)] + [mid] * 4,
    )
    a1, b1 = send(coarse_low, "gz", 1), send(coarse_high, "gz", -1)
    a2, b2 = send(coarse_low, "gz", 2), send(coarse_high, "gz", -2)
    parts = (a2, a1, coarse, b1, b2)
    to_left, to_right = call(coarse_pack_kernel, parts, [(16, 8, LANES)] * 2)
    left, right = send(to_right, "xy", 1), send(to_left, "xy", -1)
    coarsest = (16, 3, 8, LANES)
    return tuple(
        call(
            with_counts(finish_kernel),
            parts + (left, right, coarse_root, mid_q, mid_y, mid_r, fine_q, fine_y, fine_r),
            [(8, 16, 512), (8, 16, 512)],
            [(16, 24, LANES), coarsest, (10, 16, LANES), (20, 32, LANES), mid, mid, fine, fine]
            + [(32, 32, LANES)] * 2
            + [(128, 512)] * 2
            + [coarsest] * 4
            + [mid] * 4
            + [fine] * 4,
        )
    )


def solution(mesh):
    specs = (P("gz", "xy", None), P("gz", "xy", None), P("gz", "xy", None))
    return jax.shard_map(
        on_device, mesh=mesh, in_specs=specs, out_specs=specs[:2], check_vma=False
    )
```

```python
import jax
import jax.numpy as jnp
from jax import lax
from jax.experimental import pallas as pl
from jax.experimental.pallas import tpu as pltpu
from jax.sharding import PartitionSpec as P


DEGREE = 4
THETA = 1.15
DELTA = 0.85
FIRST = 1.0 / (6.0 * THETA)
LEAST = 0.05
F32 = jnp.float32
LANES = 128


def coefficients():
    sigma = THETA / DELTA
    rho = 1.0 / sigma
    pairs = []
    for turn in range(DEGREE - 1):
        rho_next = 1.0 / (2.0 * sigma - rho)
        pairs.append((rho_next * rho, 2.0 * rho_next / (6.0 * DELTA)))
        rho = rho_next
    return pairs


COEFFICIENTS = coefficients()


def iota(shape, dim):
    return lax.broadcasted_iota(jnp.int32, shape, dim)


def row_masks(n, base, count):
    masks = []
    for x in range(n):
        place = n * iota((8, LANES), 0) + (x + base)
        masks.append(jnp.where((place >= 0) & (place < count), 1.0, 0.0).astype(F32))
    return masks


def z_mask(base, count):
    def scaled(z, value):
        place = z + base
        return jnp.where((place >= 0) & (place < count), F32(value), F32(0.0))

    return scaled


def loop(low, high, body, width=2):
    turns = (high - low) // width

    def step(t, carry):
        for j in range(width):
            body(low + width * t + j)
        return carry

    if turns > 0:
        lax.fori_loop(0, turns, step, 0)
    for z in range(low + turns * width, high):
        body(z)


def around(ref, z, n):
    count = ref.shape[1]
    blocks = count // n
    here = [ref[z, i] for i in range(count)]
    lane = iota((8, LANES), 1)
    before = [jnp.where(lane == 0, 0.0, pltpu.roll(here[(blocks - 1) * n + x], 1, 1)) for x in range(n)]
    after = [jnp.where(lane == LANES - 1, 0.0, pltpu.roll(here[x], LANES - 1, 1)) for x in range(n)]
    total = []
    for k in range(blocks):
        row = here[k * n : k * n + n]
        up = pltpu.roll(row[n - 1], 1, 0)
        down = pltpu.roll(row[0], 7, 0)
        for x in range(n):
            i = k * n + x
            left = here[i - n] if k > 0 else before[x]
            right = here[i + n] if k + 1 < blocks else after[x]
            north = row[x - 1] if x > 0 else up
            south = row[x + 1] if x + 1 < n else down
            total.append(((left + right) + (north + south)) + (ref[z - 1, i] + ref[z + 1, i]))
    return here, total


def applied(ref, z, n, q):
    here, total = around(ref, z, n)
    return here, [q[z, i] - (6.0 * here[i] - total[i]) for i in range(len(here))]


def smooth(w, q, low, high, n, masks, z_scale, passes, finish=None):
    for turn in range(passes):

        def advance(z, turn=turn):
            here, rest = applied(w[turn], z, n, q)
            if finish is not None and turn == DEGREE - 1:
                finish(z, rest)
                return
            if turn < passes - 1 or passes == DEGREE:
                for i, value in enumerate(rest):
                    q[z, i] = value
            if turn < DEGREE - 1:
                c1, c2 = COEFFICIENTS[turn]
                scales = [z_scale(z, c2) * mask for mask in masks]
                for i, value in enumerate(rest):
                    w[turn + 1][z, i] = c1 * here[i] + scales[i % n] * value

        loop(low + 1 + turn, high - 1 - turn, advance)


def weave(source, z, k, blocks, n, x):
    return source[z * blocks + k, pl.ds(x, 8, n), :]


def exact_product(left, right):
    high = left.astype(jnp.bfloat16)
    rest = left - high.astype(F32)
    middle = rest.astype(jnp.bfloat16)
    low = (rest - middle.astype(F32)).astype(jnp.bfloat16)
    parts = [jnp.dot(part, right, preferred_element_type=F32) for part in (high, middle, low)]
    return (parts[2] + parts[1]) + parts[0]


def weave_matrix(dim):
    plain, woven = iota((512, 512), dim), iota((512, 512), 1 - dim)
    same = plain == 4 * (woven & (LANES - 1)) + (woven >> 7)
    return jnp.where(same, 1.0, 0.0).astype(jnp.bfloat16)


def scale_kernel(load_hbm, density_hbm, void_hbm, up, down, root, both, void, sems):
    copies = [
        pltpu.make_async_copy(load_hbm, both.at[pl.ds(0, 8)], sems.at[0]),
        pltpu.make_async_copy(density_hbm, both.at[pl.ds(8, 8)], sems.at[1]),
        pltpu.make_async_copy(void_hbm, void, sems.at[2]),
    ]
    for copy in copies:
        copy.start()
    matrix = weave_matrix(0)
    copies[2].wait()
    bricks = jnp.where(void[0] == 1, 1.0, 0.0).astype(F32)
    bricks = jnp.concatenate([jnp.broadcast_to(bricks[k : k + 1], (8, 64)) for k in range(2)], axis=0)
    spread = jnp.where((iota((64, LANES), 1) >> 1) == iota((64, LANES), 0), 1.0, 0.0).astype(jnp.bfloat16)
    voids = jnp.dot(bricks.astype(jnp.bfloat16), spread, preferred_element_type=F32)
    copies[0].wait()
    copies[1].wait()
    fields = exact_product(both[...].reshape(256, 512), matrix)
    for z in range(8):
        for k in range(4):
            b = fields[16 * z : 16 * z + 16, LANES * k : LANES * k + LANES]
            d = fields[128 + 16 * z : 144 + 16 * z, LANES * k : LANES * k + LANES]
            r = jnp.sqrt(jnp.where(voids > 0.5, 0.01, 0.01 + 0.99 * d * d * d))
            q = b / r
            up[4 * z + k] = q
            down[4 * z + k] = q
            root[4 * z + k] = r
            if z >= 3:
                up[4 * (5 + z) + k] = r
            if z < 5:
                down[4 * (8 + z) + k] = r


def fine_pack_kernel(low, up, root, high, left, right):
    at = 0
    for ref in (low, up, high):
        for i in range(32):
            left[at : at + 8] = ref[i, 0:8]
            right[at : at + 8] = ref[i, 8:16]
            at += 8
    for ref, first, count in ((low, 36, 16), (root, 0, 32), (high, 32, 16)):
        for i in range(first, first + count):
            left[at : at + 5] = ref[i, 0:5]
            right[at : at + 5] = ref[i, 11:16]
            at += 5


def fine_pre_kernel(counts, low, up, root, high, left, right, q, y, r, mid_q, mid_r, early, late, *scratch):
    natural, w = scratch[0], scratch[1:5]
    gz, xy = lax.axis_index("gz"), lax.axis_index("xy")
    masks = row_masks(4, 16 * xy - 8, 16 * counts[1])
    z_scale = z_mask(8 * gz - 8, 8 * counts[0])

    for n, ref in enumerate((low, up, high)):
        for i in range(32):
            j = 32 * n + i
            natural[j, 0:8] = left[8 * j : 8 * j + 8]
            natural[j, 8:24] = ref[i]
            natural[j, 24:32] = right[8 * j : 8 * j + 8]

    def begin(z):
        for k in range(4):
            for x in range(4):
                value = weave(natural, z, k, 4, 4, x)
                q[z, 4 * k + x] = value
                w[0][z, 4 * k + x] = FIRST * value

    loop(0, 24, begin)

    place = 0
    for ref, first, count in ((low, 32, 20), (root, 0, 32), (high, 32, 20)):
        for i in range(first, first + count):
            natural[place, 0:8] = jnp.zeros((8, LANES), F32)
            natural[place, 8:24] = ref[i]
            natural[place, 24:32] = jnp.zeros((8, LANES), F32)
            if 4 <= place < 68:
                j = 768 + 5 * (place - 4)
                natural[place, 3:8] = left[j : j + 5]
                natural[place, 24:29] = right[j : j + 5]
            place += 1

    def roots(z):
        for k in range(4):
            for x in range(4):
                r[z, 4 * k + x] = weave(natural, z, k, 4, 4, x)

    loop(0, 18, roots)
    smooth(w, q, 0, 24, 4, masks, z_scale, DEGREE)

    def total(z):
        for i in range(16):
            y[z, i] = (w[0][z + 8, i] + w[1][z + 8, i]) + (w[2][z + 8, i] + w[3][z + 8, i])

    loop(0, 8, total)

    def fold(m):
        for k in range(2):
            for x in range(2):
                sums, roots = None, None
                for z in range(2):
                    for i in (8 * k + 2 * x, 8 * k + 2 * x + 1, 8 * k + 2 * x + 4, 8 * k + 2 * x + 5):
                        a = r[2 * m + 1 + z, i]
                        b = a * q[2 * m + 4 + z, i]
                        sums = b if sums is None else sums + b
                        roots = a if roots is None else roots + a
                roots = 0.125 * roots
                mid_r[2 * m + k, pl.ds(x, 8, 2), :] = roots
                mid_q[2 * m + k, pl.ds(x, 8, 2), :] = 0.5 * sums / jnp.maximum(roots, LEAST)

    loop(0, 8, fold)
    skip = jnp.where(gz % 4 == 3, 0, 2)
    for out, start in ((early, skip), (late, 2 - skip)):
        for i in range(16):
            out[12 * i : 12 * i + 12] = mid_q[i, 2:14]
        for i in range(12):
            out[192 + 12 * i : 204 + 12 * i] = mid_r[2 * start + i, 2:14]


def mid_pairs(count):
    first, second = [], []
    for i in range(count):
        up, down = (first, second) if i % 4 != 3 else (second, first)
        if i + 2 < count:
            up.append((i, i + 2))
        if i >= 2:
            down.append((i, i - 2))
    return first, second + [(0, 1), (count - 1, count - 2)]


def mid_sides(count, gz, first, second, low, high):
    @pl.when(gz % 4 != 1)
    def _():
        low[...] = first[...]
        high[...] = second[...]

    @pl.when(gz % 4 == 1)
    def _():
        low[...] = second[...]
        high[...] = first[...]

    @pl.when(gz == 1)
    def _():
        low[0:96] = jnp.zeros((96, LANES), F32)
        low[96:192] = second[0:96]
        low[192:240] = jnp.zeros((48, LANES), F32)
        low[240:336] = second[192:288]

    @pl.when(gz == count - 2)
    def _():
        high[0:96] = second[96:192]
        high[96:192] = jnp.zeros((96, LANES), F32)
        high[192:288] = second[240:336]
        high[288:336] = jnp.zeros((48, LANES), F32)


def mid_parts(low, high, mid_q, mid_r):
    def rows(field, z, k):
        if 8 <= z < 16:
            return (mid_q, mid_r)[field][2 * (z - 8) + k, 2:14]
        at = 12 * (2 * (z if z < 8 else z - 16) + k)
        if field == 1:
            at = at + (192 if z >= 16 else 144)
        return (low if z < 8 else high)[at : at + 12]

    return rows


def mid_pack_kernel(counts, first, second, mid_q, mid_r, low, high, left, right):
    mid_sides(counts[0], lax.axis_index("gz"), first, second, low, high)
    rows = mid_parts(low, high, mid_q, mid_r)
    at = 0
    for z in range(24):
        for k in range(2):
            value = rows(0, z, k)
            right[at : at + 8] = value[0:8]
            left[at : at + 8] = value[4:12]
            at += 8
    for z in range(2, 22):
        for k in range(2):
            value = rows(1, z, k)
            right[at : at + 6] = value[2:8]
            left[at : at + 6] = value[4:10]
            at += 6


def mid_pre_kernel(counts, *refs):
    rows, (left, right), refs = mid_parts(*refs[:4]), refs[4:6], refs[6:]
    q, y, r, coarse, coarse_low, coarse_high, coarse_root, natural = refs[:8]
    w = refs[8:]
    gz, xy = lax.axis_index("gz"), lax.axis_index("xy")
    masks = row_masks(4, 8 * xy - 10, 8 * counts[1])
    z_scale = z_mask(4 * gz - 10, 4 * counts[0])
    for z in range(24):
        for k in range(2):
            i = 2 * z + k
            natural[i, 0:8] = left[8 * i : 8 * i + 8]
            natural[i, 8:20] = rows(0, z, k)
            natural[i, 20:28] = right[8 * i : 8 * i + 8]
            natural[i, 28:32] = jnp.zeros((4, LANES), F32)

    def begin(z):
        for k in range(2):
            for x in range(4):
                value = weave(natural, z, k, 2, 4, x)
                q[z, 4 * k + x] = value
                w[0][z, 4 * k + x] = FIRST * value

    loop(0, 24, begin)
    for z in range(20):
        for k in range(2):
            i = 2 * z + k
            natural[i, 0:8] = jnp.zeros((8, LANES), F32)
            natural[i, 24:32] = jnp.zeros((8, LANES), F32)
            natural[i, 2:8] = left[384 + 6 * i : 390 + 6 * i]
            natural[i, 8:20] = rows(1, z + 2, k)
            natural[i, 20:26] = right[384 + 6 * i : 390 + 6 * i]

    def roots(z):
        for k in range(2):
            for x in range(4):
                r[z, 4 * k + x] = weave(natural, z, k, 2, 4, x)

    loop(0, 20, roots)
    smooth(w, q, 0, 24, 4, masks, z_scale, DEGREE)

    def total(z):
        for i in range(8):
            y[z, i] = (w[0][z + 7, i] + w[1][z + 7, i]) + (w[2][z + 7, i] + w[3][z + 7, i])

    loop(0, 10, total)

    for m in range(10):
        for x in range(2):
            sums, mean = None, None
            for z in range(2):
                for i in (2 * x, 2 * x + 1, 2 * x + 4, 2 * x + 5):
                    a = r[2 * m + z, i]
                    b = a * q[2 * m + 2 + z, i]
                    sums = b if sums is None else sums + b
                    mean = a if mean is None else mean + a
            mean = 0.125 * mean
            coarse_root[m, pl.ds(x, 8, 2), :] = mean
            if 0 < m < 9:
                coarse[m - 1, pl.ds(x, 8, 2), :] = 0.5 * sums / jnp.maximum(mean, LEAST)
    for m in range(4):
        coarse_low[m] = coarse[m]
        coarse_high[m] = coarse[4 + m]


def coarse_pack_kernel(*refs):
    parts, left, right = refs[:3], refs[3], refs[4]
    at = 0
    for ref in parts:
        for k in range(ref.shape[0]):
            right[at + k] = ref[k, 0:8]
            left[at + k] = ref[k, 8:16]
        at += ref.shape[0]


def finish_kernel(counts, *refs):
    parts, (left, right), refs = refs[:3], refs[3:5], refs[5:]
    coarse_root, mid_q, mid_y, mid_r, fine_q, fine_y, fine_r, out_x, out_r = refs[:9]
    natural, cq, error, spread, mq, mt, fq, ft, plain_x, plain_r, rows_x, rows_r = refs[9:21]
    cw, mw, fw = refs[21:25], refs[25:29], refs[29:33]
    gz, xy = lax.axis_index("gz"), lax.axis_index("xy")

    at = 0
    for ref in parts:
        for k in range(ref.shape[0]):
            natural[at, 0:4] = left[at, 2:6]
            natural[at, 4:14] = ref[k, 2:12]
            natural[at, 14:18] = right[at, 0:4]
            natural[at, 18:24] = jnp.zeros((6, LANES), F32)
            for x in range(3):
                value = weave(natural, at, 0, 1, 3, x)
                cq[at, x] = value
                cw[0][at, x] = FIRST * value
            at += 1
    masks = row_masks(3, 4 * xy - 7, 4 * counts[1])
    smooth(cw, cq, 0, 16, 3, masks, z_mask(2 * gz - 7, 2 * counts[0]), DEGREE - 1)
    for k in range(10):
        for x in range(3):
            total = (cw[0][k + 3, x] + cw[1][k + 3, x]) + (cw[2][k + 3, x] + cw[3][k + 3, x])
            natural[k, pl.ds(x, 8, 3), :] = total
        error[k] = natural[k, 2:18] / jnp.maximum(coarse_root[k], LEAST)

    for k in range(10):
        for x in range(4):
            value = error[k, pl.ds(x >> 1, 8, 2), :]
            for i in (x, 4 + x):
                mt[2 * k + 2, i] = mid_r[2 * k, i] * value
                mt[2 * k + 3, i] = mid_r[2 * k + 1, i] * value

    masks = row_masks(4, 8 * xy - 10, 8 * counts[1])
    z_scale = z_mask(4 * gz - 10, 4 * counts[0])

    def mid_correct(z):
        _, rest = applied(mt, z, 4, mid_q)
        scales = [z_scale(z, FIRST) * mask for mask in masks]
        for i, value in enumerate(rest):
            mq[z, i] = value
            mw[0][z, i] = scales[i % 4] * value

    loop(4, 20, mid_correct)
    smooth(mw, mq, 4, 20, 4, masks, z_scale, DEGREE - 1)

    def mid_error(z):
        for k in range(2):
            for x in range(4):
                i = 4 * k + x
                total = (mw[0][z, i] + mw[1][z, i]) + (mw[2][z, i] + mw[3][z, i])
                total = total + (mid_y[z - 7, i] + mt[z, i])
                spread[2 * (z - 7) + k, pl.ds(x, 8, 4), :] = total / jnp.maximum(mid_r[z - 2, i], LEAST)

    loop(7, 17, mid_error)

    def fine_prolong(k):
        for j in range(2):
            for x in range(4):
                value = spread[2 * k + j, pl.ds(6 + (x >> 1), 8, 2), :]
                for i in (8 * j + x, 8 * j + 4 + x):
                    ft[2 * k + 2, i] = fine_r[jnp.maximum(2 * k - 1, 0), i] * value
                    ft[2 * k + 3, i] = fine_r[jnp.minimum(2 * k, 17), i] * value

    loop(0, 10, fine_prolong, 1)
    masks = row_masks(4, 16 * xy - 8, 16 * counts[1])
    z_scale = z_mask(8 * gz - 8, 8 * counts[0])

    def fine_correct(z):
        _, rest = applied(ft, z, 4, fine_q)
        scales = [z_scale(z, FIRST) * mask for mask in masks]
        for i, value in enumerate(rest):
            fq[z, i] = value
            fw[0][z, i] = scales[i % 4] * value

    loop(4, 20, fine_correct)

    def finish(z, rest):
        for k in range(4):
            for x in range(4):
                i = 4 * k + x
                r = fine_r[z - 3, i]
                total = (fw[0][z, i] + fw[1][z, i]) + (fw[2][z, i] + fw[3][z, i])
                total = total + (fine_y[z - 8, i] + ft[z, i])
                plain_x[4 * (z - 8) + k, pl.ds(x, 8, 4), :] = total / r
                plain_r[4 * (z - 8) + k, pl.ds(x, 8, 4), :] = r * rest[i]

    smooth(fw, fq, 4, 20, 4, masks, z_scale, DEGREE, finish)
    matrix = weave_matrix(1)
    for plain, rows, out in ((plain_x, rows_x, out_x), (plain_r, rows_r, out_r)):
        for z in range(8):
            for k in range(4):
                rows[16 * z : 16 * z + 16, LANES * k : LANES * k + LANES] = plain[4 * z + k, 8:24]
        out[...] = exact_product(rows[...], matrix).reshape(8, 16, 512)


def call(kernel, operands, out_shapes, scratch=(), space=pltpu.VMEM):
    whole = pl.BlockSpec(memory_space=pltpu.VMEM)
    return pl.pallas_call(
        kernel,
        out_shape=[jax.ShapeDtypeStruct(s, F32) for s in out_shapes],
        in_specs=[pl.BlockSpec(memory_space=space)] * len(operands),
        out_specs=[whole] * len(out_shapes),
        scratch_shapes=[pltpu.VMEM(s, F32) if isinstance(s, tuple) else s for s in scratch],
        compiler_params=pltpu.CompilerParams(vmem_limit_bytes=30 * 1024 * 1024),
    )(*operands)


def send(block, axis, shift):
    count = lax.axis_size(axis)
    pairs = [(i, i + shift) for i in range(count) if 0 <= i + shift < count]
    return lax.ppermute(block, axis, pairs)


def with_counts(kernel):
    counts = (lax.axis_size("gz"), lax.axis_size("xy"))
    return lambda *refs: kernel(counts, *refs)


def on_device(load_field, density, void_mask):
    up, down, root = call(
        scale_kernel,
        [pltpu.with_memory_space_constraint(x, pltpu.HBM) for x in (load_field, density, void_mask)],
        [(52, 16, LANES), (52, 16, LANES), (32, 16, LANES)],
        [(16, 16, 512), pltpu.VMEM((1, 2, 64), jnp.int32), pltpu.SemaphoreType.DMA((3,))],
        pltpu.HBM,
    )
    low, high = send(up, "gz", 1), send(down, "gz", -1)
    to_left, to_right = call(fine_pack_kernel, (low, up, root, high), [(1088, LANES)] * 2)
    left, right = send(to_right, "xy", 1), send(to_left, "xy", -1)
    fine = (24, 16, 8, LANES)
    fine_q, fine_y, fine_r, mid_q, mid_r, first, second = call(
        with_counts(fine_pre_kernel),
        (low, up, root, high, left, right),
        [fine, (8, 16, 8, LANES), (18, 16, 8, LANES)] + [(16, 16, LANES)] * 2 + [(336, LANES)] * 2,
        [(96, 32, LANES)] + [fine] * 4,
    )
    pairs = mid_pairs(lax.axis_size("gz"))
    first, second = lax.ppermute(first, "gz", pairs[0]), lax.ppermute(second, "gz", pairs[1])
    low, high, to_left, to_right = call(
        with_counts(mid_pack_kernel), (first, second, mid_q, mid_r), [(336, LANES)] * 2 + [(624, LANES)] * 2
    )
    left, right = send(to_right, "xy", 1), send(to_left, "xy", -1)
    mid = (24, 8, 8, LANES)
    mid_q, mid_y, mid_r, coarse, coarse_low, coarse_high, coarse_root = call(
        with_counts(mid_pre_kernel),
        (low, high, mid_q, mid_r, left, right),
        [mid, (10, 8, 8, LANES), (20, 8, 8, LANES), (8, 16, LANES)] + [(4, 16, LANES)] * 2 + [(10, 16, LANES)],
        [(48, 32, LANES)] + [mid] * 4,
    )
    parts = (send(coarse_low, "gz", 2), coarse, send(coarse_high, "gz", -2))
    to_left, to_right = call(coarse_pack_kernel, parts, [(16, 8, LANES)] * 2)
    left, right = send(to_right, "xy", 1), send(to_left, "xy", -1)
    coarsest = (16, 3, 8, LANES)
    return tuple(
        call(
            with_counts(finish_kernel),
            parts + (left, right, coarse_root, mid_q, mid_y, mid_r, fine_q, fine_y, fine_r),
            [(8, 16, 512), (8, 16, 512)],
            [(16, 24, LANES), coarsest, (10, 16, LANES), (20, 32, LANES), mid, mid, fine, fine]
            + [(32, 32, LANES)] * 2
            + [(128, 512)] * 2
            + [coarsest] * 4
            + [mid] * 4
            + [fine] * 4,
        )
    )


def solution(mesh):
    specs = (P("gz", "xy", None), P("gz", "xy", None), P("gz", "xy", None))
    return jax.shard_map(
        on_device, mesh=mesh, in_specs=specs, out_specs=specs[:2], check_vma=False
    )
```

```python
import jax
import jax.numpy as jnp
from jax import lax
from jax.experimental import pallas as pl
from jax.experimental.pallas import tpu as pltpu
from jax.sharding import PartitionSpec as P


DEGREE = 4
THETA = 1.15
DELTA = 0.85
FIRST = 1.0 / (6.0 * THETA)
LEAST = 0.05
F32 = jnp.float32
LANES = 128


def coefficients():
    sigma = THETA / DELTA
    rho = 1.0 / sigma
    pairs = []
    for turn in range(DEGREE - 1):
        rho_next = 1.0 / (2.0 * sigma - rho)
        pairs.append((rho_next * rho, 2.0 * rho_next / (6.0 * DELTA)))
        rho = rho_next
    return pairs


COEFFICIENTS = coefficients()


def iota(shape, dim):
    return lax.broadcasted_iota(jnp.int32, shape, dim)


def row_masks(n, base, count):
    masks = []
    for x in range(n):
        place = n * iota((8, LANES), 0) + (x + base)
        masks.append(jnp.where((place >= 0) & (place < count), 1.0, 0.0).astype(F32))
    return masks


def z_mask(base, count):
    def scaled(z, value):
        place = z + base
        return jnp.where((place >= 0) & (place < count), F32(value), F32(0.0))

    return scaled


def loop(low, high, body, width=24):
    turns = (high - low) // width if high - low > width else 0

    def step(t, carry):
        for j in range(width):
            body(low + width * t + j)
        return carry

    if turns > 0:
        lax.fori_loop(0, turns, step, 0)
    for z in range(low + turns * width, high):
        body(z)


def around(ref, z, n):
    count = ref.shape[1]
    blocks = count // n
    here = [ref[z, i] for i in range(count)]
    lane = iota((8, LANES), 1)
    before = [jnp.where(lane == 0, 0.0, pltpu.roll(here[(blocks - 1) * n + x], 1, 1)) for x in range(n)]
    after = [jnp.where(lane == LANES - 1, 0.0, pltpu.roll(here[x], LANES - 1, 1)) for x in range(n)]
    total = []
    for k in range(blocks):
        row = here[k * n : k * n + n]
        up = pltpu.roll(row[n - 1], 1, 0)
        down = pltpu.roll(row[0], 7, 0)
        for x in range(n):
            i = k * n + x
            left = here[i - n] if k > 0 else before[x]
            right = here[i + n] if k + 1 < blocks else after[x]
            north = row[x - 1] if x > 0 else up
            south = row[x + 1] if x + 1 < n else down
            total.append(((left + right) + (north + south)) + (ref[z - 1, i] + ref[z + 1, i]))
    return here, total


def applied(ref, z, n, q):
    here, total = around(ref, z, n)
    return here, [q[z, i] - (6.0 * here[i] - total[i]) for i in range(len(here))]


def smooth(w, q, low, high, n, masks, z_scale, passes, finish=None, width=24):
    for turn in range(passes):

        def advance(z, turn=turn):
            here, rest = applied(w[turn], z, n, q)
            if finish is not None and turn == DEGREE - 1:
                finish(z, rest)
                return
            if turn < passes - 1 or passes == DEGREE:
                for i, value in enumerate(rest):
                    q[z, i] = value
            if turn < DEGREE - 1:
                c1, c2 = COEFFICIENTS[turn]
                scales = [z_scale(z, c2) * mask for mask in masks]
                for i, value in enumerate(rest):
                    w[turn + 1][z, i] = c1 * here[i] + scales[i % n] * value

        loop(low + 1 + turn, high - 1 - turn, advance, width)


def weave(source, z, k, blocks, n, x):
    return source[z * blocks + k, pl.ds(x, 8, n), :]


def exact_product(left, right):
    high = left.astype(jnp.bfloat16)
    rest = left - high.astype(F32)
    middle = rest.astype(jnp.bfloat16)
    low = (rest - middle.astype(F32)).astype(jnp.bfloat16)
    parts = [jnp.dot(part, right, preferred_element_type=F32) for part in (high, middle, low)]
    return (parts[2] + parts[1]) + parts[0]


def weave_matrix(dim):
    plain, woven = iota((512, 512), dim), iota((512, 512), 1 - dim)
    same = plain == 4 * (woven & (LANES - 1)) + (woven >> 7)
    return jnp.where(same, 1.0, 0.0).astype(jnp.bfloat16)


def scale_kernel(load_hbm, density_hbm, void_hbm, up, down, root, both, void, sems):
    copies = [
        pltpu.make_async_copy(load_hbm, both.at[pl.ds(0, 8)], sems.at[0]),
        pltpu.make_async_copy(density_hbm, both.at[pl.ds(8, 8)], sems.at[1]),
        pltpu.make_async_copy(void_hbm, void, sems.at[2]),
    ]
    for copy in copies:
        copy.start()
    matrix = weave_matrix(0)
    copies[2].wait()
    bricks = jnp.where(void[0] == 1, 1.0, 0.0).astype(F32)
    bricks = jnp.concatenate([jnp.broadcast_to(bricks[k : k + 1], (8, 64)) for k in range(2)], axis=0)
    spread = jnp.where((iota((64, LANES), 1) >> 1) == iota((64, LANES), 0), 1.0, 0.0).astype(jnp.bfloat16)
    voids = jnp.dot(bricks.astype(jnp.bfloat16), spread, preferred_element_type=F32)
    copies[0].wait()
    copies[1].wait()
    fields = exact_product(both[...].reshape(256, 512), matrix)
    for z in range(8):
        for k in range(4):
            b = fields[16 * z : 16 * z + 16, LANES * k : LANES * k + LANES]
            d = fields[128 + 16 * z : 144 + 16 * z, LANES * k : LANES * k + LANES]
            r = jnp.sqrt(jnp.where(voids > 0.5, 0.01, 0.01 + 0.99 * d * d * d))
            q = b / r
            up[4 * z + k] = q
            down[4 * z + k] = q
            root[4 * z + k] = r
            if z >= 3:
                up[4 * (5 + z) + k] = r
            if z < 5:
                down[4 * (8 + z) + k] = r


def fine_pack_kernel(low, up, root, high, left, right):
    at = 0
    for ref in (low, up, high):
        for i in range(32):
            left[at : at + 8] = ref[i, 0:8]
            right[at : at + 8] = ref[i, 8:16]
            at += 8
    for ref, first, count in ((low, 36, 16), (root, 0, 32), (high, 32, 16)):
        for i in range(first, first + count):
            left[at : at + 5] = ref[i, 0:5]
            right[at : at + 5] = ref[i, 11:16]
            at += 5


def fine_pre_kernel(counts, low, up, root, high, left, right, q, y, r, mid_q, mid_r, early, late, *scratch):
    natural, w = scratch[0], scratch[1:5]
    gz, xy = lax.axis_index("gz"), lax.axis_index("xy")
    masks = row_masks(4, 16 * xy - 8, 16 * counts[1])
    z_scale = z_mask(8 * gz - 8, 8 * counts[0])

    for n, ref in enumerate((low, up, high)):
        for i in range(32):
            j = 32 * n + i
            natural[j, 0:8] = left[8 * j : 8 * j + 8]
            natural[j, 8:24] = ref[i]
            natural[j, 24:32] = right[8 * j : 8 * j + 8]

    def begin(z):
        for k in range(4):
            for x in range(4):
                value = weave(natural, z, k, 4, 4, x)
                q[z, 4 * k + x] = value
                w[0][z, 4 * k + x] = FIRST * value

    loop(0, 24, begin, 8)

    place = 0
    for ref, first, count in ((low, 32, 20), (root, 0, 32), (high, 32, 20)):
        for i in range(first, first + count):
            natural[place, 0:8] = jnp.zeros((8, LANES), F32)
            natural[place, 8:24] = ref[i]
            natural[place, 24:32] = jnp.zeros((8, LANES), F32)
            if 4 <= place < 68:
                j = 768 + 5 * (place - 4)
                natural[place, 3:8] = left[j : j + 5]
                natural[place, 24:29] = right[j : j + 5]
            place += 1

    def roots(z):
        for k in range(4):
            for x in range(4):
                r[z, 4 * k + x] = weave(natural, z, k, 4, 4, x)

    loop(0, 18, roots, 6)
    smooth(w, q, 0, 24, 4, masks, z_scale, DEGREE, width=8)

    def total(z):
        for i in range(16):
            y[z, i] = (w[0][z + 8, i] + w[1][z + 8, i]) + (w[2][z + 8, i] + w[3][z + 8, i])

    loop(0, 8, total)

    def fold(m):
        for k in range(2):
            for x in range(2):
                sums, roots = None, None
                for z in range(2):
                    for i in (8 * k + 2 * x, 8 * k + 2 * x + 1, 8 * k + 2 * x + 4, 8 * k + 2 * x + 5):
                        a = r[2 * m + 1 + z, i]
                        b = a * q[2 * m + 4 + z, i]
                        sums = b if sums is None else sums + b
                        roots = a if roots is None else roots + a
                roots = 0.125 * roots
                mid_r[2 * m + k, pl.ds(x, 8, 2), :] = roots
                mid_q[2 * m + k, pl.ds(x, 8, 2), :] = 0.5 * sums / jnp.maximum(roots, LEAST)

    loop(0, 8, fold)
    skip = jnp.where(gz % 4 == 3, 0, 2)
    for out, start in ((early, skip), (late, 2 - skip)):
        for i in range(16):
            out[12 * i : 12 * i + 12] = mid_q[i, 2:14]
        for i in range(12):
            out[192 + 12 * i : 204 + 12 * i] = mid_r[2 * start + i, 2:14]


def mid_pairs(count):
    first, second = [], []
    for i in range(count):
        up, down = (first, second) if i % 4 != 3 else (second, first)
        if i + 2 < count:
            up.append((i, i + 2))
        if i >= 2:
            down.append((i, i - 2))
    return first, second + [(0, 1), (count - 1, count - 2)]


def mid_sides(count, gz, first, second, low, high):
    @pl.when(gz % 4 != 1)
    def _():
        low[...] = first[...]
        high[...] = second[...]

    @pl.when(gz % 4 == 1)
    def _():
        low[...] = second[...]
        high[...] = first[...]

    @pl.when(gz == 1)
    def _():
        low[0:96] = jnp.zeros((96, LANES), F32)
        low[96:192] = second[0:96]
        low[192:240] = jnp.zeros((48, LANES), F32)
        low[240:336] = second[192:288]

    @pl.when(gz == count - 2)
    def _():
        high[0:96] = second[96:192]
        high[96:192] = jnp.zeros((96, LANES), F32)
        high[192:288] = second[240:336]
        high[288:336] = jnp.zeros((48, LANES), F32)


def mid_parts(low, high, mid_q, mid_r):
    def rows(field, z, k):
        if 8 <= z < 16:
            return (mid_q, mid_r)[field][2 * (z - 8) + k, 2:14]
        at = 12 * (2 * (z if z < 8 else z - 16) + k)
        if field == 1:
            at = at + (192 if z >= 16 else 144)
        return (low if z < 8 else high)[at : at + 12]

    return rows


def mid_pack_kernel(counts, first, second, mid_q, mid_r, low, high, left, right):
    mid_sides(counts[0], lax.axis_index("gz"), first, second, low, high)
    rows = mid_parts(low, high, mid_q, mid_r)
    at = 0
    for z in range(24):
        for k in range(2):
            value = rows(0, z, k)
            right[at : at + 8] = value[0:8]
            left[at : at + 8] = value[4:12]
            at += 8
    for z in range(2, 22):
        for k in range(2):
            value = rows(1, z, k)
            right[at : at + 6] = value[2:8]
            left[at : at + 6] = value[4:10]
            at += 6


def mid_pre_kernel(counts, *refs):
    rows, (left, right), refs = mid_parts(*refs[:4]), refs[4:6], refs[6:]
    q, y, r, coarse, coarse_low, coarse_high, coarse_root, natural = refs[:8]
    w = refs[8:]
    gz, xy = lax.axis_index("gz"), lax.axis_index("xy")
    masks = row_masks(4, 8 * xy - 10, 8 * counts[1])
    z_scale = z_mask(4 * gz - 10, 4 * counts[0])
    for z in range(24):
        for k in range(2):
            i = 2 * z + k
            natural[i, 0:8] = left[8 * i : 8 * i + 8]
            natural[i, 8:20] = rows(0, z, k)
            natural[i, 20:28] = right[8 * i : 8 * i + 8]
            natural[i, 28:32] = jnp.zeros((4, LANES), F32)

    def begin(z):
        for k in range(2):
            for x in range(4):
                value = weave(natural, z, k, 2, 4, x)
                q[z, 4 * k + x] = value
                w[0][z, 4 * k + x] = FIRST * value

    loop(0, 24, begin)
    for z in range(20):
        for k in range(2):
            i = 2 * z + k
            natural[i, 0:8] = jnp.zeros((8, LANES), F32)
            natural[i, 24:32] = jnp.zeros((8, LANES), F32)
            natural[i, 2:8] = left[384 + 6 * i : 390 + 6 * i]
            natural[i, 8:20] = rows(1, z + 2, k)
            natural[i, 20:26] = right[384 + 6 * i : 390 + 6 * i]

    def roots(z):
        for k in range(2):
            for x in range(4):
                r[z, 4 * k + x] = weave(natural, z, k, 2, 4, x)

    loop(0, 20, roots)
    smooth(w, q, 0, 24, 4, masks, z_scale, DEGREE)

    def total(z):
        for i in range(8):
            y[z, i] = (w[0][z + 7, i] + w[1][z + 7, i]) + (w[2][z + 7, i] + w[3][z + 7, i])

    loop(0, 10, total)

    for m in range(10):
        for x in range(2):
            sums, mean = None, None
            for z in range(2):
                for i in (2 * x, 2 * x + 1, 2 * x + 4, 2 * x + 5):
                    a = r[2 * m + z, i]
                    b = a * q[2 * m + 2 + z, i]
                    sums = b if sums is None else sums + b
                    mean = a if mean is None else mean + a
            mean = 0.125 * mean
            coarse_root[m, pl.ds(x, 8, 2), :] = mean
            if 0 < m < 9:
                coarse[m - 1, pl.ds(x, 8, 2), :] = 0.5 * sums / jnp.maximum(mean, LEAST)
    for m in range(4):
        coarse_low[m] = coarse[m]
        coarse_high[m] = coarse[4 + m]


def coarse_pack_kernel(*refs):
    parts, left, right = refs[:3], refs[3], refs[4]
    at = 0
    for ref in parts:
        for k in range(ref.shape[0]):
            right[at + k] = ref[k, 0:8]
            left[at + k] = ref[k, 8:16]
        at += ref.shape[0]


def finish_kernel(counts, *refs):
    parts, (left, right), refs = refs[:3], refs[3:5], refs[5:]
    coarse_root, mid_q, mid_y, mid_r, fine_q, fine_y, fine_r, out_x, out_r = refs[:9]
    natural, cq, error, spread, mq, mt, fq, ft, plain_x, plain_r, rows_x, rows_r = refs[9:21]
    cw, mw, fw = refs[21:25], refs[25:29], refs[29:33]
    gz, xy = lax.axis_index("gz"), lax.axis_index("xy")

    at = 0
    for ref in parts:
        for k in range(ref.shape[0]):
            natural[at, 0:4] = left[at, 2:6]
            natural[at, 4:14] = ref[k, 2:12]
            natural[at, 14:18] = right[at, 0:4]
            natural[at, 18:24] = jnp.zeros((6, LANES), F32)
            for x in range(3):
                value = weave(natural, at, 0, 1, 3, x)
                cq[at, x] = value
                cw[0][at, x] = FIRST * value
            at += 1
    masks = row_masks(3, 4 * xy - 7, 4 * counts[1])
    smooth(cw, cq, 0, 16, 3, masks, z_mask(2 * gz - 7, 2 * counts[0]), DEGREE - 1)
    for k in range(10):
        for x in range(3):
            total = (cw[0][k + 3, x] + cw[1][k + 3, x]) + (cw[2][k + 3, x] + cw[3][k + 3, x])
            natural[k, pl.ds(x, 8, 3), :] = total
        error[k] = natural[k, 2:18] / jnp.maximum(coarse_root[k], LEAST)

    for k in range(10):
        for x in range(4):
            value = error[k, pl.ds(x >> 1, 8, 2), :]
            for i in (x, 4 + x):
                mt[2 * k + 2, i] = mid_r[2 * k, i] * value
                mt[2 * k + 3, i] = mid_r[2 * k + 1, i] * value

    masks = row_masks(4, 8 * xy - 10, 8 * counts[1])
    z_scale = z_mask(4 * gz - 10, 4 * counts[0])

    def mid_correct(z):
        _, rest = applied(mt, z, 4, mid_q)
        scales = [z_scale(z, FIRST) * mask for mask in masks]
        for i, value in enumerate(rest):
            mq[z, i] = value
            mw[0][z, i] = scales[i % 4] * value

    loop(4, 20, mid_correct)
    smooth(mw, mq, 4, 20, 4, masks, z_scale, DEGREE - 1)

    def mid_error(z):
        for k in range(2):
            for x in range(4):
                i = 4 * k + x
                total = (mw[0][z, i] + mw[1][z, i]) + (mw[2][z, i] + mw[3][z, i])
                total = total + (mid_y[z - 7, i] + mt[z, i])
                spread[2 * (z - 7) + k, pl.ds(x, 8, 4), :] = total / jnp.maximum(mid_r[z - 2, i], LEAST)

    loop(7, 17, mid_error)

    def fine_prolong(k):
        for j in range(2):
            for x in range(4):
                value = spread[2 * k + j, pl.ds(6 + (x >> 1), 8, 2), :]
                for i in (8 * j + x, 8 * j + 4 + x):
                    ft[2 * k + 2, i] = fine_r[jnp.maximum(2 * k - 1, 0), i] * value
                    ft[2 * k + 3, i] = fine_r[jnp.minimum(2 * k, 17), i] * value

    loop(0, 10, fine_prolong, 1)
    masks = row_masks(4, 16 * xy - 8, 16 * counts[1])
    z_scale = z_mask(8 * gz - 8, 8 * counts[0])

    def fine_correct(z):
        _, rest = applied(ft, z, 4, fine_q)
        scales = [z_scale(z, FIRST) * mask for mask in masks]
        for i, value in enumerate(rest):
            fq[z, i] = value
            fw[0][z, i] = scales[i % 4] * value

    loop(4, 20, fine_correct)

    def finish(z, rest):
        for k in range(4):
            for x in range(4):
                i = 4 * k + x
                r = fine_r[z - 3, i]
                total = (fw[0][z, i] + fw[1][z, i]) + (fw[2][z, i] + fw[3][z, i])
                total = total + (fine_y[z - 8, i] + ft[z, i])
                plain_x[4 * (z - 8) + k, pl.ds(x, 8, 4), :] = total / r
                plain_r[4 * (z - 8) + k, pl.ds(x, 8, 4), :] = r * rest[i]

    smooth(fw, fq, 4, 20, 4, masks, z_scale, DEGREE, finish)
    matrix = weave_matrix(1)
    for plain, rows, out in ((plain_x, rows_x, out_x), (plain_r, rows_r, out_r)):
        for z in range(8):
            for k in range(4):
                rows[16 * z : 16 * z + 16, LANES * k : LANES * k + LANES] = plain[4 * z + k, 8:24]
        out[...] = exact_product(rows[...], matrix).reshape(8, 16, 512)


def call(kernel, operands, out_shapes, scratch=(), space=pltpu.VMEM):
    whole = pl.BlockSpec(memory_space=pltpu.VMEM)
    return pl.pallas_call(
        kernel,
        out_shape=[jax.ShapeDtypeStruct(s, F32) for s in out_shapes],
        in_specs=[pl.BlockSpec(memory_space=space)] * len(operands),
        out_specs=[whole] * len(out_shapes),
        scratch_shapes=[pltpu.VMEM(s, F32) if isinstance(s, tuple) else s for s in scratch],
        compiler_params=pltpu.CompilerParams(vmem_limit_bytes=30 * 1024 * 1024),
    )(*operands)


def send(block, axis, shift):
    count = lax.axis_size(axis)
    pairs = [(i, i + shift) for i in range(count) if 0 <= i + shift < count]
    return lax.ppermute(block, axis, pairs)


def with_counts(kernel):
    counts = (lax.axis_size("gz"), lax.axis_size("xy"))
    return lambda *refs: kernel(counts, *refs)


def on_device(load_field, density, void_mask):
    up, down, root = call(
        scale_kernel,
        [pltpu.with_memory_space_constraint(x, pltpu.HBM) for x in (load_field, density, void_mask)],
        [(52, 16, LANES), (52, 16, LANES), (32, 16, LANES)],
        [(16, 16, 512), pltpu.VMEM((1, 2, 64), jnp.int32), pltpu.SemaphoreType.DMA((3,))],
        pltpu.HBM,
    )
    low, high = send(up, "gz", 1), send(down, "gz", -1)
    to_left, to_right = call(fine_pack_kernel, (low, up, root, high), [(1088, LANES)] * 2)
    left, right = send(to_right, "xy", 1), send(to_left, "xy", -1)
    fine = (24, 16, 8, LANES)
    fine_q, fine_y, fine_r, mid_q, mid_r, first, second = call(
        with_counts(fine_pre_kernel),
        (low, up, root, high, left, right),
        [fine, (8, 16, 8, LANES), (18, 16, 8, LANES)] + [(16, 16, LANES)] * 2 + [(336, LANES)] * 2,
        [(96, 32, LANES)] + [fine] * 4,
    )
    pairs = mid_pairs(lax.axis_size("gz"))
    first, second = lax.ppermute(first, "gz", pairs[0]), lax.ppermute(second, "gz", pairs[1])
    low, high, to_left, to_right = call(
        with_counts(mid_pack_kernel), (first, second, mid_q, mid_r), [(336, LANES)] * 2 + [(624, LANES)] * 2
    )
    left, right = send(to_right, "xy", 1), send(to_left, "xy", -1)
    mid = (24, 8, 8, LANES)
    mid_q, mid_y, mid_r, coarse, coarse_low, coarse_high, coarse_root = call(
        with_counts(mid_pre_kernel),
        (low, high, mid_q, mid_r, left, right),
        [mid, (10, 8, 8, LANES), (20, 8, 8, LANES), (8, 16, LANES)] + [(4, 16, LANES)] * 2 + [(10, 16, LANES)],
        [(48, 32, LANES)] + [mid] * 4,
    )
    parts = (send(coarse_low, "gz", 2), coarse, send(coarse_high, "gz", -2))
    to_left, to_right = call(coarse_pack_kernel, parts, [(16, 8, LANES)] * 2)
    left, right = send(to_right, "xy", 1), send(to_left, "xy", -1)
    coarsest = (16, 3, 8, LANES)
    return tuple(
        call(
            with_counts(finish_kernel),
            parts + (left, right, coarse_root, mid_q, mid_y, mid_r, fine_q, fine_y, fine_r),
            [(8, 16, 512), (8, 16, 512)],
            [(16, 24, LANES), coarsest, (10, 16, LANES), (20, 32, LANES), mid, mid, fine, fine]
            + [(32, 32, LANES)] * 2
            + [(128, 512)] * 2
            + [coarsest] * 4
            + [mid] * 4
            + [fine] * 4,
        )
    )


def solution(mesh):
    specs = (P("gz", "xy", None), P("gz", "xy", None), P("gz", "xy", None))
    return jax.shard_map(
        on_device, mesh=mesh, in_specs=specs, out_specs=specs[:2], check_vma=False
    )
```

```python
import jax
import jax.numpy as jnp
from jax import lax
from jax.experimental import pallas as pl
from jax.experimental.pallas import tpu as pltpu
from jax.sharding import PartitionSpec as P


DEGREE = 4
THETA = 1.15
DELTA = 0.85
FIRST = 1.0 / (6.0 * THETA)
LEAST = 0.05
F32 = jnp.float32
LANES = 128


def coefficients():
    sigma = THETA / DELTA
    rho = 1.0 / sigma
    pairs = []
    for turn in range(DEGREE - 1):
        rho_next = 1.0 / (2.0 * sigma - rho)
        pairs.append((rho_next * rho, 2.0 * rho_next / (6.0 * DELTA)))
        rho = rho_next
    return pairs


COEFFICIENTS = coefficients()


def iota(shape, dim):
    return lax.broadcasted_iota(jnp.int32, shape, dim)


def inner(xy, count):
    return jnp.where(xy > 0, F32(1.0), F32(0.0)), jnp.where(xy < count - 1, F32(1.0), F32(0.0))


def row_masks(n, base, count):
    masks = []
    for x in range(n):
        place = n * iota((8, LANES), 0) + (x + base)
        masks.append(jnp.where((place >= 0) & (place < count), 1.0, 0.0).astype(F32))
    return masks


def z_mask(base, count):
    def scaled(z, value):
        place = z + base
        return jnp.where((place >= 0) & (place < count), F32(value), F32(0.0))

    return scaled


def loop(low, high, body, width=24):
    turns = (high - low) // width if high - low > width else 0

    def step(t, carry):
        for j in range(width):
            body(low + width * t + j)
        return carry

    if turns > 0:
        lax.fori_loop(0, turns, step, 0)
    for z in range(low + turns * width, high):
        body(z)


def around(ref, z, n):
    count = ref.shape[1]
    blocks = count // n
    here = [ref[z, i] for i in range(count)]
    lane = iota((8, LANES), 1)
    before = [jnp.where(lane == 0, 0.0, pltpu.roll(here[(blocks - 1) * n + x], 1, 1)) for x in range(n)]
    after = [jnp.where(lane == LANES - 1, 0.0, pltpu.roll(here[x], LANES - 1, 1)) for x in range(n)]
    total = []
    for k in range(blocks):
        row = here[k * n : k * n + n]
        up = pltpu.roll(row[n - 1], 1, 0)
        down = pltpu.roll(row[0], 7, 0)
        for x in range(n):
            i = k * n + x
            left = here[i - n] if k > 0 else before[x]
            right = here[i + n] if k + 1 < blocks else after[x]
            north = row[x - 1] if x > 0 else up
            south = row[x + 1] if x + 1 < n else down
            total.append(((left + right) + (north + south)) + (ref[z - 1, i] + ref[z + 1, i]))
    return here, total


def applied(ref, z, n, q):
    here, total = around(ref, z, n)
    return here, [q[z, i] - (6.0 * here[i] - total[i]) for i in range(len(here))]


def smooth(w, q, low, high, n, masks, z_scale, passes, finish=None, width=24):
    for turn in range(passes):

        def advance(z, turn=turn):
            here, rest = applied(w[turn], z, n, q)
            if finish is not None and turn == DEGREE - 1:
                finish(z, rest)
                return
            if turn < passes - 1 or passes == DEGREE:
                for i, value in enumerate(rest):
                    q[z, i] = value
            if turn < DEGREE - 1:
                c1, c2 = COEFFICIENTS[turn]
                scales = [z_scale(z, c2) * mask for mask in masks]
                for i, value in enumerate(rest):
                    w[turn + 1][z, i] = c1 * here[i] + scales[i % n] * value

        loop(low + 1 + turn, high - 1 - turn, advance, width)


def weave(source, z, k, blocks, n, x):
    return source[z * blocks + k, pl.ds(x, 8, n), :]


def exact_product(left, right):
    high = left.astype(jnp.bfloat16)
    rest = left - high.astype(F32)
    middle = rest.astype(jnp.bfloat16)
    low = (rest - middle.astype(F32)).astype(jnp.bfloat16)
    parts = [jnp.dot(part, right, preferred_element_type=F32) for part in (high, middle, low)]
    return (parts[2] + parts[1]) + parts[0]


def weave_matrix(dim):
    plain, woven = iota((512, 512), dim), iota((512, 512), 1 - dim)
    same = plain == 4 * (woven & (LANES - 1)) + (woven >> 7)
    return jnp.where(same, 1.0, 0.0).astype(jnp.bfloat16)


def scale_kernel(load_hbm, density_hbm, void_hbm, up, down, root, both, void, sems):
    copies = [
        pltpu.make_async_copy(load_hbm, both.at[pl.ds(0, 8)], sems.at[0]),
        pltpu.make_async_copy(density_hbm, both.at[pl.ds(8, 8)], sems.at[1]),
        pltpu.make_async_copy(void_hbm, void, sems.at[2]),
    ]
    for copy in copies:
        copy.start()
    matrix = weave_matrix(0)
    copies[2].wait()
    bricks = jnp.where(void[0] == 1, 1.0, 0.0).astype(F32)
    bricks = jnp.concatenate([jnp.broadcast_to(bricks[k : k + 1], (8, 64)) for k in range(2)], axis=0)
    spread = jnp.where((iota((64, LANES), 1) >> 1) == iota((64, LANES), 0), 1.0, 0.0).astype(jnp.bfloat16)
    voids = jnp.dot(bricks.astype(jnp.bfloat16), spread, preferred_element_type=F32)
    copies[0].wait()
    copies[1].wait()
    fields = exact_product(both[...].reshape(256, 512), matrix)
    for z in range(8):
        for k in range(4):
            b = fields[16 * z : 16 * z + 16, LANES * k : LANES * k + LANES]
            d = fields[128 + 16 * z : 144 + 16 * z, LANES * k : LANES * k + LANES]
            r = jnp.sqrt(jnp.where(voids > 0.5, 0.01, 0.01 + 0.99 * d * d * d))
            q = b / r
            up[4 * z + k] = q
            down[4 * z + k] = q
            root[4 * z + k] = r
            if z >= 3:
                up[4 * (5 + z) + k] = r
            if z < 5:
                down[4 * (8 + z) + k] = r


def fine_pack_kernel(low, up, root, high, left, right):
    at = 0
    for ref in (low, up, high):
        for i in range(32):
            left[at : at + 8] = ref[i, 0:8]
            right[at : at + 8] = ref[i, 8:16]
            at += 8
    for ref, first, count in ((low, 36, 16), (root, 0, 32), (high, 32, 16)):
        for i in range(first, first + count):
            left[at : at + 5] = ref[i, 0:5]
            right[at : at + 5] = ref[i, 11:16]
            at += 5


def fine_pre_kernel(counts, low, up, root, high, left, right, q, y, r, mid_q, mid_r, early, late, *scratch):
    natural, w = scratch[0], scratch[1:5]
    gz, xy = lax.axis_index("gz"), lax.axis_index("xy")
    on_left, on_right = inner(xy, counts[1])
    masks = row_masks(4, 16 * xy - 8, 16 * counts[1])
    z_scale = z_mask(8 * gz - 8, 8 * counts[0])

    for n, ref in enumerate((low, up, high)):
        for i in range(32):
            j = 32 * n + i
            natural[j, 0:8] = on_left * left[8 * j : 8 * j + 8]
            natural[j, 8:24] = ref[i]
            natural[j, 24:32] = on_right * right[8 * j : 8 * j + 8]

    def begin(z):
        for k in range(4):
            for x in range(4):
                value = weave(natural, z, k, 4, 4, x)
                q[z, 4 * k + x] = value
                w[0][z, 4 * k + x] = FIRST * value

    loop(0, 24, begin, 8)

    place = 0
    for ref, first, count in ((low, 32, 20), (root, 0, 32), (high, 32, 20)):
        for i in range(first, first + count):
            natural[place, 0:8] = jnp.zeros((8, LANES), F32)
            natural[place, 8:24] = ref[i]
            natural[place, 24:32] = jnp.zeros((8, LANES), F32)
            if 4 <= place < 68:
                j = 768 + 5 * (place - 4)
                natural[place, 3:8] = on_left * left[j : j + 5]
                natural[place, 24:29] = on_right * right[j : j + 5]
            place += 1

    def roots(z):
        for k in range(4):
            for x in range(4):
                r[z, 4 * k + x] = weave(natural, z, k, 4, 4, x)

    loop(0, 18, roots, 6)
    smooth(w, q, 0, 24, 4, masks, z_scale, DEGREE, width=8)

    def total(z):
        for i in range(16):
            y[z, i] = (w[0][z + 8, i] + w[1][z + 8, i]) + (w[2][z + 8, i] + w[3][z + 8, i])

    loop(0, 8, total)

    def fold(m):
        for k in range(2):
            for x in range(2):
                sums, roots = None, None
                for z in range(2):
                    for i in (8 * k + 2 * x, 8 * k + 2 * x + 1, 8 * k + 2 * x + 4, 8 * k + 2 * x + 5):
                        a = r[2 * m + 1 + z, i]
                        b = a * q[2 * m + 4 + z, i]
                        sums = b if sums is None else sums + b
                        roots = a if roots is None else roots + a
                roots = 0.125 * roots
                mid_r[2 * m + k, pl.ds(x, 8, 2), :] = roots
                mid_q[2 * m + k, pl.ds(x, 8, 2), :] = 0.5 * sums / jnp.maximum(roots, LEAST)

    loop(0, 8, fold)
    skip = jnp.where(gz % 4 == 3, 0, 2)
    for out, start in ((early, skip), (late, 2 - skip)):
        for i in range(16):
            out[12 * i : 12 * i + 12] = mid_q[i, 2:14]
        for i in range(12):
            out[192 + 12 * i : 204 + 12 * i] = mid_r[2 * start + i, 2:14]


def mid_pairs(count):
    first, second = [], []
    for i in range(count):
        up, down = (first, second) if i % 4 != 3 else (second, first)
        if i + 2 < count:
            up.append((i, i + 2))
        if i >= 2:
            down.append((i, i - 2))
    return first, second + [(0, 1), (count - 1, count - 2)]


def mid_sides(count, gz, first, second, low, high):
    @pl.when(gz % 4 != 1)
    def _():
        low[...] = first[...]
        high[...] = second[...]

    @pl.when(gz % 4 == 1)
    def _():
        low[...] = second[...]
        high[...] = first[...]

    @pl.when(gz == 1)
    def _():
        low[0:96] = jnp.zeros((96, LANES), F32)
        low[96:192] = second[0:96]
        low[192:240] = jnp.zeros((48, LANES), F32)
        low[240:336] = second[192:288]

    @pl.when(gz == count - 2)
    def _():
        high[0:96] = second[96:192]
        high[96:192] = jnp.zeros((96, LANES), F32)
        high[192:288] = second[240:336]
        high[288:336] = jnp.zeros((48, LANES), F32)


def mid_parts(low, high, mid_q, mid_r):
    def rows(field, z, k):
        if 8 <= z < 16:
            return (mid_q, mid_r)[field][2 * (z - 8) + k, 2:14]
        at = 12 * (2 * (z if z < 8 else z - 16) + k)
        if field == 1:
            at = at + (192 if z >= 16 else 144)
        return (low if z < 8 else high)[at : at + 12]

    return rows


def mid_pack_kernel(counts, first, second, mid_q, mid_r, low, high, left, right):
    mid_sides(counts[0], lax.axis_index("gz"), first, second, low, high)
    rows = mid_parts(low, high, mid_q, mid_r)
    at = 0
    for z in range(24):
        for k in range(2):
            value = rows(0, z, k)
            right[at : at + 8] = value[0:8]
            left[at : at + 8] = value[4:12]
            at += 8
    for z in range(2, 22):
        for k in range(2):
            value = rows(1, z, k)
            right[at : at + 6] = value[2:8]
            left[at : at + 6] = value[4:10]
            at += 6


def mid_pre_kernel(counts, *refs):
    rows, (left, right), refs = mid_parts(*refs[:4]), refs[4:6], refs[6:]
    q, y, r, coarse, coarse_low, coarse_high, coarse_root, natural = refs[:8]
    w = refs[8:]
    gz, xy = lax.axis_index("gz"), lax.axis_index("xy")
    on_left, on_right = inner(xy, counts[1])
    masks = row_masks(4, 8 * xy - 10, 8 * counts[1])
    z_scale = z_mask(4 * gz - 10, 4 * counts[0])
    for z in range(24):
        for k in range(2):
            i = 2 * z + k
            natural[i, 0:8] = on_left * left[8 * i : 8 * i + 8]
            natural[i, 8:20] = rows(0, z, k)
            natural[i, 20:28] = on_right * right[8 * i : 8 * i + 8]
            natural[i, 28:32] = jnp.zeros((4, LANES), F32)

    def begin(z):
        for k in range(2):
            for x in range(4):
                value = weave(natural, z, k, 2, 4, x)
                q[z, 4 * k + x] = value
                w[0][z, 4 * k + x] = FIRST * value

    loop(0, 24, begin)
    for z in range(20):
        for k in range(2):
            i = 2 * z + k
            natural[i, 0:8] = jnp.zeros((8, LANES), F32)
            natural[i, 24:32] = jnp.zeros((8, LANES), F32)
            natural[i, 2:8] = on_left * left[384 + 6 * i : 390 + 6 * i]
            natural[i, 8:20] = rows(1, z + 2, k)
            natural[i, 20:26] = on_right * right[384 + 6 * i : 390 + 6 * i]

    def roots(z):
        for k in range(2):
            for x in range(4):
                r[z, 4 * k + x] = weave(natural, z, k, 2, 4, x)

    loop(0, 20, roots)
    smooth(w, q, 0, 24, 4, masks, z_scale, DEGREE)

    def total(z):
        for i in range(8):
            y[z, i] = (w[0][z + 7, i] + w[1][z + 7, i]) + (w[2][z + 7, i] + w[3][z + 7, i])

    loop(0, 10, total)

    for m in range(10):
        for x in range(2):
            sums, mean = None, None
            for z in range(2):
                for i in (2 * x, 2 * x + 1, 2 * x + 4, 2 * x + 5):
                    a = r[2 * m + z, i]
                    b = a * q[2 * m + 2 + z, i]
                    sums = b if sums is None else sums + b
                    mean = a if mean is None else mean + a
            mean = 0.125 * mean
            coarse_root[m, pl.ds(x, 8, 2), :] = mean
            if 0 < m < 9:
                coarse[m - 1, pl.ds(x, 8, 2), :] = 0.5 * sums / jnp.maximum(mean, LEAST)
    for m in range(4):
        coarse_low[m] = coarse[m]
        coarse_high[m] = coarse[4 + m]


def coarse_pack_kernel(*refs):
    parts, left, right = refs[:3], refs[3], refs[4]
    at = 0
    for ref in parts:
        for k in range(ref.shape[0]):
            right[at + k] = ref[k, 0:8]
            left[at + k] = ref[k, 8:16]
        at += ref.shape[0]


def finish_kernel(counts, *refs):
    parts, (left, right), refs = refs[:3], refs[3:5], refs[5:]
    coarse_root, mid_q, mid_y, mid_r, fine_q, fine_y, fine_r, out_x, out_r = refs[:9]
    natural, cq, error, spread, mq, mt, fq, ft, plain_x, plain_r, rows_x, rows_r = refs[9:21]
    cw, mw, fw = refs[21:25], refs[25:29], refs[29:33]
    gz, xy = lax.axis_index("gz"), lax.axis_index("xy")

    on_left, on_right = inner(xy, counts[1])

    at = 0
    for ref in parts:
        for k in range(ref.shape[0]):
            natural[at, 0:4] = on_left * left[at, 2:6]
            natural[at, 4:14] = ref[k, 2:12]
            natural[at, 14:18] = on_right * right[at, 0:4]
            natural[at, 18:24] = jnp.zeros((6, LANES), F32)
            for x in range(3):
                value = weave(natural, at, 0, 1, 3, x)
                cq[at, x] = value
                cw[0][at, x] = FIRST * value
            at += 1
    masks = row_masks(3, 4 * xy - 7, 4 * counts[1])
    smooth(cw, cq, 0, 16, 3, masks, z_mask(2 * gz - 7, 2 * counts[0]), DEGREE - 1)
    for k in range(10):
        for x in range(3):
            total = (cw[0][k + 3, x] + cw[1][k + 3, x]) + (cw[2][k + 3, x] + cw[3][k + 3, x])
            natural[k, pl.ds(x, 8, 3), :] = total
        error[k] = natural[k, 2:18] / jnp.maximum(coarse_root[k], LEAST)

    for k in range(10):
        for x in range(4):
            value = error[k, pl.ds(x >> 1, 8, 2), :]
            for i in (x, 4 + x):
                mt[2 * k + 2, i] = mid_r[2 * k, i] * value
                mt[2 * k + 3, i] = mid_r[2 * k + 1, i] * value

    masks = row_masks(4, 8 * xy - 10, 8 * counts[1])
    z_scale = z_mask(4 * gz - 10, 4 * counts[0])

    def mid_correct(z):
        _, rest = applied(mt, z, 4, mid_q)
        scales = [z_scale(z, FIRST) * mask for mask in masks]
        for i, value in enumerate(rest):
            mq[z, i] = value
            mw[0][z, i] = scales[i % 4] * value

    loop(4, 20, mid_correct)
    smooth(mw, mq, 4, 20, 4, masks, z_scale, DEGREE - 1)

    def mid_error(z):
        for k in range(2):
            for x in range(4):
                i = 4 * k + x
                total = (mw[0][z, i] + mw[1][z, i]) + (mw[2][z, i] + mw[3][z, i])
                total = total + (mid_y[z - 7, i] + mt[z, i])
                spread[2 * (z - 7) + k, pl.ds(x, 8, 4), :] = total / jnp.maximum(mid_r[z - 2, i], LEAST)

    loop(7, 17, mid_error)

    def fine_prolong(k):
        for j in range(2):
            for x in range(4):
                value = spread[2 * k + j, pl.ds(6 + (x >> 1), 8, 2), :]
                for i in (8 * j + x, 8 * j + 4 + x):
                    ft[2 * k + 2, i] = fine_r[jnp.maximum(2 * k - 1, 0), i] * value
                    ft[2 * k + 3, i] = fine_r[jnp.minimum(2 * k, 17), i] * value

    loop(0, 10, fine_prolong, 1)
    masks = row_masks(4, 16 * xy - 8, 16 * counts[1])
    z_scale = z_mask(8 * gz - 8, 8 * counts[0])

    def fine_correct(z):
        _, rest = applied(ft, z, 4, fine_q)
        scales = [z_scale(z, FIRST) * mask for mask in masks]
        for i, value in enumerate(rest):
            fq[z, i] = value
            fw[0][z, i] = scales[i % 4] * value

    loop(4, 20, fine_correct)

    def finish(z, rest):
        for k in range(4):
            for x in range(4):
                i = 4 * k + x
                r = fine_r[z - 3, i]
                total = (fw[0][z, i] + fw[1][z, i]) + (fw[2][z, i] + fw[3][z, i])
                total = total + (fine_y[z - 8, i] + ft[z, i])
                plain_x[4 * (z - 8) + k, pl.ds(x, 8, 4), :] = total / r
                plain_r[4 * (z - 8) + k, pl.ds(x, 8, 4), :] = r * rest[i]

    smooth(fw, fq, 4, 20, 4, masks, z_scale, DEGREE, finish)
    matrix = weave_matrix(1)
    for plain, rows, out in ((plain_x, rows_x, out_x), (plain_r, rows_r, out_r)):
        for z in range(8):
            for k in range(4):
                rows[16 * z : 16 * z + 16, LANES * k : LANES * k + LANES] = plain[4 * z + k, 8:24]
        out[...] = exact_product(rows[...], matrix).reshape(8, 16, 512)


def call(kernel, operands, out_shapes, scratch=(), space=pltpu.VMEM):
    whole = pl.BlockSpec(memory_space=pltpu.VMEM)
    return pl.pallas_call(
        kernel,
        out_shape=[jax.ShapeDtypeStruct(s, F32) for s in out_shapes],
        in_specs=[pl.BlockSpec(memory_space=space)] * len(operands),
        out_specs=[whole] * len(out_shapes),
        scratch_shapes=[pltpu.VMEM(s, F32) if isinstance(s, tuple) else s for s in scratch],
        compiler_params=pltpu.CompilerParams(vmem_limit_bytes=30 * 1024 * 1024),
    )(*operands)


def send(block, axis, shift):
    count = lax.axis_size(axis)
    pairs = [(i, i + shift) for i in range(count) if 0 <= i + shift < count]
    return lax.ppermute(block, axis, pairs)


def turn(to_left, to_right):
    count = lax.axis_size("xy")
    left = lax.ppermute(to_right, "xy", [(i, (i + 1) % count) for i in range(count)])
    right = lax.ppermute(to_left, "xy", [(i, (i - 1) % count) for i in range(count)])
    return left, right


def with_counts(kernel):
    counts = (lax.axis_size("gz"), lax.axis_size("xy"))
    return lambda *refs: kernel(counts, *refs)


def on_device(load_field, density, void_mask):
    up, down, root = call(
        scale_kernel,
        [pltpu.with_memory_space_constraint(x, pltpu.HBM) for x in (load_field, density, void_mask)],
        [(52, 16, LANES), (52, 16, LANES), (32, 16, LANES)],
        [(16, 16, 512), pltpu.VMEM((1, 2, 64), jnp.int32), pltpu.SemaphoreType.DMA((3,))],
        pltpu.HBM,
    )
    low, high = send(up, "gz", 1), send(down, "gz", -1)
    to_left, to_right = call(fine_pack_kernel, (low, up, root, high), [(1088, LANES)] * 2)
    left, right = turn(to_left, to_right)
    fine = (24, 16, 8, LANES)
    fine_q, fine_y, fine_r, mid_q, mid_r, first, second = call(
        with_counts(fine_pre_kernel),
        (low, up, root, high, left, right),
        [fine, (8, 16, 8, LANES), (18, 16, 8, LANES)] + [(16, 16, LANES)] * 2 + [(336, LANES)] * 2,
        [(96, 32, LANES)] + [fine] * 4,
    )
    pairs = mid_pairs(lax.axis_size("gz"))
    first, second = lax.ppermute(first, "gz", pairs[0]), lax.ppermute(second, "gz", pairs[1])
    low, high, to_left, to_right = call(
        with_counts(mid_pack_kernel), (first, second, mid_q, mid_r), [(336, LANES)] * 2 + [(624, LANES)] * 2
    )
    left, right = turn(to_left, to_right)
    mid = (24, 8, 8, LANES)
    mid_q, mid_y, mid_r, coarse, coarse_low, coarse_high, coarse_root = call(
        with_counts(mid_pre_kernel),
        (low, high, mid_q, mid_r, left, right),
        [mid, (10, 8, 8, LANES), (20, 8, 8, LANES), (8, 16, LANES)] + [(4, 16, LANES)] * 2 + [(10, 16, LANES)],
        [(48, 32, LANES)] + [mid] * 4,
    )
    parts = (send(coarse_low, "gz", 2), coarse, send(coarse_high, "gz", -2))
    to_left, to_right = call(coarse_pack_kernel, parts, [(16, 8, LANES)] * 2)
    left, right = turn(to_left, to_right)
    coarsest = (16, 3, 8, LANES)
    return tuple(
        call(
            with_counts(finish_kernel),
            parts + (left, right, coarse_root, mid_q, mid_y, mid_r, fine_q, fine_y, fine_r),
            [(8, 16, 512), (8, 16, 512)],
            [(16, 24, LANES), coarsest, (10, 16, LANES), (20, 32, LANES), mid, mid, fine, fine]
            + [(32, 32, LANES)] * 2
            + [(128, 512)] * 2
            + [coarsest] * 4
            + [mid] * 4
            + [fine] * 4,
        )
    )


def solution(mesh):
    specs = (P("gz", "xy", None), P("gz", "xy", None), P("gz", "xy", None))
    return jax.shard_map(
        on_device, mesh=mesh, in_specs=specs, out_specs=specs[:2], check_vma=False
    )
```

```python
import jax
import jax.numpy as jnp
from jax import lax
from jax.experimental import pallas as pl
from jax.experimental.pallas import tpu as pltpu
from jax.sharding import PartitionSpec as P


DEGREE = 4
THETA = 1.15
DELTA = 0.85
FIRST = 1.0 / (6.0 * THETA)
LEAST = 0.05
F32 = jnp.float32
LANES = 128


def coefficients():
    sigma = THETA / DELTA
    rho = 1.0 / sigma
    pairs = []
    for turn in range(DEGREE - 1):
        rho_next = 1.0 / (2.0 * sigma - rho)
        pairs.append((rho_next * rho, 2.0 * rho_next / (6.0 * DELTA)))
        rho = rho_next
    return pairs


COEFFICIENTS = coefficients()


def iota(shape, dim):
    return lax.broadcasted_iota(jnp.int32, shape, dim)


def inner(xy, count):
    return jnp.where(xy > 0, F32(1.0), F32(0.0)), jnp.where(xy < count - 1, F32(1.0), F32(0.0))


def row_masks(n, base, count):
    masks = []
    for x in range(n):
        place = n * iota((8, LANES), 0) + (x + base)
        masks.append(jnp.where((place >= 0) & (place < count), 1.0, 0.0).astype(F32))
    return masks


def z_mask(base, count):
    def scaled(z, value):
        place = z + base
        return jnp.where((place >= 0) & (place < count), F32(value), F32(0.0))

    return scaled


def loop(low, high, body, width=24):
    turns = (high - low) // width if high - low > width else 0

    def step(t, carry):
        for j in range(width):
            body(low + width * t + j)
        return carry

    if turns > 0:
        lax.fori_loop(0, turns, step, 0)
    for z in range(low + turns * width, high):
        body(z)


def around(ref, z, n):
    count = ref.shape[1]
    blocks = count // n
    here = [ref[z, i] for i in range(count)]
    lane = iota((8, LANES), 1)
    before = [jnp.where(lane == 0, 0.0, pltpu.roll(here[(blocks - 1) * n + x], 1, 1)) for x in range(n)]
    after = [jnp.where(lane == LANES - 1, 0.0, pltpu.roll(here[x], LANES - 1, 1)) for x in range(n)]
    total = []
    for k in range(blocks):
        row = here[k * n : k * n + n]
        up = pltpu.roll(row[n - 1], 1, 0)
        down = pltpu.roll(row[0], 7, 0)
        for x in range(n):
            i = k * n + x
            left = here[i - n] if k > 0 else before[x]
            right = here[i + n] if k + 1 < blocks else after[x]
            north = row[x - 1] if x > 0 else up
            south = row[x + 1] if x + 1 < n else down
            total.append(((left + right) + (north + south)) + (ref[z - 1, i] + ref[z + 1, i]))
    return here, total


def applied(ref, z, n, q):
    here, total = around(ref, z, n)
    return here, [q[z, i] - (6.0 * here[i] - total[i]) for i in range(len(here))]


def smooth(w, q, low, high, n, masks, z_scale, passes, finish=None, width=24):
    for turn in range(passes):

        def advance(z, turn=turn):
            here, rest = applied(w[turn], z, n, q)
            if finish is not None and turn == DEGREE - 1:
                finish(z, rest)
                return
            if turn < passes - 1 or passes == DEGREE:
                for i, value in enumerate(rest):
                    q[z, i] = value
            if turn < DEGREE - 1:
                c1, c2 = COEFFICIENTS[turn]
                scales = [z_scale(z, c2) * mask for mask in masks]
                for i, value in enumerate(rest):
                    w[turn + 1][z, i] = c1 * here[i] + scales[i % n] * value

        loop(low + 1 + turn, high - 1 - turn, advance, width)


def weave(source, z, k, blocks, n, x):
    return source[z * blocks + k, pl.ds(x, 8, n), :]


def exact_product(left, right):
    high = left.astype(jnp.bfloat16)
    rest = left - high.astype(F32)
    middle = rest.astype(jnp.bfloat16)
    low = (rest - middle.astype(F32)).astype(jnp.bfloat16)
    parts = [jnp.dot(part, right, preferred_element_type=F32) for part in (high, middle, low)]
    return (parts[2] + parts[1]) + parts[0]


def weave_matrix(dim):
    plain, woven = iota((512, 512), dim), iota((512, 512), 1 - dim)
    same = plain == 4 * (woven & (LANES - 1)) + (woven >> 7)
    return jnp.where(same, 1.0, 0.0).astype(jnp.bfloat16)


CORNER = [8, 8, 8, 8, 7, 6, 5, 4]


def corner_plan(blocks, first, last, rows):
    plan, at = [], 0
    for side in range(2):
        for layer in range(8):
            away = 8 - layer if side == 0 else layer + 1
            if not first <= away <= last:
                continue
            for k in range(blocks):
                count = rows if rows else CORNER[away - 1]
                plan.append((side, layer, k, count, at))
                at += count
    return plan, at


FINE_Q, FINE_Q_ROWS = corner_plan(4, 1, 8, 0)
FINE_R, FINE_R_ROWS = corner_plan(4, 1, 4, 4)
MID_Q, MID_Q_ROWS = corner_plan(2, 1, 8, 0)
MID_R, MID_R_ROWS = corner_plan(2, 1, 6, 6)


def scale_kernel(load_hbm, density_hbm, void_hbm, up, down, root, left, right, both, void, sems):
    copies = [
        pltpu.make_async_copy(load_hbm, both.at[pl.ds(0, 8)], sems.at[0]),
        pltpu.make_async_copy(density_hbm, both.at[pl.ds(8, 8)], sems.at[1]),
        pltpu.make_async_copy(void_hbm, void, sems.at[2]),
    ]
    for copy in copies:
        copy.start()
    matrix = weave_matrix(0)
    copies[2].wait()
    bricks = jnp.where(void[0] == 1, 1.0, 0.0).astype(F32)
    bricks = jnp.concatenate([jnp.broadcast_to(bricks[k : k + 1], (8, 64)) for k in range(2)], axis=0)
    spread = jnp.where((iota((64, LANES), 1) >> 1) == iota((64, LANES), 0), 1.0, 0.0).astype(jnp.bfloat16)
    voids = jnp.dot(bricks.astype(jnp.bfloat16), spread, preferred_element_type=F32)
    copies[0].wait()
    copies[1].wait()
    fields = exact_product(both[...].reshape(256, 512), matrix)
    for z in range(8):
        for k in range(4):
            b = fields[16 * z : 16 * z + 16, LANES * k : LANES * k + LANES]
            d = fields[128 + 16 * z : 144 + 16 * z, LANES * k : LANES * k + LANES]
            r = jnp.sqrt(jnp.where(voids > 0.5, 0.01, 0.01 + 0.99 * d * d * d))
            q = b / r
            up[4 * z + k] = q
            down[4 * z + k] = q
            root[4 * z + k] = r
            i = 4 * z + k
            left[8 * i : 8 * i + 8] = q[0:8]
            right[8 * i : 8 * i + 8] = q[8:16]
            left[256 + 5 * i : 261 + 5 * i] = r[0:5]
            right[256 + 5 * i : 261 + 5 * i] = r[11:16]
            if z >= 3:
                up[4 * (5 + z) + k] = r
            if z < 5:
                down[4 * (8 + z) + k] = r


def fine_pack_kernel(low, high, left, right):
    for side, layer, k, n, at in FINE_Q:
        ref, i = (low, high)[side], 4 * layer + k
        left[at : at + n] = ref[i, 0:n]
        right[at : at + n] = ref[i, 16 - n : 16]
    for side, layer, k, n, at in FINE_R:
        ref, i = (low, high)[side], 32 + 4 * (layer - 3 if side == 0 else layer) + k
        at += FINE_Q_ROWS
        left[at : at + n] = ref[i, 0:n]
        right[at : at + n] = ref[i, 16 - n : 16]


def fine_pre_kernel(
    counts, low, up, root, high, left, right, far_left, far_right, q, y, r, mid_q, mid_r, early, late, mid_left, mid_right, *scratch
):
    natural, w = scratch[0], scratch[1:5]
    gz, xy = lax.axis_index("gz"), lax.axis_index("xy")
    on_left, on_right = inner(xy, counts[1])
    masks = row_masks(4, 16 * xy - 8, 16 * counts[1])
    z_scale = z_mask(8 * gz - 8, 8 * counts[0])

    blank = jnp.zeros((8, LANES), F32)
    for n, ref in enumerate((low, up, high)):
        for i in range(32):
            natural[32 * n + i, 8:24] = ref[i]
    for i in range(32):
        natural[32 + i, 0:8] = on_left * left[8 * i : 8 * i + 8]
        natural[32 + i, 24:32] = on_right * right[8 * i : 8 * i + 8]
    for side, layer, k, n, at in FINE_Q:
        j = 64 * side + 4 * layer + k
        if n < 8:
            natural[j, 0:8] = blank
            natural[j, 24:32] = blank
        natural[j, 8 - n : 8] = on_left * far_left[at : at + n]
        natural[j, 24 : 24 + n] = on_right * far_right[at : at + n]

    def begin(z):
        for k in range(4):
            for x in range(4):
                value = weave(natural, z, k, 4, 4, x)
                q[z, 4 * k + x] = value
                w[0][z, 4 * k + x] = FIRST * value

    loop(0, 24, begin, 8)

    place = 0
    for ref, first, count in ((low, 32, 20), (root, 0, 32), (high, 32, 20)):
        for i in range(first, first + count):
            natural[place, 0:8] = blank
            natural[place, 8:24] = ref[i]
            natural[place, 24:32] = blank
            place += 1
    for i in range(32):
        natural[20 + i, 3:8] = on_left * left[256 + 5 * i : 261 + 5 * i]
        natural[20 + i, 24:29] = on_right * right[256 + 5 * i : 261 + 5 * i]
    for side, layer, k, n, at in FINE_R:
        j = 4 * (layer - 3 if side == 0 else 13 + layer) + k
        at += FINE_Q_ROWS
        natural[j, 8 - n : 8] = on_left * far_left[at : at + n]
        natural[j, 24 : 24 + n] = on_right * far_right[at : at + n]

    def roots(z):
        for k in range(4):
            for x in range(4):
                r[z, 4 * k + x] = weave(natural, z, k, 4, 4, x)

    loop(0, 18, roots, 6)
    smooth(w, q, 0, 24, 4, masks, z_scale, DEGREE, width=8)

    def total(z):
        for i in range(16):
            y[z, i] = (w[0][z + 8, i] + w[1][z + 8, i]) + (w[2][z + 8, i] + w[3][z + 8, i])

    loop(0, 8, total)

    def fold(m):
        for k in range(2):
            for x in range(2):
                sums, roots = None, None
                for z in range(2):
                    for i in (8 * k + 2 * x, 8 * k + 2 * x + 1, 8 * k + 2 * x + 4, 8 * k + 2 * x + 5):
                        a = r[2 * m + 1 + z, i]
                        b = a * q[2 * m + 4 + z, i]
                        sums = b if sums is None else sums + b
                        roots = a if roots is None else roots + a
                roots = 0.125 * roots
                mid_r[2 * m + k, pl.ds(x, 8, 2), :] = roots
                mid_q[2 * m + k, pl.ds(x, 8, 2), :] = 0.5 * sums / jnp.maximum(roots, LEAST)

    loop(0, 8, fold)
    skip = jnp.where(gz % 4 == 3, 0, 2)
    for out, start in ((early, skip), (late, 2 - skip)):
        for i in range(16):
            out[12 * i : 12 * i + 12] = mid_q[i, 2:14]
        for i in range(12):
            out[192 + 12 * i : 204 + 12 * i] = mid_r[2 * start + i, 2:14]
    for i in range(16):
        mid_right[8 * i : 8 * i + 8] = mid_q[i, 2:10]
        mid_left[8 * i : 8 * i + 8] = mid_q[i, 6:14]
        mid_right[128 + 6 * i : 134 + 6 * i] = mid_r[i, 4:10]
        mid_left[128 + 6 * i : 134 + 6 * i] = mid_r[i, 6:12]


def mid_pairs(count):
    first, second = [], []
    for i in range(count):
        up, down = (first, second) if i % 4 != 3 else (second, first)
        if i + 2 < count:
            up.append((i, i + 2))
        if i >= 2:
            down.append((i, i - 2))
    return first, second + [(0, 1), (count - 1, count - 2)]


def mid_sides(count, gz, first, second, low, high):
    @pl.when(gz % 4 != 1)
    def _():
        low[...] = first[...]
        high[...] = second[...]

    @pl.when(gz % 4 == 1)
    def _():
        low[...] = second[...]
        high[...] = first[...]

    @pl.when(gz == 1)
    def _():
        low[0:96] = jnp.zeros((96, LANES), F32)
        low[96:192] = second[0:96]
        low[192:240] = jnp.zeros((48, LANES), F32)
        low[240:336] = second[192:288]

    @pl.when(gz == count - 2)
    def _():
        high[0:96] = second[96:192]
        high[96:192] = jnp.zeros((96, LANES), F32)
        high[192:288] = second[240:336]
        high[288:336] = jnp.zeros((48, LANES), F32)


def mid_rows(low, high, field, side, layer, k, start, stop):
    at = 12 * (2 * layer + k) + (0 if field == 0 else 144 if side == 0 else 192)
    return (low, high)[side][at + start : at + stop]


def mid_pack_kernel(counts, first, second, low, high, left, right):
    mid_sides(counts[0], lax.axis_index("gz"), first, second, low, high)
    for field, plan, base in ((0, MID_Q, 0), (1, MID_R, MID_Q_ROWS)):
        for side, layer, k, n, at in plan:
            at += base
            right[at : at + n] = mid_rows(low, high, field, side, layer, k, 8 - n, 8)
            left[at : at + n] = mid_rows(low, high, field, side, layer, k, 4, 4 + n)


def mid_pre_kernel(counts, *refs):
    (low, high, own_q, own_r, left, right, far_left, far_right), refs = refs[:8], refs[8:]
    q, y, r, coarse, coarse_low, coarse_high, coarse_root, natural = refs[:8]
    w = refs[8:]
    gz, xy = lax.axis_index("gz"), lax.axis_index("xy")
    on_left, on_right = inner(xy, counts[1])
    masks = row_masks(4, 8 * xy - 10, 8 * counts[1])
    z_scale = z_mask(4 * gz - 10, 4 * counts[0])
    blank = jnp.zeros((8, LANES), F32)
    for i in range(16):
        natural[16 + i, 0:8] = on_left * left[8 * i : 8 * i + 8]
        natural[16 + i, 24:32] = blank
        natural[16 + i, 8:20] = own_q[i, 2:14]
        natural[16 + i, 20:28] = on_right * right[8 * i : 8 * i + 8]
    for side, layer, k, n, at in MID_Q:
        i = 32 * side + 2 * layer + k
        natural[i, 0:8] = blank
        natural[i, 24:32] = blank
        natural[i, 8 - n : 8] = on_left * far_left[at : at + n]
        natural[i, 8:20] = mid_rows(low, high, 0, side, layer, k, 0, 12)
        natural[i, 20:28] = blank
        natural[i, 20 : 20 + n] = on_right * far_right[at : at + n]

    def begin(z):
        for k in range(2):
            for x in range(4):
                value = weave(natural, z, k, 2, 4, x)
                q[z, 4 * k + x] = value
                w[0][z, 4 * k + x] = FIRST * value

    loop(0, 24, begin)
    for i in range(40):
        natural[i, 0:8] = blank
        natural[i, 24:32] = blank
    for i in range(16):
        natural[12 + i, 2:8] = on_left * left[128 + 6 * i : 134 + 6 * i]
        natural[12 + i, 8:20] = own_r[i, 2:14]
        natural[12 + i, 20:26] = on_right * right[128 + 6 * i : 134 + 6 * i]
    for side, layer, k, n, at in MID_R:
        i = 2 * (layer - 2 if side == 0 else 14 + layer) + k
        at += MID_Q_ROWS
        natural[i, 8 - n : 8] = on_left * far_left[at : at + n]
        natural[i, 8:20] = mid_rows(low, high, 1, side, layer, k, 0, 12)
        natural[i, 20 : 20 + n] = on_right * far_right[at : at + n]

    def roots(z):
        for k in range(2):
            for x in range(4):
                r[z, 4 * k + x] = weave(natural, z, k, 2, 4, x)

    loop(0, 20, roots)
    smooth(w, q, 0, 24, 4, masks, z_scale, DEGREE)

    def total(z):
        for i in range(8):
            y[z, i] = (w[0][z + 7, i] + w[1][z + 7, i]) + (w[2][z + 7, i] + w[3][z + 7, i])

    loop(0, 10, total)

    for m in range(10):
        for x in range(2):
            sums, mean = None, None
            for z in range(2):
                for i in (2 * x, 2 * x + 1, 2 * x + 4, 2 * x + 5):
                    a = r[2 * m + z, i]
                    b = a * q[2 * m + 2 + z, i]
                    sums = b if sums is None else sums + b
                    mean = a if mean is None else mean + a
            mean = 0.125 * mean
            coarse_root[m, pl.ds(x, 8, 2), :] = mean
            if 0 < m < 9:
                coarse[m - 1, pl.ds(x, 8, 2), :] = 0.5 * sums / jnp.maximum(mean, LEAST)
    for m in range(4):
        coarse_low[m] = coarse[m]
        coarse_high[m] = coarse[4 + m]


def coarse_pack_kernel(*refs):
    parts, left, right = refs[:3], refs[3], refs[4]
    at = 0
    for ref in parts:
        for k in range(ref.shape[0]):
            right[at + k] = ref[k, 0:8]
            left[at + k] = ref[k, 8:16]
        at += ref.shape[0]


def finish_kernel(counts, *refs):
    parts, (left, right), refs = refs[:3], refs[3:5], refs[5:]
    coarse_root, mid_q, mid_y, mid_r, fine_q, fine_y, fine_r, out_x, out_r = refs[:9]
    natural, cq, error, spread, mq, mt, fq, ft, plain_x, plain_r, rows_x, rows_r = refs[9:21]
    cw, mw, fw = refs[21:25], refs[25:29], refs[29:33]
    gz, xy = lax.axis_index("gz"), lax.axis_index("xy")

    on_left, on_right = inner(xy, counts[1])

    at = 0
    for ref in parts:
        for k in range(ref.shape[0]):
            natural[at, 0:4] = on_left * left[at, 2:6]
            natural[at, 4:14] = ref[k, 2:12]
            natural[at, 14:18] = on_right * right[at, 0:4]
            natural[at, 18:24] = jnp.zeros((6, LANES), F32)
            for x in range(3):
                value = weave(natural, at, 0, 1, 3, x)
                cq[at, x] = value
                cw[0][at, x] = FIRST * value
            at += 1
    masks = row_masks(3, 4 * xy - 7, 4 * counts[1])
    smooth(cw, cq, 0, 16, 3, masks, z_mask(2 * gz - 7, 2 * counts[0]), DEGREE - 1)
    for k in range(10):
        for x in range(3):
            total = (cw[0][k + 3, x] + cw[1][k + 3, x]) + (cw[2][k + 3, x] + cw[3][k + 3, x])
            natural[k, pl.ds(x, 8, 3), :] = total
        error[k] = natural[k, 2:18] / jnp.maximum(coarse_root[k], LEAST)

    for k in range(10):
        for x in range(4):
            value = error[k, pl.ds(x >> 1, 8, 2), :]
            for i in (x, 4 + x):
                mt[2 * k + 2, i] = mid_r[2 * k, i] * value
                mt[2 * k + 3, i] = mid_r[2 * k + 1, i] * value

    masks = row_masks(4, 8 * xy - 10, 8 * counts[1])
    z_scale = z_mask(4 * gz - 10, 4 * counts[0])

    def mid_correct(z):
        _, rest = applied(mt, z, 4, mid_q)
        scales = [z_scale(z, FIRST) * mask for mask in masks]
        for i, value in enumerate(rest):
            mq[z, i] = value
            mw[0][z, i] = scales[i % 4] * value

    loop(4, 20, mid_correct)
    smooth(mw, mq, 4, 20, 4, masks, z_scale, DEGREE - 1)

    def mid_error(z):
        for k in range(2):
            for x in range(4):
                i = 4 * k + x
                total = (mw[0][z, i] + mw[1][z, i]) + (mw[2][z, i] + mw[3][z, i])
                total = total + (mid_y[z - 7, i] + mt[z, i])
                spread[2 * (z - 7) + k, pl.ds(x, 8, 4), :] = total / jnp.maximum(mid_r[z - 2, i], LEAST)

    loop(7, 17, mid_error)

    def fine_prolong(k):
        for j in range(2):
            for x in range(4):
                value = spread[2 * k + j, pl.ds(6 + (x >> 1), 8, 2), :]
                for i in (8 * j + x, 8 * j + 4 + x):
                    ft[2 * k + 2, i] = fine_r[jnp.maximum(2 * k - 1, 0), i] * value
                    ft[2 * k + 3, i] = fine_r[jnp.minimum(2 * k, 17), i] * value

    loop(0, 10, fine_prolong, 1)
    masks = row_masks(4, 16 * xy - 8, 16 * counts[1])
    z_scale = z_mask(8 * gz - 8, 8 * counts[0])

    def fine_correct(z):
        _, rest = applied(ft, z, 4, fine_q)
        scales = [z_scale(z, FIRST) * mask for mask in masks]
        for i, value in enumerate(rest):
            fq[z, i] = value
            fw[0][z, i] = scales[i % 4] * value

    loop(4, 20, fine_correct)

    def finish(z, rest):
        for k in range(4):
            for x in range(4):
                i = 4 * k + x
                r = fine_r[z - 3, i]
                total = (fw[0][z, i] + fw[1][z, i]) + (fw[2][z, i] + fw[3][z, i])
                total = total + (fine_y[z - 8, i] + ft[z, i])
                plain_x[4 * (z - 8) + k, pl.ds(x, 8, 4), :] = total / r
                plain_r[4 * (z - 8) + k, pl.ds(x, 8, 4), :] = r * rest[i]

    smooth(fw, fq, 4, 20, 4, masks, z_scale, DEGREE, finish)
    matrix = weave_matrix(1)
    for plain, rows, out in ((plain_x, rows_x, out_x), (plain_r, rows_r, out_r)):
        for z in range(8):
            for k in range(4):
                rows[16 * z : 16 * z + 16, LANES * k : LANES * k + LANES] = plain[4 * z + k, 8:24]
        out[...] = exact_product(rows[...], matrix).reshape(8, 16, 512)


def call(kernel, operands, out_shapes, scratch=(), space=pltpu.VMEM):
    whole = pl.BlockSpec(memory_space=pltpu.VMEM)
    return pl.pallas_call(
        kernel,
        out_shape=[jax.ShapeDtypeStruct(s, F32) for s in out_shapes],
        in_specs=[pl.BlockSpec(memory_space=space)] * len(operands),
        out_specs=[whole] * len(out_shapes),
        scratch_shapes=[pltpu.VMEM(s, F32) if isinstance(s, tuple) else s for s in scratch],
        compiler_params=pltpu.CompilerParams(vmem_limit_bytes=30 * 1024 * 1024),
    )(*operands)


def send(block, axis, shift):
    count = lax.axis_size(axis)
    pairs = [(i, i + shift) for i in range(count) if 0 <= i + shift < count]
    return lax.ppermute(block, axis, pairs)


def turn(to_left, to_right):
    count = lax.axis_size("xy")
    left = lax.ppermute(to_right, "xy", [(i, (i + 1) % count) for i in range(count)])
    right = lax.ppermute(to_left, "xy", [(i, (i - 1) % count) for i in range(count)])
    return left, right


def with_counts(kernel):
    counts = (lax.axis_size("gz"), lax.axis_size("xy"))
    return lambda *refs: kernel(counts, *refs)


def on_device(load_field, density, void_mask):
    up, down, root, to_left, to_right = call(
        scale_kernel,
        [pltpu.with_memory_space_constraint(x, pltpu.HBM) for x in (load_field, density, void_mask)],
        [(52, 16, LANES), (52, 16, LANES), (32, 16, LANES)] + [(416, LANES)] * 2,
        [(16, 16, 512), pltpu.VMEM((1, 2, 64), jnp.int32), pltpu.SemaphoreType.DMA((3,))],
        pltpu.HBM,
    )
    low, high = send(up, "gz", 1), send(down, "gz", -1)
    left, right = turn(to_left, to_right)
    low, high, left, right = lax.optimization_barrier((low, high, left, right))
    to_left, to_right = call(fine_pack_kernel, (low, high), [(FINE_Q_ROWS + FINE_R_ROWS, LANES)] * 2)
    far_left, far_right = turn(to_left, to_right)
    fine = (24, 16, 8, LANES)
    fine_q, fine_y, fine_r, mid_q, mid_r, first, second, to_left, to_right = call(
        with_counts(fine_pre_kernel),
        (low, up, root, high, left, right, far_left, far_right),
        [fine, (8, 16, 8, LANES), (18, 16, 8, LANES)] + [(16, 16, LANES)] * 2 + [(336, LANES)] * 2 + [(224, LANES)] * 2,
        [(96, 32, LANES)] + [fine] * 4,
    )
    pairs = mid_pairs(lax.axis_size("gz"))
    first, second = lax.ppermute(first, "gz", pairs[0]), lax.ppermute(second, "gz", pairs[1])
    left, right = turn(to_left, to_right)
    first, second, left, right = lax.optimization_barrier((first, second, left, right))
    low, high, to_left, to_right = call(
        with_counts(mid_pack_kernel), (first, second), [(336, LANES)] * 2 + [(MID_Q_ROWS + MID_R_ROWS, LANES)] * 2
    )
    far_left, far_right = turn(to_left, to_right)
    mid = (24, 8, 8, LANES)
    mid_q, mid_y, mid_r, coarse, coarse_low, coarse_high, coarse_root = call(
        with_counts(mid_pre_kernel),
        (low, high, mid_q, mid_r, left, right, far_left, far_right),
        [mid, (10, 8, 8, LANES), (20, 8, 8, LANES), (8, 16, LANES)] + [(4, 16, LANES)] * 2 + [(10, 16, LANES)],
        [(48, 32, LANES)] + [mid] * 4,
    )
    parts = (send(coarse_low, "gz", 2), coarse, send(coarse_high, "gz", -2))
    to_left, to_right = call(coarse_pack_kernel, parts, [(16, 8, LANES)] * 2)
    left, right = turn(to_left, to_right)
    coarsest = (16, 3, 8, LANES)
    return tuple(
        call(
            with_counts(finish_kernel),
            parts + (left, right, coarse_root, mid_q, mid_y, mid_r, fine_q, fine_y, fine_r),
            [(8, 16, 512), (8, 16, 512)],
            [(16, 24, LANES), coarsest, (10, 16, LANES), (20, 32, LANES), mid, mid, fine, fine]
            + [(32, 32, LANES)] * 2
            + [(128, 512)] * 2
            + [coarsest] * 4
            + [mid] * 4
            + [fine] * 4,
        )
    )


def solution(mesh):
    specs = (P("gz", "xy", None), P("gz", "xy", None), P("gz", "xy", None))
    return jax.shard_map(
        on_device, mesh=mesh, in_specs=specs, out_specs=specs[:2], check_vma=False
    )
```

```python
import jax
import jax.numpy as jnp
from jax import lax
from jax.experimental import pallas as pl
from jax.experimental.pallas import tpu as pltpu
from jax.sharding import PartitionSpec as P


DEGREE = 4
THETA = 1.15
DELTA = 0.85
FIRST = 1.0 / (6.0 * THETA)
LEAST = 0.05
F32 = jnp.float32
LANES = 128


def coefficients():
    sigma = THETA / DELTA
    rho = 1.0 / sigma
    pairs = []
    for turn in range(DEGREE - 1):
        rho_next = 1.0 / (2.0 * sigma - rho)
        pairs.append((rho_next * rho, 2.0 * rho_next / (6.0 * DELTA)))
        rho = rho_next
    return pairs


def recurrences():
    out, c1_old, c2_old = [], 0.0, FIRST
    for c1, c2 in coefficients():
        out.append((c1 + c2 / c2_old - 6.0 * c2, c2 * c1_old / c2_old, c2))
        c1_old, c2_old = c1, c2
    return out, (1.0 / c2_old - 6.0, c1_old / c2_old)


STEPS, LAST = recurrences()


def iota(shape, dim):
    return lax.broadcasted_iota(jnp.int32, shape, dim)


def inner(xy, count):
    return jnp.where(xy > 0, F32(1.0), F32(0.0)), jnp.where(xy < count - 1, F32(1.0), F32(0.0))


def row_masks(n, base, count):
    masks = []
    for x in range(n):
        place = n * iota((8, LANES), 0) + (x + base)
        masks.append(jnp.where((place >= 0) & (place < count), 1.0, 0.0).astype(F32))
    return masks


def z_mask(base, count):
    def scaled(z, value):
        place = z + base
        return jnp.where((place >= 0) & (place < count), F32(value), F32(0.0))

    return scaled


def loop(low, high, body, width=24):
    turns = (high - low) // width if high - low > width else 0

    def step(t, carry):
        for j in range(width):
            body(low + width * t + j)
        return carry

    if turns > 0:
        lax.fori_loop(0, turns, step, 0)
    for z in range(low + turns * width, high):
        body(z)


def around(ref, z, n):
    count = ref.shape[1]
    blocks = count // n
    here = [ref[z, i] for i in range(count)]
    lane = iota((8, LANES), 1)
    before = [jnp.where(lane == 0, 0.0, pltpu.roll(here[(blocks - 1) * n + x], 1, 1)) for x in range(n)]
    after = [jnp.where(lane == LANES - 1, 0.0, pltpu.roll(here[x], LANES - 1, 1)) for x in range(n)]
    total = []
    for k in range(blocks):
        row = here[k * n : k * n + n]
        up = pltpu.roll(row[n - 1], 1, 0)
        down = pltpu.roll(row[0], 7, 0)
        for x in range(n):
            i = k * n + x
            left = here[i - n] if k > 0 else before[x]
            right = here[i + n] if k + 1 < blocks else after[x]
            north = row[x - 1] if x > 0 else up
            south = row[x + 1] if x + 1 < n else down
            total.append(((left + right) + (north + south)) + (ref[z - 1, i] + ref[z + 1, i]))
    return here, total


def applied(ref, z, n, q):
    here, total = around(ref, z, n)
    return here, [q[z, i] - (6.0 * here[i] - total[i]) for i in range(len(here))]


def smooth(w, low, high, n, masks, z_scale, width=24):
    for turn, (a, b, c) in enumerate(STEPS):

        def advance(z, turn=turn, a=a, b=b, c=c):
            here, total = around(w[turn], z, n)
            scales = [z_scale(z, c) * mask for mask in masks]
            for i in range(len(here)):
                value = a * here[i] + scales[i % n] * total[i]
                w[turn + 1][z, i] = value if turn == 0 else value - b * w[turn - 1][z, i]

        loop(low + 1 + turn, high - 1 - turn, advance, width)


def remains(w, z, n):
    here, total = around(w[DEGREE - 1], z, n)
    return [(LAST[0] * here[i] + total[i]) - LAST[1] * w[DEGREE - 2][z, i] for i in range(len(here))]


def weave(source, z, k, blocks, n, x):
    return source[z * blocks + k, pl.ds(x, 8, n), :]


def moved(left, right):
    high = left.astype(jnp.bfloat16)
    low = (left - high.astype(F32)).astype(jnp.bfloat16)
    return jnp.dot(high, right, preferred_element_type=F32) + jnp.dot(low, right, preferred_element_type=F32)


def weave_matrix(dim):
    plain, woven = iota((512, 512), dim), iota((512, 512), 1 - dim)
    same = plain == 4 * (woven & (LANES - 1)) + (woven >> 7)
    return jnp.where(same, 1.0, 0.0).astype(jnp.bfloat16)


CORNER = [8, 8, 8, 8, 7, 6, 5, 4]


def corner_plan(blocks, first, last, rows):
    plan, at = [], 0
    for side in range(2):
        for layer in range(8):
            away = 8 - layer if side == 0 else layer + 1
            if not first <= away <= last:
                continue
            for k in range(blocks):
                count = rows if rows else CORNER[away - 1]
                plan.append((side, layer, k, count, at))
                at += count
    return plan, at


FINE_Q, FINE_Q_ROWS = corner_plan(4, 1, 8, 0)
FINE_R, FINE_R_ROWS = corner_plan(4, 1, 4, 4)
MID_Q, MID_Q_ROWS = corner_plan(2, 1, 8, 0)
MID_R, MID_R_ROWS = corner_plan(2, 1, 6, 6)


def scale_kernel(load_hbm, density_hbm, void_hbm, up, down, root, left, right, both, void, sems):
    copies = [
        pltpu.make_async_copy(load_hbm, both.at[pl.ds(0, 8)], sems.at[0]),
        pltpu.make_async_copy(density_hbm, both.at[pl.ds(8, 8)], sems.at[1]),
        pltpu.make_async_copy(void_hbm, void, sems.at[2]),
    ]
    for copy in copies:
        copy.start()
    matrix = weave_matrix(0)
    copies[2].wait()
    bricks = jnp.where(void[0] == 1, 1.0, 0.0).astype(F32)
    bricks = jnp.concatenate([jnp.broadcast_to(bricks[k : k + 1], (8, 64)) for k in range(2)], axis=0)
    spread = jnp.where((iota((64, LANES), 1) >> 1) == iota((64, LANES), 0), 1.0, 0.0).astype(jnp.bfloat16)
    voids = jnp.dot(bricks.astype(jnp.bfloat16), spread, preferred_element_type=F32)
    copies[0].wait()
    copies[1].wait()
    fields = moved(both[...].reshape(256, 512), matrix)
    for z in range(8):
        for k in range(4):
            b = fields[16 * z : 16 * z + 16, LANES * k : LANES * k + LANES]
            d = fields[128 + 16 * z : 144 + 16 * z, LANES * k : LANES * k + LANES]
            r = jnp.sqrt(jnp.where(voids > 0.5, 0.01, 0.01 + 0.99 * d * d * d))
            q = b / r
            up[4 * z + k] = q
            down[4 * z + k] = q
            root[4 * z + k] = r
            i = 4 * z + k
            left[8 * i : 8 * i + 8] = q[0:8]
            right[8 * i : 8 * i + 8] = q[8:16]
            left[256 + 5 * i : 261 + 5 * i] = r[0:5]
            right[256 + 5 * i : 261 + 5 * i] = r[11:16]
            if z >= 3:
                up[4 * (5 + z) + k] = r
            if z < 5:
                down[4 * (8 + z) + k] = r


def fine_pack_kernel(low, high, left, right):
    for side, layer, k, n, at in FINE_Q:
        ref, i = (low, high)[side], 4 * layer + k
        left[at : at + n] = ref[i, 0:n]
        right[at : at + n] = ref[i, 16 - n : 16]
    for side, layer, k, n, at in FINE_R:
        ref, i = (low, high)[side], 32 + 4 * (layer - 3 if side == 0 else layer) + k
        at += FINE_Q_ROWS
        left[at : at + n] = ref[i, 0:n]
        right[at : at + n] = ref[i, 16 - n : 16]


def fine_pre_kernel(
    counts, low, up, root, high, left, right, far_left, far_right, q, y, r, mid_q, mid_r, early, late, mid_left, mid_right, *scratch
):
    natural, w = scratch[0], scratch[1:5]
    gz, xy = lax.axis_index("gz"), lax.axis_index("xy")
    on_left, on_right = inner(xy, counts[1])
    masks = row_masks(4, 16 * xy - 8, 16 * counts[1])
    z_scale = z_mask(8 * gz - 8, 8 * counts[0])

    blank = jnp.zeros((8, LANES), F32)
    for n, ref in enumerate((low, up, high)):
        for i in range(32):
            natural[32 * n + i, 8:24] = ref[i]
    for i in range(32):
        natural[32 + i, 0:8] = on_left * left[8 * i : 8 * i + 8]
        natural[32 + i, 24:32] = on_right * right[8 * i : 8 * i + 8]
    for side, layer, k, n, at in FINE_Q:
        j = 64 * side + 4 * layer + k
        if n < 8:
            natural[j, 0:8] = blank
            natural[j, 24:32] = blank
        natural[j, 8 - n : 8] = on_left * far_left[at : at + n]
        natural[j, 24 : 24 + n] = on_right * far_right[at : at + n]

    def begin(z):
        for k in range(4):
            for x in range(4):
                w[0][z, 4 * k + x] = FIRST * weave(natural, z, k, 4, 4, x)

    loop(0, 24, begin, 8)

    place = 0
    for ref, first, count in ((low, 32, 20), (root, 0, 32), (high, 32, 20)):
        for i in range(first, first + count):
            natural[place, 0:8] = blank
            natural[place, 8:24] = ref[i]
            natural[place, 24:32] = blank
            place += 1
    for i in range(32):
        natural[20 + i, 3:8] = on_left * left[256 + 5 * i : 261 + 5 * i]
        natural[20 + i, 24:29] = on_right * right[256 + 5 * i : 261 + 5 * i]
    for side, layer, k, n, at in FINE_R:
        j = 4 * (layer - 3 if side == 0 else 13 + layer) + k
        at += FINE_Q_ROWS
        natural[j, 8 - n : 8] = on_left * far_left[at : at + n]
        natural[j, 24 : 24 + n] = on_right * far_right[at : at + n]

    def roots(z):
        for k in range(4):
            for x in range(4):
                r[z, 4 * k + x] = weave(natural, z, k, 4, 4, x)

    loop(0, 18, roots, 6)
    smooth(w, 0, 24, 4, masks, z_scale, 8)

    def rest(z):
        for i, value in enumerate(remains(w, z, 4)):
            q[z, i] = value

    loop(4, 20, rest, 8)

    def total(z):
        for i in range(16):
            y[z, i] = (w[0][z + 8, i] + w[1][z + 8, i]) + (w[2][z + 8, i] + w[3][z + 8, i])

    loop(0, 8, total)

    def fold(m):
        for k in range(2):
            for x in range(2):
                sums, roots = None, None
                for z in range(2):
                    for i in (8 * k + 2 * x, 8 * k + 2 * x + 1, 8 * k + 2 * x + 4, 8 * k + 2 * x + 5):
                        a = r[2 * m + 1 + z, i]
                        b = a * q[2 * m + 4 + z, i]
                        sums = b if sums is None else sums + b
                        roots = a if roots is None else roots + a
                roots = 0.125 * roots
                mid_r[2 * m + k, pl.ds(x, 8, 2), :] = roots
                mid_q[2 * m + k, pl.ds(x, 8, 2), :] = 0.5 * sums / jnp.maximum(roots, LEAST)

    loop(0, 8, fold)
    skip = jnp.where(gz % 4 == 3, 0, 2)
    for out, start in ((early, skip), (late, 2 - skip)):
        for i in range(16):
            out[12 * i : 12 * i + 12] = mid_q[i, 2:14]
        for i in range(12):
            out[192 + 12 * i : 204 + 12 * i] = mid_r[2 * start + i, 2:14]
    for i in range(16):
        mid_right[8 * i : 8 * i + 8] = mid_q[i, 2:10]
        mid_left[8 * i : 8 * i + 8] = mid_q[i, 6:14]
        mid_right[128 + 6 * i : 134 + 6 * i] = mid_r[i, 4:10]
        mid_left[128 + 6 * i : 134 + 6 * i] = mid_r[i, 6:12]


def mid_pairs(count):
    first, second = [], []
    for i in range(count):
        up, down = (first, second) if i % 4 != 3 else (second, first)
        if i + 2 < count:
            up.append((i, i + 2))
        if i >= 2:
            down.append((i, i - 2))
    return first, second + [(0, 1), (count - 1, count - 2)]


def mid_sides(count, gz, first, second, low, high):
    @pl.when(gz % 4 != 1)
    def _():
        low[...] = first[...]
        high[...] = second[...]

    @pl.when(gz % 4 == 1)
    def _():
        low[...] = second[...]
        high[...] = first[...]

    @pl.when(gz == 1)
    def _():
        low[0:96] = jnp.zeros((96, LANES), F32)
        low[96:192] = second[0:96]
        low[192:240] = jnp.zeros((48, LANES), F32)
        low[240:336] = second[192:288]

    @pl.when(gz == count - 2)
    def _():
        high[0:96] = second[96:192]
        high[96:192] = jnp.zeros((96, LANES), F32)
        high[192:288] = second[240:336]
        high[288:336] = jnp.zeros((48, LANES), F32)


def mid_rows(low, high, field, side, layer, k, start, stop):
    at = 12 * (2 * layer + k) + (0 if field == 0 else 144 if side == 0 else 192)
    return (low, high)[side][at + start : at + stop]


def mid_pack_kernel(counts, first, second, low, high, left, right):
    mid_sides(counts[0], lax.axis_index("gz"), first, second, low, high)
    for field, plan, base in ((0, MID_Q, 0), (1, MID_R, MID_Q_ROWS)):
        for side, layer, k, n, at in plan:
            at += base
            right[at : at + n] = mid_rows(low, high, field, side, layer, k, 8 - n, 8)
            left[at : at + n] = mid_rows(low, high, field, side, layer, k, 4, 4 + n)


def mid_pre_kernel(counts, *refs):
    (low, high, own_q, own_r, left, right, far_left, far_right), refs = refs[:8], refs[8:]
    q, y, r, coarse, coarse_low, coarse_high, coarse_root, natural = refs[:8]
    w = refs[8:]
    gz, xy = lax.axis_index("gz"), lax.axis_index("xy")
    on_left, on_right = inner(xy, counts[1])
    masks = row_masks(4, 8 * xy - 10, 8 * counts[1])
    z_scale = z_mask(4 * gz - 10, 4 * counts[0])
    blank = jnp.zeros((8, LANES), F32)
    for i in range(16):
        natural[16 + i, 0:8] = on_left * left[8 * i : 8 * i + 8]
        natural[16 + i, 24:32] = blank
        natural[16 + i, 8:20] = own_q[i, 2:14]
        natural[16 + i, 20:28] = on_right * right[8 * i : 8 * i + 8]
    for side, layer, k, n, at in MID_Q:
        i = 32 * side + 2 * layer + k
        natural[i, 0:8] = blank
        natural[i, 24:32] = blank
        natural[i, 8 - n : 8] = on_left * far_left[at : at + n]
        natural[i, 8:20] = mid_rows(low, high, 0, side, layer, k, 0, 12)
        natural[i, 20:28] = blank
        natural[i, 20 : 20 + n] = on_right * far_right[at : at + n]

    def begin(z):
        for k in range(2):
            for x in range(4):
                w[0][z, 4 * k + x] = FIRST * weave(natural, z, k, 2, 4, x)

    loop(0, 24, begin)
    for i in range(40):
        natural[i, 0:8] = blank
        natural[i, 24:32] = blank
    for i in range(16):
        natural[12 + i, 2:8] = on_left * left[128 + 6 * i : 134 + 6 * i]
        natural[12 + i, 8:20] = own_r[i, 2:14]
        natural[12 + i, 20:26] = on_right * right[128 + 6 * i : 134 + 6 * i]
    for side, layer, k, n, at in MID_R:
        i = 2 * (layer - 2 if side == 0 else 14 + layer) + k
        at += MID_Q_ROWS
        natural[i, 8 - n : 8] = on_left * far_left[at : at + n]
        natural[i, 8:20] = mid_rows(low, high, 1, side, layer, k, 0, 12)
        natural[i, 20 : 20 + n] = on_right * far_right[at : at + n]

    def roots(z):
        for k in range(2):
            for x in range(4):
                r[z, 4 * k + x] = weave(natural, z, k, 2, 4, x)

    loop(0, 20, roots)
    smooth(w, 0, 24, 4, masks, z_scale)

    def rest(z):
        for i, value in enumerate(remains(w, z, 4)):
            q[z, i] = value

    loop(4, 20, rest)

    def total(z):
        for i in range(8):
            y[z, i] = (w[0][z + 7, i] + w[1][z + 7, i]) + (w[2][z + 7, i] + w[3][z + 7, i])

    loop(0, 10, total)

    for m in range(10):
        for x in range(2):
            sums, mean = None, None
            for z in range(2):
                for i in (2 * x, 2 * x + 1, 2 * x + 4, 2 * x + 5):
                    a = r[2 * m + z, i]
                    b = a * q[2 * m + 2 + z, i]
                    sums = b if sums is None else sums + b
                    mean = a if mean is None else mean + a
            mean = 0.125 * mean
            coarse_root[m, pl.ds(x, 8, 2), :] = mean
            if 0 < m < 9:
                coarse[m - 1, pl.ds(x, 8, 2), :] = 0.5 * sums / jnp.maximum(mean, LEAST)
    for m in range(4):
        coarse_low[m] = coarse[m]
        coarse_high[m] = coarse[4 + m]


def coarse_pack_kernel(*refs):
    parts, left, right = refs[:3], refs[3], refs[4]
    at = 0
    for ref in parts:
        for k in range(ref.shape[0]):
            right[at + k] = ref[k, 0:8]
            left[at + k] = ref[k, 8:16]
        at += ref.shape[0]


def finish_kernel(counts, *refs):
    parts, (left, right), refs = refs[:3], refs[3:5], refs[5:]
    coarse_root, mid_q, mid_y, mid_r, fine_q, fine_y, fine_r, out_x, out_r = refs[:9]
    natural, error, spread, mt, ft, plain_x, plain_r, rows_x, rows_r = refs[9:18]
    cw, mw, fw = refs[18:22], refs[22:26], refs[26:30]
    ready_x, ready_r, sems = refs[30:]
    gz, xy = lax.axis_index("gz"), lax.axis_index("xy")

    on_left, on_right = inner(xy, counts[1])

    at = 0
    for ref in parts:
        for k in range(ref.shape[0]):
            natural[at, 0:4] = on_left * left[at, 2:6]
            natural[at, 4:14] = ref[k, 2:12]
            natural[at, 14:18] = on_right * right[at, 0:4]
            natural[at, 18:24] = jnp.zeros((6, LANES), F32)
            for x in range(3):
                cw[0][at, x] = FIRST * weave(natural, at, 0, 1, 3, x)
            at += 1
    masks = row_masks(3, 4 * xy - 7, 4 * counts[1])
    smooth(cw, 0, 16, 3, masks, z_mask(2 * gz - 7, 2 * counts[0]))
    for k in range(10):
        for x in range(3):
            total = (cw[0][k + 3, x] + cw[1][k + 3, x]) + (cw[2][k + 3, x] + cw[3][k + 3, x])
            natural[k, pl.ds(x, 8, 3), :] = total
        error[k] = natural[k, 2:18] / jnp.maximum(coarse_root[k], LEAST)

    for k in range(10):
        for x in range(4):
            value = error[k, pl.ds(x >> 1, 8, 2), :]
            for i in (x, 4 + x):
                mt[2 * k + 2, i] = mid_r[2 * k, i] * value
                mt[2 * k + 3, i] = mid_r[2 * k + 1, i] * value

    masks = row_masks(4, 8 * xy - 10, 8 * counts[1])
    z_scale = z_mask(4 * gz - 10, 4 * counts[0])

    def mid_correct(z):
        _, rest = applied(mt, z, 4, mid_q)
        scales = [z_scale(z, FIRST) * mask for mask in masks]
        for i, value in enumerate(rest):
            mw[0][z, i] = scales[i % 4] * value

    loop(4, 20, mid_correct)
    smooth(mw, 4, 20, 4, masks, z_scale)

    def mid_error(z):
        for k in range(2):
            for x in range(4):
                i = 4 * k + x
                total = (mw[0][z, i] + mw[1][z, i]) + (mw[2][z, i] + mw[3][z, i])
                total = total + (mid_y[z - 7, i] + mt[z, i])
                spread[2 * (z - 7) + k, pl.ds(x, 8, 4), :] = total / jnp.maximum(mid_r[z - 2, i], LEAST)

    loop(7, 17, mid_error)

    def fine_prolong(k):
        for j in range(2):
            for x in range(4):
                value = spread[2 * k + j, pl.ds(6 + (x >> 1), 8, 2), :]
                for i in (8 * j + x, 8 * j + 4 + x):
                    ft[2 * k + 2, i] = fine_r[jnp.maximum(2 * k - 1, 0), i] * value
                    ft[2 * k + 3, i] = fine_r[jnp.minimum(2 * k, 17), i] * value

    loop(0, 10, fine_prolong, 10)
    masks = row_masks(4, 16 * xy - 8, 16 * counts[1])
    z_scale = z_mask(8 * gz - 8, 8 * counts[0])

    def fine_correct(z):
        _, rest = applied(ft, z, 4, fine_q)
        scales = [z_scale(z, FIRST) * mask for mask in masks]
        for i, value in enumerate(rest):
            fw[0][z, i] = scales[i % 4] * value

    loop(4, 20, fine_correct)

    smooth(fw, 4, 20, 4, masks, z_scale)
    matrix = weave_matrix(1)

    def leave(plain, rows, ready, out, sem):
        for z in range(8):
            for k in range(4):
                rows[16 * z : 16 * z + 16, LANES * k : LANES * k + LANES] = plain[4 * z + k, 8:24]
        ready[...] = moved(rows[...], matrix).reshape(8, 16, 512)
        copy = pltpu.make_async_copy(ready, out, sem)
        copy.start()
        return copy

    for z in range(8, 16):
        for k in range(4):
            for x in range(4):
                i = 4 * k + x
                total = (fw[0][z, i] + fw[1][z, i]) + (fw[2][z, i] + fw[3][z, i])
                total = total + (fine_y[z - 8, i] + ft[z, i])
                plain_x[4 * (z - 8) + k, pl.ds(x, 8, 4), :] = total / fine_r[z - 3, i]
    first = leave(plain_x, rows_x, ready_x, out_x, sems.at[0])
    for z in range(8, 16):
        rest = remains(fw, z, 4)
        for k in range(4):
            for x in range(4):
                i = 4 * k + x
                plain_r[4 * (z - 8) + k, pl.ds(x, 8, 4), :] = fine_r[z - 3, i] * rest[i]
    second = leave(plain_r, rows_r, ready_r, out_r, sems.at[1])
    first.wait()
    second.wait()


def call(kernel, operands, out_shapes, scratch=(), space=pltpu.VMEM, out_space=pltpu.VMEM):
    whole = pl.BlockSpec(memory_space=out_space)
    return pl.pallas_call(
        kernel,
        out_shape=[jax.ShapeDtypeStruct(s, F32) for s in out_shapes],
        in_specs=[pl.BlockSpec(memory_space=space)] * len(operands),
        out_specs=[whole] * len(out_shapes),
        scratch_shapes=[pltpu.VMEM(s, F32) if isinstance(s, tuple) else s for s in scratch],
        compiler_params=pltpu.CompilerParams(vmem_limit_bytes=30 * 1024 * 1024),
    )(*operands)


def send(block, axis, shift):
    count = lax.axis_size(axis)
    pairs = [(i, i + shift) for i in range(count) if 0 <= i + shift < count]
    return lax.ppermute(block, axis, pairs)


def turn(to_left, to_right):
    count = lax.axis_size("xy")
    left = lax.ppermute(to_right, "xy", [(i, (i + 1) % count) for i in range(count)])
    right = lax.ppermute(to_left, "xy", [(i, (i - 1) % count) for i in range(count)])
    return left, right


def with_counts(kernel):
    counts = (lax.axis_size("gz"), lax.axis_size("xy"))
    return lambda *refs: kernel(counts, *refs)


def on_device(load_field, density, void_mask):
    up, down, root, to_left, to_right = call(
        scale_kernel,
        [pltpu.with_memory_space_constraint(x, pltpu.HBM) for x in (load_field, density, void_mask)],
        [(52, 16, LANES), (52, 16, LANES), (32, 16, LANES)] + [(416, LANES)] * 2,
        [(16, 16, 512), pltpu.VMEM((1, 2, 64), jnp.int32), pltpu.SemaphoreType.DMA((3,))],
        pltpu.HBM,
    )
    low, high = send(up, "gz", 1), send(down, "gz", -1)
    left, right = turn(to_left, to_right)
    low, high, left, right = lax.optimization_barrier((low, high, left, right))
    to_left, to_right = call(fine_pack_kernel, (low, high), [(FINE_Q_ROWS + FINE_R_ROWS, LANES)] * 2)
    far_left, far_right = turn(to_left, to_right)
    fine = (24, 16, 8, LANES)
    fine_q, fine_y, fine_r, mid_q, mid_r, first, second, to_left, to_right = call(
        with_counts(fine_pre_kernel),
        (low, up, root, high, left, right, far_left, far_right),
        [fine, (8, 16, 8, LANES), (18, 16, 8, LANES)] + [(16, 16, LANES)] * 2 + [(336, LANES)] * 2 + [(224, LANES)] * 2,
        [(96, 32, LANES)] + [fine] * 4,
    )
    pairs = mid_pairs(lax.axis_size("gz"))
    first, second = lax.ppermute(first, "gz", pairs[0]), lax.ppermute(second, "gz", pairs[1])
    left, right = turn(to_left, to_right)
    first, second, left, right = lax.optimization_barrier((first, second, left, right))
    low, high, to_left, to_right = call(
        with_counts(mid_pack_kernel), (first, second), [(336, LANES)] * 2 + [(MID_Q_ROWS + MID_R_ROWS, LANES)] * 2
    )
    far_left, far_right = turn(to_left, to_right)
    mid = (24, 8, 8, LANES)
    mid_q, mid_y, mid_r, coarse, coarse_low, coarse_high, coarse_root = call(
        with_counts(mid_pre_kernel),
        (low, high, mid_q, mid_r, left, right, far_left, far_right),
        [mid, (10, 8, 8, LANES), (20, 8, 8, LANES), (8, 16, LANES)] + [(4, 16, LANES)] * 2 + [(10, 16, LANES)],
        [(48, 32, LANES)] + [mid] * 4,
    )
    parts = (send(coarse_low, "gz", 2), coarse, send(coarse_high, "gz", -2))
    to_left, to_right = call(coarse_pack_kernel, parts, [(16, 8, LANES)] * 2)
    left, right = turn(to_left, to_right)
    coarsest = (16, 3, 8, LANES)
    return tuple(
        call(
            with_counts(finish_kernel),
            parts + (left, right, coarse_root, mid_q, mid_y, mid_r, fine_q, fine_y, fine_r),
            [(8, 16, 512), (8, 16, 512)],
            [(16, 24, LANES), (10, 16, LANES), (20, 32, LANES), mid, fine]
            + [(32, 32, LANES)] * 2
            + [(128, 512)] * 2
            + [coarsest] * 4
            + [mid] * 4
            + [fine] * 4
            + [(8, 16, 512)] * 2
            + [pltpu.SemaphoreType.DMA((2,))],
            out_space=pl.ANY,
        )
    )


def solution(mesh):
    specs = (P("gz", "xy", None), P("gz", "xy", None), P("gz", "xy", None))
    return jax.shard_map(
        on_device, mesh=mesh, in_specs=specs, out_specs=specs[:2], check_vma=False
    )
```

```python
import jax
import jax.numpy as jnp
from jax import lax
from jax.experimental import pallas as pl
from jax.experimental.pallas import tpu as pltpu
from jax.sharding import PartitionSpec as P


DEGREE = 4
THETA = 1.15
DELTA = 0.85
FIRST = 1.0 / (6.0 * THETA)
LEAST = 0.05
F32 = jnp.float32
LANES = 128


def coefficients():
    sigma = THETA / DELTA
    rho = 1.0 / sigma
    pairs = []
    for turn in range(DEGREE - 1):
        rho_next = 1.0 / (2.0 * sigma - rho)
        pairs.append((rho_next * rho, 2.0 * rho_next / (6.0 * DELTA)))
        rho = rho_next
    return pairs


def recurrences():
    out, c1_old, c2_old = [], 0.0, FIRST
    for c1, c2 in coefficients():
        out.append((c1 + c2 / c2_old - 6.0 * c2, c2 * c1_old / c2_old, c2))
        c1_old, c2_old = c1, c2
    return out, (1.0 / c2_old - 6.0, c1_old / c2_old)


STEPS, LAST = recurrences()


def iota(shape, dim):
    return lax.broadcasted_iota(jnp.int32, shape, dim)


def inner(xy, count):
    return jnp.where(xy > 0, F32(1.0), F32(0.0)), jnp.where(xy < count - 1, F32(1.0), F32(0.0))


def row_masks(n, base, count):
    masks = []
    for x in range(n):
        place = n * iota((8, LANES), 0) + (x + base)
        masks.append(jnp.where((place >= 0) & (place < count), 1.0, 0.0).astype(F32))
    return masks


def z_mask(base, count):
    def scaled(z, value):
        place = z + base
        return jnp.where((place >= 0) & (place < count), F32(value), F32(0.0))

    return scaled


def loop(low, high, body, width=24):
    turns = (high - low) // width if high - low > width else 0

    def step(t, carry):
        for j in range(width):
            body(low + width * t + j)
        return carry

    if turns > 0:
        lax.fori_loop(0, turns, step, 0)
    for z in range(low + turns * width, high):
        body(z)


def around(ref, z, n):
    count = ref.shape[1]
    blocks = count // n
    here = [ref[z, i] for i in range(count)]
    lane = iota((8, LANES), 1)
    before = [jnp.where(lane == 0, 0.0, pltpu.roll(here[(blocks - 1) * n + x], 1, 1)) for x in range(n)]
    after = [jnp.where(lane == LANES - 1, 0.0, pltpu.roll(here[x], LANES - 1, 1)) for x in range(n)]
    total = []
    for k in range(blocks):
        row = here[k * n : k * n + n]
        up = pltpu.roll(row[n - 1], 1, 0)
        down = pltpu.roll(row[0], 7, 0)
        for x in range(n):
            i = k * n + x
            left = here[i - n] if k > 0 else before[x]
            right = here[i + n] if k + 1 < blocks else after[x]
            north = row[x - 1] if x > 0 else up
            south = row[x + 1] if x + 1 < n else down
            total.append(((left + right) + (north + south)) + (ref[z - 1, i] + ref[z + 1, i]))
    return here, total


def applied(ref, z, n, q):
    here, total = around(ref, z, n)
    return here, [q[z, i] - (6.0 * here[i] - total[i]) for i in range(len(here))]


def smooth(w, low, high, n, masks, z_scale, width=24):
    for turn, (a, b, c) in enumerate(STEPS):

        def advance(z, turn=turn, a=a, b=b, c=c):
            here, total = around(w[turn], z, n)
            scales = [z_scale(z, c) * mask for mask in masks]
            for i in range(len(here)):
                value = a * here[i] + scales[i % n] * total[i]
                w[turn + 1][z, i] = value if turn == 0 else value - b * w[turn - 1][z, i]

        loop(low + 1 + turn, high - 1 - turn, advance, width)


def remains(w, z, n):
    here, total = around(w[DEGREE - 1], z, n)
    return [(LAST[0] * here[i] + total[i]) - LAST[1] * w[DEGREE - 2][z, i] for i in range(len(here))]


def weave(source, z, k, blocks, n, x):
    return source[z * blocks + k, pl.ds(x, 8, n), :]


def moved(left, right):
    high = left.astype(jnp.bfloat16)
    low = (left - high.astype(F32)).astype(jnp.bfloat16)
    return jnp.dot(high, right, preferred_element_type=F32) + jnp.dot(low, right, preferred_element_type=F32)


def weave_matrix(dim):
    plain, woven = iota((512, 512), dim), iota((512, 512), 1 - dim)
    same = plain == 4 * (woven & (LANES - 1)) + (woven >> 7)
    return jnp.where(same, 1.0, 0.0).astype(jnp.bfloat16)


CORNER = [8, 8, 8, 8, 7, 6, 5, 4]


def corner_plan(blocks, first, last, rows):
    plan, at = [], 0
    for side in range(2):
        for layer in range(8):
            away = 8 - layer if side == 0 else layer + 1
            if not first <= away <= last:
                continue
            for k in range(blocks):
                count = rows if rows else CORNER[away - 1]
                plan.append((side, layer, k, count, at))
                at += count
    return plan, at


FINE_Q, FINE_Q_ROWS = corner_plan(4, 1, 8, 0)
FINE_R, FINE_R_ROWS = corner_plan(4, 1, 4, 4)
MID_Q, MID_Q_ROWS = corner_plan(2, 1, 8, 0)
MID_R, MID_R_ROWS = corner_plan(2, 1, 6, 8)


def scale_kernel(load_hbm, density_hbm, void_hbm, up, down, root, left, right, both, void, sems):
    copies = [
        pltpu.make_async_copy(load_hbm, both.at[pl.ds(0, 8)], sems.at[0]),
        pltpu.make_async_copy(density_hbm, both.at[pl.ds(8, 8)], sems.at[1]),
        pltpu.make_async_copy(void_hbm, void, sems.at[2]),
    ]
    for copy in copies:
        copy.start()
    matrix = weave_matrix(0)
    copies[2].wait()
    bricks = jnp.where(void[0] == 1, 1.0, 0.0).astype(F32)
    bricks = jnp.concatenate([jnp.broadcast_to(bricks[k : k + 1], (8, 64)) for k in range(2)], axis=0)
    spread = jnp.where((iota((64, LANES), 1) >> 1) == iota((64, LANES), 0), 1.0, 0.0).astype(jnp.bfloat16)
    voids = jnp.dot(bricks.astype(jnp.bfloat16), spread, preferred_element_type=F32)
    copies[0].wait()
    copies[1].wait()
    fields = moved(both[...].reshape(256, 512), matrix)
    for z in range(8):
        for k in range(4):
            b = fields[16 * z : 16 * z + 16, LANES * k : LANES * k + LANES]
            d = fields[128 + 16 * z : 144 + 16 * z, LANES * k : LANES * k + LANES]
            r = jnp.sqrt(jnp.where(voids > 0.5, 0.01, 0.01 + 0.99 * d * d * d))
            q = b / r
            up[4 * z + k] = q
            down[4 * z + k] = q
            root[4 * z + k] = r
            i = 4 * z + k
            left[8 * i : 8 * i + 8] = q[0:8]
            right[8 * i : 8 * i + 8] = q[8:16]
            left[256 + 5 * i : 261 + 5 * i] = r[0:5]
            right[256 + 5 * i : 261 + 5 * i] = r[11:16]
            if z >= 3:
                up[4 * (5 + z) + k] = r
            if z < 5:
                down[4 * (8 + z) + k] = r


def fine_pack_kernel(low, high, left, right):
    for side, layer, k, n, at in FINE_Q:
        ref, i = (low, high)[side], 4 * layer + k
        left[at : at + n] = ref[i, 0:n]
        right[at : at + n] = ref[i, 16 - n : 16]
    for side, layer, k, n, at in FINE_R:
        ref, i = (low, high)[side], 32 + 4 * (layer - 3 if side == 0 else layer) + k
        at += FINE_Q_ROWS
        left[at : at + n] = ref[i, 0:n]
        right[at : at + n] = ref[i, 16 - n : 16]


def fine_pre_kernel(
    counts, low, up, root, high, left, right, far_left, far_right, q, y, r, mid_q, mid_r, early, late, mid_left, mid_right, *scratch
):
    natural, w = scratch[0], scratch[1:5]
    gz, xy = lax.axis_index("gz"), lax.axis_index("xy")
    on_left, on_right = inner(xy, counts[1])
    masks = row_masks(4, 16 * xy - 8, 16 * counts[1])
    z_scale = z_mask(8 * gz - 8, 8 * counts[0])

    blank = jnp.zeros((8, LANES), F32)
    for n, ref in enumerate((low, up, high)):
        for i in range(32):
            natural[32 * n + i, 8:24] = ref[i]
    for i in range(32):
        natural[32 + i, 0:8] = on_left * left[8 * i : 8 * i + 8]
        natural[32 + i, 24:32] = on_right * right[8 * i : 8 * i + 8]
    for side, layer, k, n, at in FINE_Q:
        j = 64 * side + 4 * layer + k
        if n < 8:
            natural[j, 0:8] = blank
            natural[j, 24:32] = blank
        natural[j, 8 - n : 8] = on_left * far_left[at : at + n]
        natural[j, 24 : 24 + n] = on_right * far_right[at : at + n]

    def begin(z):
        for k in range(4):
            for x in range(4):
                w[0][z, 4 * k + x] = FIRST * weave(natural, z, k, 4, 4, x)

    loop(0, 24, begin, 8)

    place = 0
    for ref, first, count in ((low, 32, 20), (root, 0, 32), (high, 32, 20)):
        for i in range(first, first + count):
            natural[place, 0:8] = blank
            natural[place, 8:24] = ref[i]
            natural[place, 24:32] = blank
            place += 1
    for i in range(32):
        natural[20 + i, 3:8] = on_left * left[256 + 5 * i : 261 + 5 * i]
        natural[20 + i, 24:29] = on_right * right[256 + 5 * i : 261 + 5 * i]
    for side, layer, k, n, at in FINE_R:
        j = 4 * (layer - 3 if side == 0 else 13 + layer) + k
        at += FINE_Q_ROWS
        natural[j, 8 - n : 8] = on_left * far_left[at : at + n]
        natural[j, 24 : 24 + n] = on_right * far_right[at : at + n]

    def roots(z):
        for k in range(4):
            for x in range(4):
                r[z, 4 * k + x] = weave(natural, z, k, 4, 4, x)

    loop(0, 18, roots, 6)
    smooth(w, 0, 24, 4, masks, z_scale, 8)

    def rest(z):
        for i, value in enumerate(remains(w, z, 4)):
            q[z, i] = value

    loop(4, 20, rest, 8)

    def total(z):
        for i in range(16):
            y[z, i] = (w[0][z + 8, i] + w[1][z + 8, i]) + (w[2][z + 8, i] + w[3][z + 8, i])

    loop(0, 8, total)

    def fold(m):
        for k in range(2):
            for x in range(2):
                sums, roots = None, None
                for z in range(2):
                    for i in (8 * k + 2 * x, 8 * k + 2 * x + 1, 8 * k + 2 * x + 4, 8 * k + 2 * x + 5):
                        a = r[2 * m + 1 + z, i]
                        b = a * q[2 * m + 4 + z, i]
                        sums = b if sums is None else sums + b
                        roots = a if roots is None else roots + a
                roots = 0.125 * roots
                mid_r[2 * m + k, pl.ds(x, 8, 2), :] = roots
                mid_q[2 * m + k, pl.ds(x, 8, 2), :] = 0.5 * sums / jnp.maximum(roots, LEAST)

    loop(0, 8, fold)
    skip = jnp.where(gz % 4 == 3, 0, 2)
    for out, start in ((early, skip), (late, 2 - skip)):
        for i in range(16):
            out[12 * i : 12 * i + 12] = mid_q[i, 2:14]
        for i in range(12):
            out[192 + 8 * i : 200 + 8 * i] = mid_r[2 * start + i, 4:12]
    for i in range(16):
        mid_right[8 * i : 8 * i + 8] = mid_q[i, 2:10]
        mid_left[8 * i : 8 * i + 8] = mid_q[i, 6:14]
        mid_right[128 + 6 * i : 134 + 6 * i] = mid_r[i, 4:10]
        mid_left[128 + 6 * i : 134 + 6 * i] = mid_r[i, 6:12]


def mid_pairs(count):
    first, second = [], []
    for i in range(count):
        up, down = (first, second) if i % 4 != 3 else (second, first)
        if i + 2 < count:
            up.append((i, i + 2))
        if i >= 2:
            down.append((i, i - 2))
    return first, second + [(0, 1), (count - 1, count - 2)]


def mid_sides(count, gz, first, second, low, high):
    @pl.when(gz % 4 != 1)
    def _():
        low[...] = first[...]
        high[...] = second[...]

    @pl.when(gz % 4 == 1)
    def _():
        low[...] = second[...]
        high[...] = first[...]

    @pl.when(gz == 1)
    def _():
        low[0:96] = jnp.zeros((96, LANES), F32)
        low[96:192] = second[0:96]
        low[192:224] = jnp.zeros((32, LANES), F32)
        low[224:288] = second[192:256]

    @pl.when(gz == count - 2)
    def _():
        high[0:96] = second[96:192]
        high[96:192] = jnp.zeros((96, LANES), F32)
        high[192:256] = second[224:288]
        high[256:288] = jnp.zeros((32, LANES), F32)


def mid_rows(low, high, side, layer, k, start, stop):
    at = 12 * (2 * layer + k)
    return (low, high)[side][at + start : at + stop]


def mid_root_rows(low, high, side, layer, k):
    at = 192 + 8 * (2 * (layer - 2 if side == 0 else layer) + k)
    return (low, high)[side][at : at + 8]


def mid_pack_kernel(counts, first, second, low, high, left, right):
    mid_sides(counts[0], lax.axis_index("gz"), first, second, low, high)
    for side, layer, k, n, at in MID_Q:
        right[at : at + n] = mid_rows(low, high, side, layer, k, 8 - n, 8)
        left[at : at + n] = mid_rows(low, high, side, layer, k, 4, 4 + n)
    for side, layer, k, n, at in MID_R:
        at += MID_Q_ROWS
        right[at : at + n] = mid_root_rows(low, high, side, layer, k)
        left[at : at + n] = mid_root_rows(low, high, side, layer, k)


def mid_pre_kernel(counts, *refs):
    (low, high, own_q, own_r, left, right, far_left, far_right), refs = refs[:8], refs[8:]
    q, y, r, coarse, coarse_low, coarse_high, coarse_root, natural = refs[:8]
    w = refs[8:]
    gz, xy = lax.axis_index("gz"), lax.axis_index("xy")
    on_left, on_right = inner(xy, counts[1])
    masks = row_masks(4, 8 * xy - 10, 8 * counts[1])
    z_scale = z_mask(4 * gz - 10, 4 * counts[0])
    blank = jnp.zeros((8, LANES), F32)
    for i in range(16):
        natural[16 + i, 0:8] = on_left * left[8 * i : 8 * i + 8]
        natural[16 + i, 24:32] = blank
        natural[16 + i, 8:20] = own_q[i, 2:14]
        natural[16 + i, 20:28] = on_right * right[8 * i : 8 * i + 8]
    for side, layer, k, n, at in MID_Q:
        i = 32 * side + 2 * layer + k
        natural[i, 0:8] = blank
        natural[i, 24:32] = blank
        natural[i, 8 - n : 8] = on_left * far_left[at : at + n]
        natural[i, 8:20] = mid_rows(low, high, side, layer, k, 0, 12)
        natural[i, 20:28] = blank
        natural[i, 20 : 20 + n] = on_right * far_right[at : at + n]

    def begin(z):
        for k in range(2):
            for x in range(4):
                w[0][z, 4 * k + x] = FIRST * weave(natural, z, k, 2, 4, x)

    loop(0, 24, begin)
    for i in range(40):
        natural[i, 0:8] = blank
        natural[i, 24:32] = blank
    for i in range(16):
        natural[12 + i, 2:8] = on_left * left[128 + 6 * i : 134 + 6 * i]
        natural[12 + i, 8:20] = own_r[i, 2:14]
        natural[12 + i, 20:26] = on_right * right[128 + 6 * i : 134 + 6 * i]
    for side, layer, k, n, at in MID_R:
        i = 2 * (layer - 2 if side == 0 else 14 + layer) + k
        at += MID_Q_ROWS
        natural[i, 2:10] = on_left * far_left[at : at + n]
        natural[i, 10:18] = mid_root_rows(low, high, side, layer, k)
        natural[i, 18:26] = on_right * far_right[at : at + n]

    def roots(z):
        for k in range(2):
            for x in range(4):
                r[z, 4 * k + x] = weave(natural, z, k, 2, 4, x)

    loop(0, 20, roots)
    smooth(w, 0, 24, 4, masks, z_scale)

    def rest(z):
        for i, value in enumerate(remains(w, z, 4)):
            q[z, i] = value

    loop(4, 20, rest)

    def total(z):
        for i in range(8):
            y[z, i] = (w[0][z + 7, i] + w[1][z + 7, i]) + (w[2][z + 7, i] + w[3][z + 7, i])

    loop(0, 10, total)

    for m in range(10):
        for x in range(2):
            sums, mean = None, None
            for z in range(2):
                for i in (2 * x, 2 * x + 1, 2 * x + 4, 2 * x + 5):
                    a = r[2 * m + z, i]
                    b = a * q[2 * m + 2 + z, i]
                    sums = b if sums is None else sums + b
                    mean = a if mean is None else mean + a
            mean = 0.125 * mean
            coarse_root[m, pl.ds(x, 8, 2), :] = mean
            if 0 < m < 9:
                coarse[m - 1, pl.ds(x, 8, 2), :] = 0.5 * sums / jnp.maximum(mean, LEAST)
    for m in range(4):
        coarse_low[m] = coarse[m]
        coarse_high[m] = coarse[4 + m]


def coarse_pack_kernel(*refs):
    parts, left, right = refs[:3], refs[3], refs[4]
    at = 0
    for ref in parts:
        for k in range(ref.shape[0]):
            right[at + k] = ref[k, 0:8]
            left[at + k] = ref[k, 8:16]
        at += ref.shape[0]


def finish_kernel(counts, *refs):
    parts, (left, right), refs = refs[:3], refs[3:5], refs[5:]
    coarse_root, mid_q, mid_y, mid_r, fine_q, fine_y, fine_r, out_x, out_r = refs[:9]
    natural, error, spread, mt, ft, plain_x, plain_r, rows_x, rows_r = refs[9:18]
    cw, mw, fw = refs[18:22], refs[22:26], refs[26:30]
    ready_x, ready_r, sems = refs[30:]
    gz, xy = lax.axis_index("gz"), lax.axis_index("xy")

    on_left, on_right = inner(xy, counts[1])

    at = 0
    for ref in parts:
        for k in range(ref.shape[0]):
            natural[at, 0:4] = on_left * left[at, 2:6]
            natural[at, 4:14] = ref[k, 2:12]
            natural[at, 14:18] = on_right * right[at, 0:4]
            natural[at, 18:24] = jnp.zeros((6, LANES), F32)
            for x in range(3):
                cw[0][at, x] = FIRST * weave(natural, at, 0, 1, 3, x)
            at += 1
    masks = row_masks(3, 4 * xy - 7, 4 * counts[1])
    smooth(cw, 0, 16, 3, masks, z_mask(2 * gz - 7, 2 * counts[0]))
    for k in range(10):
        for x in range(3):
            total = (cw[0][k + 3, x] + cw[1][k + 3, x]) + (cw[2][k + 3, x] + cw[3][k + 3, x])
            natural[k, pl.ds(x, 8, 3), :] = total
        error[k] = natural[k, 2:18] / jnp.maximum(coarse_root[k], LEAST)

    for k in range(10):
        for x in range(4):
            value = error[k, pl.ds(x >> 1, 8, 2), :]
            for i in (x, 4 + x):
                mt[2 * k + 2, i] = mid_r[2 * k, i] * value
                mt[2 * k + 3, i] = mid_r[2 * k + 1, i] * value

    masks = row_masks(4, 8 * xy - 10, 8 * counts[1])
    z_scale = z_mask(4 * gz - 10, 4 * counts[0])

    def mid_correct(z):
        _, rest = applied(mt, z, 4, mid_q)
        scales = [z_scale(z, FIRST) * mask for mask in masks]
        for i, value in enumerate(rest):
            mw[0][z, i] = scales[i % 4] * value

    loop(4, 20, mid_correct)
    smooth(mw, 4, 20, 4, masks, z_scale)

    def mid_error(z):
        for k in range(2):
            for x in range(4):
                i = 4 * k + x
                total = (mw[0][z, i] + mw[1][z, i]) + (mw[2][z, i] + mw[3][z, i])
                total = total + (mid_y[z - 7, i] + mt[z, i])
                spread[2 * (z - 7) + k, pl.ds(x, 8, 4), :] = total / jnp.maximum(mid_r[z - 2, i], LEAST)

    loop(7, 17, mid_error)

    def fine_prolong(k):
        for j in range(2):
            for x in range(4):
                value = spread[2 * k + j, pl.ds(6 + (x >> 1), 8, 2), :]
                for i in (8 * j + x, 8 * j + 4 + x):
                    ft[2 * k + 2, i] = fine_r[jnp.maximum(2 * k - 1, 0), i] * value
                    ft[2 * k + 3, i] = fine_r[jnp.minimum(2 * k, 17), i] * value

    loop(0, 10, fine_prolong, 10)
    masks = row_masks(4, 16 * xy - 8, 16 * counts[1])
    z_scale = z_mask(8 * gz - 8, 8 * counts[0])

    def fine_correct(z):
        _, rest = applied(ft, z, 4, fine_q)
        scales = [z_scale(z, FIRST) * mask for mask in masks]
        for i, value in enumerate(rest):
            fw[0][z, i] = scales[i % 4] * value

    loop(4, 20, fine_correct)

    smooth(fw, 4, 20, 4, masks, z_scale)
    matrix = weave_matrix(1)

    def leave(plain, rows, ready, out, sem):
        for z in range(8):
            for k in range(4):
                rows[16 * z : 16 * z + 16, LANES * k : LANES * k + LANES] = plain[4 * z + k, 8:24]
        ready[...] = moved(rows[...], matrix).reshape(8, 16, 512)
        copy = pltpu.make_async_copy(ready, out, sem)
        copy.start()
        return copy

    for z in range(8, 16):
        for k in range(4):
            for x in range(4):
                i = 4 * k + x
                total = (fw[0][z, i] + fw[1][z, i]) + (fw[2][z, i] + fw[3][z, i])
                total = total + (fine_y[z - 8, i] + ft[z, i])
                plain_x[4 * (z - 8) + k, pl.ds(x, 8, 4), :] = total / fine_r[z - 3, i]
    first = leave(plain_x, rows_x, ready_x, out_x, sems.at[0])
    for z in range(8, 16):
        rest = remains(fw, z, 4)
        for k in range(4):
            for x in range(4):
                i = 4 * k + x
                plain_r[4 * (z - 8) + k, pl.ds(x, 8, 4), :] = fine_r[z - 3, i] * rest[i]
    second = leave(plain_r, rows_r, ready_r, out_r, sems.at[1])
    first.wait()
    second.wait()


def call(kernel, operands, out_shapes, scratch=(), space=pltpu.VMEM, out_space=pltpu.VMEM):
    whole = pl.BlockSpec(memory_space=out_space)
    return pl.pallas_call(
        kernel,
        out_shape=[jax.ShapeDtypeStruct(s, F32) for s in out_shapes],
        in_specs=[pl.BlockSpec(memory_space=space)] * len(operands),
        out_specs=[whole] * len(out_shapes),
        scratch_shapes=[pltpu.VMEM(s, F32) if isinstance(s, tuple) else s for s in scratch],
        compiler_params=pltpu.CompilerParams(vmem_limit_bytes=30 * 1024 * 1024),
    )(*operands)


def send(block, axis, shift):
    count = lax.axis_size(axis)
    pairs = [(i, i + shift) for i in range(count) if 0 <= i + shift < count]
    return lax.ppermute(block, axis, pairs)


def turn(to_left, to_right):
    count = lax.axis_size("xy")
    left = lax.ppermute(to_right, "xy", [(i, (i + 1) % count) for i in range(count)])
    right = lax.ppermute(to_left, "xy", [(i, (i - 1) % count) for i in range(count)])
    return left, right


def with_counts(kernel):
    counts = (lax.axis_size("gz"), lax.axis_size("xy"))
    return lambda *refs: kernel(counts, *refs)


def on_device(load_field, density, void_mask):
    up, down, root, to_left, to_right = call(
        scale_kernel,
        [pltpu.with_memory_space_constraint(x, pltpu.HBM) for x in (load_field, density, void_mask)],
        [(52, 16, LANES), (52, 16, LANES), (32, 16, LANES)] + [(416, LANES)] * 2,
        [(16, 16, 512), pltpu.VMEM((1, 2, 64), jnp.int32), pltpu.SemaphoreType.DMA((3,))],
        pltpu.HBM,
    )
    low, high = send(up, "gz", 1), send(down, "gz", -1)
    left, right = turn(to_left, to_right)
    low, high, left, right = lax.optimization_barrier((low, high, left, right))
    to_left, to_right = call(fine_pack_kernel, (low, high), [(FINE_Q_ROWS + FINE_R_ROWS, LANES)] * 2)
    far_left, far_right = turn(to_left, to_right)
    fine = (24, 16, 8, LANES)
    fine_q, fine_y, fine_r, mid_q, mid_r, first, second, to_left, to_right = call(
        with_counts(fine_pre_kernel),
        (low, up, root, high, left, right, far_left, far_right),
        [fine, (8, 16, 8, LANES), (18, 16, 8, LANES)] + [(16, 16, LANES)] * 2 + [(288, LANES)] * 2 + [(224, LANES)] * 2,
        [(96, 32, LANES)] + [fine] * 4,
    )
    pairs = mid_pairs(lax.axis_size("gz"))
    first, second = lax.ppermute(first, "gz", pairs[0]), lax.ppermute(second, "gz", pairs[1])
    left, right = turn(to_left, to_right)
    first, second, left, right = lax.optimization_barrier((first, second, left, right))
    low, high, to_left, to_right = call(
        with_counts(mid_pack_kernel), (first, second), [(288, LANES)] * 2 + [(MID_Q_ROWS + MID_R_ROWS, LANES)] * 2
    )
    far_left, far_right = turn(to_left, to_right)
    mid = (24, 8, 8, LANES)
    mid_q, mid_y, mid_r, coarse, coarse_low, coarse_high, coarse_root = call(
        with_counts(mid_pre_kernel),
        (low, high, mid_q, mid_r, left, right, far_left, far_right),
        [mid, (10, 8, 8, LANES), (20, 8, 8, LANES), (8, 16, LANES)] + [(4, 16, LANES)] * 2 + [(10, 16, LANES)],
        [(48, 32, LANES)] + [mid] * 4,
    )
    parts = (send(coarse_low, "gz", 2), coarse, send(coarse_high, "gz", -2))
    to_left, to_right = call(coarse_pack_kernel, parts, [(16, 8, LANES)] * 2)
    left, right = turn(to_left, to_right)
    coarsest = (16, 3, 8, LANES)
    return tuple(
        call(
            with_counts(finish_kernel),
            parts + (left, right, coarse_root, mid_q, mid_y, mid_r, fine_q, fine_y, fine_r),
            [(8, 16, 512), (8, 16, 512)],
            [(16, 24, LANES), (10, 16, LANES), (20, 32, LANES), mid, fine]
            + [(32, 32, LANES)] * 2
            + [(128, 512)] * 2
            + [coarsest] * 4
            + [mid] * 4
            + [fine] * 4
            + [(8, 16, 512)] * 2
            + [pltpu.SemaphoreType.DMA((2,))],
            out_space=pl.ANY,
        )
    )


def solution(mesh):
    specs = (P("gz", "xy", None), P("gz", "xy", None), P("gz", "xy", None))
    return jax.shard_map(
        on_device, mesh=mesh, in_specs=specs, out_specs=specs[:2], check_vma=False
    )
```

```python
import jax
import jax.numpy as jnp
from jax import lax
from jax.experimental import pallas as pl
from jax.experimental.pallas import tpu as pltpu
from jax.sharding import PartitionSpec as P


DEGREE = 4
THETA = 1.15
DELTA = 0.85
FIRST = 1.0 / (6.0 * THETA)
LEAST = 0.05
F32 = jnp.float32
LANES = 128


def coefficients():
    sigma = THETA / DELTA
    rho = 1.0 / sigma
    pairs = []
    for turn in range(DEGREE - 1):
        rho_next = 1.0 / (2.0 * sigma - rho)
        pairs.append((rho_next * rho, 2.0 * rho_next / (6.0 * DELTA)))
        rho = rho_next
    return pairs


def recurrences():
    out, c1_old, c2_old = [], 0.0, FIRST
    for c1, c2 in coefficients():
        out.append((c1 + c2 / c2_old - 6.0 * c2, c2 * c1_old / c2_old, c2))
        c1_old, c2_old = c1, c2
    return out, (1.0 / c2_old - 6.0, c1_old / c2_old)


STEPS, LAST = recurrences()


def iota(shape, dim):
    return lax.broadcasted_iota(jnp.int32, shape, dim)


def inner(xy, count):
    return jnp.where(xy > 0, F32(1.0), F32(0.0)), jnp.where(xy < count - 1, F32(1.0), F32(0.0))


def row_masks(n, base, count):
    masks = []
    for x in range(n):
        place = n * iota((8, LANES), 0) + (x + base)
        masks.append(jnp.where((place >= 0) & (place < count), 1.0, 0.0).astype(F32))
    return masks


def z_mask(base, count):
    def scaled(z, value):
        place = z + base
        return jnp.where((place >= 0) & (place < count), F32(value), F32(0.0))

    return scaled


def loop(low, high, body, width=24):
    turns = (high - low) // width if high - low > width else 0

    def step(t, carry):
        for j in range(width):
            body(low + width * t + j)
        return carry

    if turns > 0:
        lax.fori_loop(0, turns, step, 0)
    for z in range(low + turns * width, high):
        body(z)


def around(ref, z, n):
    count = ref.shape[1]
    blocks = count // n
    here = [ref[z, i] for i in range(count)]
    lane = iota((8, LANES), 1)
    before = [jnp.where(lane == 0, 0.0, pltpu.roll(here[(blocks - 1) * n + x], 1, 1)) for x in range(n)]
    after = [jnp.where(lane == LANES - 1, 0.0, pltpu.roll(here[x], LANES - 1, 1)) for x in range(n)]
    total = []
    for k in range(blocks):
        row = here[k * n : k * n + n]
        up = pltpu.roll(row[n - 1], 1, 0)
        down = pltpu.roll(row[0], 7, 0)
        for x in range(n):
            i = k * n + x
            left = here[i - n] if k > 0 else before[x]
            right = here[i + n] if k + 1 < blocks else after[x]
            north = row[x - 1] if x > 0 else up
            south = row[x + 1] if x + 1 < n else down
            total.append(((left + right) + (north + south)) + (ref[z - 1, i] + ref[z + 1, i]))
    return here, total


def applied(ref, z, n, q):
    here, total = around(ref, z, n)
    return here, [q[z, i] - (6.0 * here[i] - total[i]) for i in range(len(here))]


def smooth(w, low, high, n, masks, z_scale, width=24):
    for turn, (a, b, c) in enumerate(STEPS):

        def advance(z, turn=turn, a=a, b=b, c=c):
            here, total = around(w[turn], z, n)
            scales = [z_scale(z, c) * mask for mask in masks]
            for i in range(len(here)):
                value = a * here[i] + scales[i % n] * total[i]
                w[turn + 1][z, i] = value if turn == 0 else value - b * w[turn - 1][z, i]

        loop(low + 1 + turn, high - 1 - turn, advance, width)


def remains(w, z, n):
    here, total = around(w[DEGREE - 1], z, n)
    return [(LAST[0] * here[i] + total[i]) - LAST[1] * w[DEGREE - 2][z, i] for i in range(len(here))]


def weave(source, z, k, blocks, n, x):
    return source[z * blocks + k, pl.ds(x, 8, n), :]


def moved(left, right):
    high = left.astype(jnp.bfloat16)
    low = (left - high.astype(F32)).astype(jnp.bfloat16)
    return jnp.dot(high, right, preferred_element_type=F32) + jnp.dot(low, right, preferred_element_type=F32)


def weave_matrix(dim):
    plain, woven = iota((512, 512), dim), iota((512, 512), 1 - dim)
    same = plain == 4 * (woven & (LANES - 1)) + (woven >> 7)
    return jnp.where(same, 1.0, 0.0).astype(jnp.bfloat16)


CORNER = [8, 8, 8, 8, 7, 6, 5, 4]
MID_CORNER = [8, 8, 8, 8, 7, 8, 7, 6]


def corner_plan(blocks, first, last, rows):
    plan, at = [], 0
    for side in range(2):
        for layer in range(8):
            away = 8 - layer if side == 0 else layer + 1
            if not first <= away <= last:
                continue
            for k in range(blocks):
                count = rows if isinstance(rows, int) else rows[away - 1]
                plan.append((side, layer, k, count, at))
                at += count
    return plan, at


FINE_Q, FINE_Q_ROWS = corner_plan(4, 1, 8, CORNER)
FINE_R, FINE_R_ROWS = corner_plan(4, 1, 4, 4)
MID_Q, MID_Q_ROWS = corner_plan(2, 1, 8, MID_CORNER)
MID_R, MID_R_ROWS = corner_plan(2, 1, 6, 8)


def scale_kernel(load_hbm, density_hbm, void_hbm, up, down, root, left, right, both, void, sems):
    copies = [
        pltpu.make_async_copy(load_hbm, both.at[pl.ds(0, 8)], sems.at[0]),
        pltpu.make_async_copy(density_hbm, both.at[pl.ds(8, 8)], sems.at[1]),
        pltpu.make_async_copy(void_hbm, void, sems.at[2]),
    ]
    for copy in copies:
        copy.start()
    matrix = weave_matrix(0)
    copies[2].wait()
    bricks = jnp.where(void[0] == 1, 1.0, 0.0).astype(F32)
    bricks = jnp.concatenate([jnp.broadcast_to(bricks[k : k + 1], (8, 64)) for k in range(2)], axis=0)
    spread = jnp.where((iota((64, LANES), 1) >> 1) == iota((64, LANES), 0), 1.0, 0.0).astype(jnp.bfloat16)
    voids = jnp.dot(bricks.astype(jnp.bfloat16), spread, preferred_element_type=F32)
    copies[0].wait()
    copies[1].wait()
    fields = moved(both[...].reshape(256, 512), matrix)
    for z in range(8):
        for k in range(4):
            b = fields[16 * z : 16 * z + 16, LANES * k : LANES * k + LANES]
            d = fields[128 + 16 * z : 144 + 16 * z, LANES * k : LANES * k + LANES]
            r = jnp.sqrt(jnp.where(voids > 0.5, 0.01, 0.01 + 0.99 * d * d * d))
            q = b / r
            up[4 * z + k] = q
            down[4 * z + k] = q
            root[4 * z + k] = r
            i = 4 * z + k
            left[8 * i : 8 * i + 8] = q[0:8]
            right[8 * i : 8 * i + 8] = q[8:16]
            left[256 + 5 * i : 261 + 5 * i] = r[0:5]
            right[256 + 5 * i : 261 + 5 * i] = r[11:16]
            if z >= 3:
                up[4 * (5 + z) + k] = r
            if z < 5:
                down[4 * (8 + z) + k] = r


def fine_pack_kernel(low, high, left, right):
    for side, layer, k, n, at in FINE_Q:
        ref, i = (low, high)[side], 4 * layer + k
        left[at : at + n] = ref[i, 0:n]
        right[at : at + n] = ref[i, 16 - n : 16]
    for side, layer, k, n, at in FINE_R:
        ref, i = (low, high)[side], 32 + 4 * (layer - 3 if side == 0 else layer) + k
        at += FINE_Q_ROWS
        left[at : at + n] = ref[i, 0:n]
        right[at : at + n] = ref[i, 16 - n : 16]


def fine_pre_kernel(
    counts, low, up, root, high, left, right, far_left, far_right, q, y, r, mid_q, mid_r, early, late, mid_left, mid_right, *scratch
):
    natural, w = scratch[0], scratch[1:5]
    gz, xy = lax.axis_index("gz"), lax.axis_index("xy")
    on_left, on_right = inner(xy, counts[1])
    masks = row_masks(4, 16 * xy - 8, 16 * counts[1])
    z_scale = z_mask(8 * gz - 8, 8 * counts[0])

    blank = jnp.zeros((8, LANES), F32)
    for n, ref in enumerate((low, up, high)):
        for i in range(32):
            natural[32 * n + i, 8:24] = ref[i]
    for i in range(32):
        natural[32 + i, 0:8] = on_left * left[8 * i : 8 * i + 8]
        natural[32 + i, 24:32] = on_right * right[8 * i : 8 * i + 8]
    for side, layer, k, n, at in FINE_Q:
        j = 64 * side + 4 * layer + k
        if n < 8:
            natural[j, 0:8] = blank
            natural[j, 24:32] = blank
        natural[j, 8 - n : 8] = on_left * far_left[at : at + n]
        natural[j, 24 : 24 + n] = on_right * far_right[at : at + n]

    def begin(z):
        for k in range(4):
            for x in range(4):
                w[0][z, 4 * k + x] = FIRST * weave(natural, z, k, 4, 4, x)

    loop(0, 24, begin, 8)

    place = 0
    for ref, first, count in ((low, 32, 20), (root, 0, 32), (high, 32, 20)):
        for i in range(first, first + count):
            natural[place, 0:8] = blank
            natural[place, 8:24] = ref[i]
            natural[place, 24:32] = blank
            place += 1
    for i in range(32):
        natural[20 + i, 3:8] = on_left * left[256 + 5 * i : 261 + 5 * i]
        natural[20 + i, 24:29] = on_right * right[256 + 5 * i : 261 + 5 * i]
    for side, layer, k, n, at in FINE_R:
        j = 4 * (layer - 3 if side == 0 else 13 + layer) + k
        at += FINE_Q_ROWS
        natural[j, 8 - n : 8] = on_left * far_left[at : at + n]
        natural[j, 24 : 24 + n] = on_right * far_right[at : at + n]

    def roots(z):
        for k in range(4):
            for x in range(4):
                r[z, 4 * k + x] = weave(natural, z, k, 4, 4, x)

    loop(0, 18, roots, 6)
    smooth(w, 0, 24, 4, masks, z_scale, 8)

    def rest(z):
        for i, value in enumerate(remains(w, z, 4)):
            q[z, i] = value

    loop(4, 20, rest, 8)

    def total(z):
        for i in range(16):
            y[z, i] = (w[0][z + 8, i] + w[1][z + 8, i]) + (w[2][z + 8, i] + w[3][z + 8, i])

    loop(0, 8, total)

    def fold(m):
        for k in range(2):
            for x in range(2):
                sums, roots = None, None
                for z in range(2):
                    for i in (8 * k + 2 * x, 8 * k + 2 * x + 1, 8 * k + 2 * x + 4, 8 * k + 2 * x + 5):
                        a = r[2 * m + 1 + z, i]
                        b = a * q[2 * m + 4 + z, i]
                        sums = b if sums is None else sums + b
                        roots = a if roots is None else roots + a
                roots = 0.125 * roots
                mid_r[2 * m + k, pl.ds(x, 8, 2), :] = roots
                mid_q[2 * m + k, pl.ds(x, 8, 2), :] = 0.5 * sums / jnp.maximum(roots, LEAST)

    loop(0, 8, fold)
    skip = jnp.where(gz % 4 == 3, 0, 2)
    for out, start in ((early, skip), (late, 2 - skip)):
        for near in range(8):
            layer = jnp.where(start == 2, 7 - near, near)
            for k in range(2):
                at, count = mid_place(near, k)
                out[at : at + count] = mid_q[2 * layer + k, 8 - count // 2 : 8 + count // 2]
        for i in range(12):
            out[168 + 8 * i : 176 + 8 * i] = mid_r[2 * start + i, 4:12]
    for i in range(16):
        mid_right[8 * i : 8 * i + 8] = mid_q[i, 2:10]
        mid_left[8 * i : 8 * i + 8] = mid_q[i, 6:14]
        mid_right[128 + 6 * i : 134 + 6 * i] = mid_r[i, 4:10]
        mid_left[128 + 6 * i : 134 + 6 * i] = mid_r[i, 6:12]


def mid_pairs(count):
    first, second = [], []
    for i in range(count):
        up, down = (first, second) if i % 4 != 3 else (second, first)
        if i + 2 < count:
            up.append((i, i + 2))
        if i >= 2:
            down.append((i, i - 2))
    return first, second + [(0, 1), (count - 1, count - 2)]


def mid_sides(count, gz, first, second, low, high):
    @pl.when(gz % 4 != 1)
    def _():
        low[...] = first[...]
        high[...] = second[...]

    @pl.when(gz % 4 == 1)
    def _():
        low[...] = second[...]
        high[...] = first[...]

    @pl.when(gz == 1)
    def _():
        for near in range(4):
            low[24 * near : 24 * near + 24] = second[72 - 24 * near : 96 - 24 * near]
        low[96:200] = jnp.zeros((104, LANES), F32)
        low[200:264] = second[168:232]

    @pl.when(gz == count - 2)
    def _():
        for near in range(4):
            high[24 * near : 24 * near + 24] = second[72 - 24 * near : 96 - 24 * near]
        high[96:168] = jnp.zeros((72, LANES), F32)
        high[168:232] = second[200:264]
        high[232:264] = jnp.zeros((32, LANES), F32)


def mid_place(near, k):
    return (24 * near + 12 * k, 12) if near < 5 else (120 + 16 * (near - 5) + 8 * k, 8)


def mid_rows(low, high, side, layer, k):
    at, count = mid_place(7 - layer if side == 0 else layer, k)
    return (low, high)[side], at, count


def mid_root_rows(low, high, side, layer, k):
    at = 168 + 8 * (2 * (layer - 2 if side == 0 else layer) + k)
    return (low, high)[side][at : at + 8]


def mid_pack_kernel(counts, first, second, low, high, left, right):
    mid_sides(counts[0], lax.axis_index("gz"), first, second, low, high)
    for side, layer, k, n, at in MID_Q:
        ref, place, count = mid_rows(low, high, side, layer, k)
        right[at : at + n] = ref[place + 8 - n : place + 8]
        left[at : at + n] = ref[place + count - 8 : place + count - 8 + n]
    for side, layer, k, n, at in MID_R:
        at += MID_Q_ROWS
        right[at : at + n] = mid_root_rows(low, high, side, layer, k)
        left[at : at + n] = mid_root_rows(low, high, side, layer, k)


def mid_pre_kernel(counts, *refs):
    (low, high, own_q, own_r, left, right, far_left, far_right), refs = refs[:8], refs[8:]
    q, y, r, coarse, coarse_low, coarse_high, coarse_root, natural = refs[:8]
    w = refs[8:]
    gz, xy = lax.axis_index("gz"), lax.axis_index("xy")
    on_left, on_right = inner(xy, counts[1])
    masks = row_masks(4, 8 * xy - 10, 8 * counts[1])
    z_scale = z_mask(4 * gz - 10, 4 * counts[0])
    blank = jnp.zeros((8, LANES), F32)
    for i in range(16):
        natural[16 + i, 0:8] = on_left * left[8 * i : 8 * i + 8]
        natural[16 + i, 24:32] = blank
        natural[16 + i, 8:20] = own_q[i, 2:14]
        natural[16 + i, 20:28] = on_right * right[8 * i : 8 * i + 8]
    for side, layer, k, n, at in MID_Q:
        i = 32 * side + 2 * layer + k
        natural[i, 0:8] = blank
        natural[i, 24:32] = blank
        ref, place, count = mid_rows(low, high, side, layer, k)
        first, last = 14 - count // 2, 14 + count // 2
        natural[i, 20:28] = blank
        natural[i, first:last] = ref[place : place + count]
        natural[i, first - n : first] = on_left * far_left[at : at + n]
        natural[i, last : last + n] = on_right * far_right[at : at + n]

    def begin(z):
        for k in range(2):
            for x in range(4):
                w[0][z, 4 * k + x] = FIRST * weave(natural, z, k, 2, 4, x)

    loop(0, 24, begin)
    for i in range(40):
        natural[i, 0:8] = blank
        natural[i, 24:32] = blank
    for i in range(16):
        natural[12 + i, 2:8] = on_left * left[128 + 6 * i : 134 + 6 * i]
        natural[12 + i, 8:20] = own_r[i, 2:14]
        natural[12 + i, 20:26] = on_right * right[128 + 6 * i : 134 + 6 * i]
    for side, layer, k, n, at in MID_R:
        i = 2 * (layer - 2 if side == 0 else 14 + layer) + k
        at += MID_Q_ROWS
        natural[i, 2:10] = on_left * far_left[at : at + n]
        natural[i, 10:18] = mid_root_rows(low, high, side, layer, k)
        natural[i, 18:26] = on_right * far_right[at : at + n]

    def roots(z):
        for k in range(2):
            for x in range(4):
                r[z, 4 * k + x] = weave(natural, z, k, 2, 4, x)

    loop(0, 20, roots)
    smooth(w, 0, 24, 4, masks, z_scale)

    def rest(z):
        for i, value in enumerate(remains(w, z, 4)):
            q[z, i] = value

    loop(4, 20, rest)

    def total(z):
        for i in range(8):
            y[z, i] = (w[0][z + 7, i] + w[1][z + 7, i]) + (w[2][z + 7, i] + w[3][z + 7, i])

    loop(0, 10, total)

    for m in range(10):
        for x in range(2):
            sums, mean = None, None
            for z in range(2):
                for i in (2 * x, 2 * x + 1, 2 * x + 4, 2 * x + 5):
                    a = r[2 * m + z, i]
                    b = a * q[2 * m + 2 + z, i]
                    sums = b if sums is None else sums + b
                    mean = a if mean is None else mean + a
            mean = 0.125 * mean
            coarse_root[m, pl.ds(x, 8, 2), :] = mean
            if 0 < m < 9:
                coarse[m - 1, pl.ds(x, 8, 2), :] = 0.5 * sums / jnp.maximum(mean, LEAST)
    for m in range(4):
        coarse_low[m] = coarse[m]
        coarse_high[m] = coarse[4 + m]


def coarse_pack_kernel(*refs):
    parts, left, right = refs[:3], refs[3], refs[4]
    at = 0
    for ref in parts:
        for k in range(ref.shape[0]):
            right[at + k] = ref[k, 0:8]
            left[at + k] = ref[k, 8:16]
        at += ref.shape[0]


def finish_kernel(counts, *refs):
    parts, (left, right), refs = refs[:3], refs[3:5], refs[5:]
    coarse_root, mid_q, mid_y, mid_r, fine_q, fine_y, fine_r, out_x, out_r = refs[:9]
    natural, error, spread, mt, ft, plain_x, plain_r, rows_x, rows_r = refs[9:18]
    cw, mw, fw = refs[18:22], refs[22:26], refs[26:30]
    ready_x, ready_r, sems = refs[30:]
    gz, xy = lax.axis_index("gz"), lax.axis_index("xy")

    on_left, on_right = inner(xy, counts[1])

    at = 0
    for ref in parts:
        for k in range(ref.shape[0]):
            natural[at, 0:4] = on_left * left[at, 2:6]
            natural[at, 4:14] = ref[k, 2:12]
            natural[at, 14:18] = on_right * right[at, 0:4]
            natural[at, 18:24] = jnp.zeros((6, LANES), F32)
            for x in range(3):
                cw[0][at, x] = FIRST * weave(natural, at, 0, 1, 3, x)
            at += 1
    masks = row_masks(3, 4 * xy - 7, 4 * counts[1])
    smooth(cw, 0, 16, 3, masks, z_mask(2 * gz - 7, 2 * counts[0]))
    for k in range(10):
        for x in range(3):
            total = (cw[0][k + 3, x] + cw[1][k + 3, x]) + (cw[2][k + 3, x] + cw[3][k + 3, x])
            natural[k, pl.ds(x, 8, 3), :] = total
        error[k] = natural[k, 2:18] / jnp.maximum(coarse_root[k], LEAST)

    for k in range(10):
        for x in range(4):
            value = error[k, pl.ds(x >> 1, 8, 2), :]
            for i in (x, 4 + x):
                mt[2 * k + 2, i] = mid_r[2 * k, i] * value
                mt[2 * k + 3, i] = mid_r[2 * k + 1, i] * value

    masks = row_masks(4, 8 * xy - 10, 8 * counts[1])
    z_scale = z_mask(4 * gz - 10, 4 * counts[0])

    def mid_correct(z):
        _, rest = applied(mt, z, 4, mid_q)
        scales = [z_scale(z, FIRST) * mask for mask in masks]
        for i, value in enumerate(rest):
            mw[0][z, i] = scales[i % 4] * value

    loop(4, 20, mid_correct)
    smooth(mw, 4, 20, 4, masks, z_scale)

    def mid_error(z):
        for k in range(2):
            for x in range(4):
                i = 4 * k + x
                total = (mw[0][z, i] + mw[1][z, i]) + (mw[2][z, i] + mw[3][z, i])
                total = total + (mid_y[z - 7, i] + mt[z, i])
                spread[2 * (z - 7) + k, pl.ds(x, 8, 4), :] = total / jnp.maximum(mid_r[z - 2, i], LEAST)

    loop(7, 17, mid_error)

    def fine_prolong(k):
        for j in range(2):
            for x in range(4):
                value = spread[2 * k + j, pl.ds(6 + (x >> 1), 8, 2), :]
                for i in (8 * j + x, 8 * j + 4 + x):
                    ft[2 * k + 2, i] = fine_r[jnp.maximum(2 * k - 1, 0), i] * value
                    ft[2 * k + 3, i] = fine_r[jnp.minimum(2 * k, 17), i] * value

    loop(0, 10, fine_prolong, 10)
    masks = row_masks(4, 16 * xy - 8, 16 * counts[1])
    z_scale = z_mask(8 * gz - 8, 8 * counts[0])

    def fine_correct(z):
        _, rest = applied(ft, z, 4, fine_q)
        scales = [z_scale(z, FIRST) * mask for mask in masks]
        for i, value in enumerate(rest):
            fw[0][z, i] = scales[i % 4] * value

    loop(4, 20, fine_correct)

    smooth(fw, 4, 20, 4, masks, z_scale)
    matrix = weave_matrix(1)

    def leave(plain, rows, ready, out, sem):
        for z in range(8):
            for k in range(4):
                rows[16 * z : 16 * z + 16, LANES * k : LANES * k + LANES] = plain[4 * z + k, 8:24]
        ready[...] = moved(rows[...], matrix).reshape(8, 16, 512)
        copy = pltpu.make_async_copy(ready, out, sem)
        copy.start()
        return copy

    for z in range(8, 16):
        for k in range(4):
            for x in range(4):
                i = 4 * k + x
                total = (fw[0][z, i] + fw[1][z, i]) + (fw[2][z, i] + fw[3][z, i])
                total = total + (fine_y[z - 8, i] + ft[z, i])
                plain_x[4 * (z - 8) + k, pl.ds(x, 8, 4), :] = total / fine_r[z - 3, i]
    first = leave(plain_x, rows_x, ready_x, out_x, sems.at[0])
    for z in range(8, 16):
        rest = remains(fw, z, 4)
        for k in range(4):
            for x in range(4):
                i = 4 * k + x
                plain_r[4 * (z - 8) + k, pl.ds(x, 8, 4), :] = fine_r[z - 3, i] * rest[i]
    second = leave(plain_r, rows_r, ready_r, out_r, sems.at[1])
    first.wait()
    second.wait()


def call(kernel, operands, out_shapes, scratch=(), space=pltpu.VMEM, out_space=pltpu.VMEM):
    whole = pl.BlockSpec(memory_space=out_space)
    return pl.pallas_call(
        kernel,
        out_shape=[jax.ShapeDtypeStruct(s, F32) for s in out_shapes],
        in_specs=[pl.BlockSpec(memory_space=space)] * len(operands),
        out_specs=[whole] * len(out_shapes),
        scratch_shapes=[pltpu.VMEM(s, F32) if isinstance(s, tuple) else s for s in scratch],
        compiler_params=pltpu.CompilerParams(vmem_limit_bytes=30 * 1024 * 1024),
    )(*operands)


def send(block, axis, shift):
    count = lax.axis_size(axis)
    pairs = [(i, i + shift) for i in range(count) if 0 <= i + shift < count]
    return lax.ppermute(block, axis, pairs)


def turn(to_left, to_right):
    count = lax.axis_size("xy")
    left = lax.ppermute(to_right, "xy", [(i, (i + 1) % count) for i in range(count)])
    right = lax.ppermute(to_left, "xy", [(i, (i - 1) % count) for i in range(count)])
    return left, right


def with_counts(kernel):
    counts = (lax.axis_size("gz"), lax.axis_size("xy"))
    return lambda *refs: kernel(counts, *refs)


def on_device(load_field, density, void_mask):
    up, down, root, to_left, to_right = call(
        scale_kernel,
        [pltpu.with_memory_space_constraint(x, pltpu.HBM) for x in (load_field, density, void_mask)],
        [(52, 16, LANES), (52, 16, LANES), (32, 16, LANES)] + [(416, LANES)] * 2,
        [(16, 16, 512), pltpu.VMEM((1, 2, 64), jnp.int32), pltpu.SemaphoreType.DMA((3,))],
        pltpu.HBM,
    )
    low, high = send(up, "gz", 1), send(down, "gz", -1)
    left, right = turn(to_left, to_right)
    low, high, left, right = lax.optimization_barrier((low, high, left, right))
    to_left, to_right = call(fine_pack_kernel, (low, high), [(FINE_Q_ROWS + FINE_R_ROWS, LANES)] * 2)
    far_left, far_right = turn(to_left, to_right)
    fine = (24, 16, 8, LANES)
    fine_q, fine_y, fine_r, mid_q, mid_r, first, second, to_left, to_right = call(
        with_counts(fine_pre_kernel),
        (low, up, root, high, left, right, far_left, far_right),
        [fine, (8, 16, 8, LANES), (18, 16, 8, LANES)] + [(16, 16, LANES)] * 2 + [(264, LANES)] * 2 + [(224, LANES)] * 2,
        [(96, 32, LANES)] + [fine] * 4,
    )
    pairs = mid_pairs(lax.axis_size("gz"))
    first, second = lax.ppermute(first, "gz", pairs[0]), lax.ppermute(second, "gz", pairs[1])
    left, right = turn(to_left, to_right)
    first, second, left, right = lax.optimization_barrier((first, second, left, right))
    low, high, to_left, to_right = call(
        with_counts(mid_pack_kernel), (first, second), [(264, LANES)] * 2 + [(MID_Q_ROWS + MID_R_ROWS, LANES)] * 2
    )
    far_left, far_right = turn(to_left, to_right)
    mid = (24, 8, 8, LANES)
    mid_q, mid_y, mid_r, coarse, coarse_low, coarse_high, coarse_root = call(
        with_counts(mid_pre_kernel),
        (low, high, mid_q, mid_r, left, right, far_left, far_right),
        [mid, (10, 8, 8, LANES), (20, 8, 8, LANES), (8, 16, LANES)] + [(4, 16, LANES)] * 2 + [(10, 16, LANES)],
        [(48, 32, LANES)] + [mid] * 4,
    )
    parts = (send(coarse_low, "gz", 2), coarse, send(coarse_high, "gz", -2))
    to_left, to_right = call(coarse_pack_kernel, parts, [(16, 8, LANES)] * 2)
    left, right = turn(to_left, to_right)
    coarsest = (16, 3, 8, LANES)
    return tuple(
        call(
            with_counts(finish_kernel),
            parts + (left, right, coarse_root, mid_q, mid_y, mid_r, fine_q, fine_y, fine_r),
            [(8, 16, 512), (8, 16, 512)],
            [(16, 24, LANES), (10, 16, LANES), (20, 32, LANES), mid, fine]
            + [(32, 32, LANES)] * 2
            + [(128, 512)] * 2
            + [coarsest] * 4
            + [mid] * 4
            + [fine] * 4
            + [(8, 16, 512)] * 2
            + [pltpu.SemaphoreType.DMA((2,))],
            out_space=pl.ANY,
        )
    )


def solution(mesh):
    specs = (P("gz", "xy", None), P("gz", "xy", None), P("gz", "xy", None))
    return jax.shard_map(
        on_device, mesh=mesh, in_specs=specs, out_specs=specs[:2], check_vma=False
    )
```
